512 devices in a mesh: tm: 16 (over x, y), space: 32 (over z, core).
Axes of the slice: x: 4, y: 4, z: 16, core: 2. Of those that a mesh axis runs over, the one named last changes fastest.
Arguments:
- starts: float32 [16, 3, 64, 16, 512], P('tm', None, 'space'), may hold values from -1 to 1, as said below
- anisotropy: float32 [64, 16, 512], P('space'), may hold values from 0.1 to 1
- applied: float32 [3], replicated, may hold values from -1 to 1
Outputs:
- slice_ends: float32 [16, 3, 64, 16, 512], P('tm', None, 'space')
The draws below stay inside these ranges and needn't reach their ends.
Inputs may be any that keep to these rules, and one draw needn't show every extreme that they name: `starts`: the three components of every site form a unit vector.
All inputs are finite; a program needn't handle non-finite values.
Results may differ from the reference program's by a relative error of at most 0.00002.
Values sent between devices are 32-bit elements; how exact they have to be, the bound alone decides.
No kernel may reach another device: no remote copies, remote signals or barrier semaphores. Data moves between devices by JAX's collectives and lax.ppermute only.
A program may use at most 64 MiB of HBM per device.

```python
import math
import jax
import jax.numpy as jnp
from jax import lax

LZ = 16
LY = 512
FINE_STEPS = 2
SLICES = 16
NX = 64


def draw_starts(key, part):
    key = jax.random.fold_in(key, 11)
    key_cos, key_phase = jax.random.split(key)
    grid_shape = (SLICES, NX, LZ, LY)
    cosine = jax.random.uniform(key_cos, grid_shape, jnp.float32, -1.0, 1.0)
    phase = jax.random.uniform(key_phase, grid_shape, jnp.float32, -math.pi, math.pi)
    sine_part = jnp.sqrt(jnp.maximum(1.0 - cosine * cosine, 0.0))
    return jnp.stack([sine_part * jnp.cos(phase), sine_part * jnp.sin(phase), cosine], axis=1)


def block_scale(key, shape, cuts, low, top_value):
    def one(axis_at, shards_of):
        draws = jax.random.uniform(jax.random.fold_in(jax.random.fold_in(key, 6), axis_at), (shards_of,), jnp.float32, low / len(cuts), top_value / len(cuts))
        return jnp.repeat(jnp.exp(draws), shape[axis_at] // shards_of).reshape((-1,) + (1,) * (len(shape) - axis_at - 1))

    gain = one(*cuts[0])
    for cut in cuts[1:]:
        gain = gain * one(*cut)
    return gain


def setup_inputs(seed: int = 0) -> dict:
    key_of = jax.random.split(jax.random.key(seed), 4)
    starts = draw_starts(jax.random.fold_in(key_of[3], 71), 0)
    anisotropy = jnp.clip(jnp.exp(math.log(1.0) - 2.3025851 * jax.random.uniform(key_of[1], (NX, LZ, LY), jnp.float32) ** block_scale(key_of[1], (NX, LZ, LY), ((0, 32),), -0.2, 0.2)), 0.1, 1.0)
    applied = jnp.clip(jax.random.uniform(key_of[2], (3,), jnp.float32, -1.0, 1.0), -1.0, 1.0)
    return {"starts": starts, "anisotropy": anisotropy, "applied": applied}


damping = 0.1
step_size = 0.02


def layer_field(forward, behind):
    forward = forward + jnp.roll(forward, -1, axis=-1)
    behind = behind + jnp.roll(behind, 1, axis=-1)
    layers = forward.shape[-2]
    odd_layer = (lax.iota(jnp.int32, layers) % 2 == 1)[:, None]
    chosen = jnp.where(odd_layer, forward, behind)
    widths = [(0, 0)] * (chosen.ndim - 2) + [(1, 1), (0, 0)]
    padded = jnp.pad(chosen, widths)
    return padded[..., :-2, :] + padded[..., 2:, :]


def neighbour_sum(spins):
    forward = spins + jnp.roll(spins, -1, axis=-3)
    behind = jnp.roll(spins, 1, axis=-3) + spins
    return layer_field(forward, behind)


def spin_rate(near, spins, anisotropy, applied):
    spin_x = spins[..., 0, :, :, :]
    spin_y = spins[..., 1, :, :, :]
    spin_z = spins[..., 2, :, :, :]
    field_x = near[..., 0, :, :, :] + applied[0]
    field_y = near[..., 1, :, :, :] + applied[1]
    field_z = near[..., 2, :, :, :] + 2.0 * anisotropy * spin_z + applied[2]
    cross_x = spin_y * field_z - spin_z * field_y
    cross_y = spin_z * field_x - spin_x * field_z
    cross_z = spin_x * field_y - spin_y * field_x
    double_x = spin_y * cross_z - spin_z * cross_y
    double_y = spin_z * cross_x - spin_x * cross_z
    double_z = spin_x * cross_y - spin_y * cross_x
    factor = -1.0 / (1.0 + damping * damping)
    return jnp.stack([factor * (cross_x + damping * double_x),
                      factor * (cross_y + damping * double_y),
                      factor * (cross_z + damping * double_z)], axis=-4)


def heun_step(spins, anisotropy, applied, step_len):
    rate_start = spin_rate(neighbour_sum(spins), spins, anisotropy, applied)
    predicted = spins + step_len * rate_start
    rate_end = spin_rate(neighbour_sum(predicted), predicted, anisotropy, applied)
    return spins + (0.5 * step_len) * (rate_start + rate_end)


def reference(starts, anisotropy, applied):
    fine_state = starts
    for repeat in range(FINE_STEPS):
        fine_state = heun_step(fine_state, anisotropy, applied, step_size)
    coarse_len = FINE_STEPS * step_size
    correction = fine_state - heun_step(starts, anisotropy, applied, coarse_len)

    def advance(current, corr_slice):
        advanced = heun_step(current, anisotropy, applied, coarse_len) + corr_slice
        return advanced, advanced

    carried, slice_ends = lax.scan(advance, starts[0], correction)
    return slice_ends
```

```python
import functools

import jax
import jax.numpy as jnp
from jax import lax
from jax.experimental import pallas as pl
from jax.experimental.pallas import tpu as pltpu
from jax.sharding import PartitionSpec as P

DAMPING = 0.1
STEP = 0.02
COARSE = 2 * STEP
GAIN = -1.0 / (1.0 + DAMPING * DAMPING)
F32 = jnp.float32
VMEM = pl.BlockSpec(memory_space=pltpu.VMEM)
SMEM = pl.BlockSpec(memory_space=pltpu.SMEM)


def near_odd(even_below, even_here):
    out = []
    for below, here in zip(even_below, even_here):
        pair = below + here
        pair = pair + pltpu.roll(pair, 1, axis=1)
        row = lax.broadcasted_iota(jnp.int32, pair.shape, 0)
        out.append(pair + jnp.where(row < 7, pltpu.roll(pair, 7, axis=0), 0.0))
    return out


def near_even(odd_here, odd_above):
    out = []
    for here, above in zip(odd_here, odd_above):
        pair = here + above
        pair = pair + pltpu.roll(pair, pair.shape[1] - 1, axis=1)
        row = lax.broadcasted_iota(jnp.int32, pair.shape, 0)
        out.append(pair + jnp.where(row > 0, pltpu.roll(pair, 1, axis=0), 0.0))
    return out


def cross(a, b):
    return [a[1] * b[2] - a[2] * b[1], a[2] * b[0] - a[0] * b[2], a[0] * b[1] - a[1] * b[0]]


def bare_rate(spin, near, twice_aniso, applied):
    field = [n + h for n, h in zip(near, applied)]
    field[2] = field[2] + twice_aniso * spin[2]
    turn = cross(spin, field)
    return cross(spin, [f + DAMPING * c for f, c in zip(field, turn)])


def rates(even, odd, aniso_even, aniso_odd, applied, evens, odds):
    rate_even = {x: bare_rate(even[x], near_even(odd[x], odd[x + 1]), aniso_even(x), applied) for x in evens}
    rate_odd = {x: bare_rate(odd[x], near_odd(even[x - 1], even[x]), aniso_odd(x), applied) for x in odds}
    return rate_even, rate_odd


def ahead(spins, rate, length):
    return {x: [s + (length * GAIN) * r for s, r in zip(spins[x], rate[x])] for x in rate}


def finish(spins, first, second, length, planes):
    return {
        x: [s + (0.5 * length * GAIN) * (f + g) for s, f, g in zip(spins[x], first[x], second[x])]
        for x in planes
    }


def heun(even, odd, aniso_even, aniso_odd, applied, length, low, high):
    evens, odds, inner = range(low, high), range(low + 1, high + 1), range(low + 1, high)
    first_e, first_o = rates(even, odd, aniso_even, aniso_odd, applied, evens, odds)
    pred_e, pred_o = ahead(even, first_e, length), ahead(odd, first_o, length)
    second_e, second_o = rates(pred_e, pred_o, aniso_even, aniso_odd, applied, inner, inner)
    return finish(even, first_e, second_e, length, inner), finish(odd, first_o, second_o, length, inner)


def lane_select(tile, low, high, a, b):
    lane = lax.broadcasted_iota(jnp.int32, (8, 128), 1) % tile
    return jnp.where((lane >= low) & (lane < high), a, b)


def tiles_of(wide):
    return [wide[:, 128 * q : 128 * (q + 1)] for q in range(wide.shape[1] // 128)]


def turn(x, by):
    by = by % x.shape[1]
    return pltpu.roll(x, by, axis=1) if by else x


def prologue(own, left, right, applied_ref, row_ref, payload, windows, layers):
    applied = [applied_ref[c] for c in range(3)]
    tiles = own.shape[3] // 128
    for base, ref in enumerate((left, own, right)):
        for q in range(tiles):
            layers[:, 2 * base : 2 * base + 2, q] = ref[:, :, :, 128 * q : 128 * (q + 1)]

    def load(comp, plane, parity):
        parts = [layers[comp, plane + 2, q, pl.ds(parity, 8, stride=2), :] for q in range(tiles)]
        return jnp.concatenate(parts, axis=1)

    planes = range(-2, 4)
    even = {x: [load(c, x, 0) for c in range(3)] for x in planes}
    odd = {x: [load(c, x, 1) for c in range(3)] for x in planes}

    def aniso_even(x):
        return 2.0 * load(3, x, 0)

    def aniso_odd(x):
        return 2.0 * load(3, x, 1)

    sides = (aniso_even, aniso_odd, applied)
    first_e, first_o = rates(even, odd, *sides, range(-2, 3), range(-1, 4))
    pred_e, pred_o = ahead(even, first_e, STEP), ahead(odd, first_o, STEP)
    second_e, second_o = rates(pred_e, pred_o, *sides, range(-1, 3), range(-1, 3))
    fine_e = finish(even, first_e, second_e, STEP, range(-1, 3))
    fine_o = finish(odd, first_o, second_o, STEP, range(-1, 3))
    fine_e, fine_o = heun(fine_e, fine_o, *sides, STEP, -1, 2)
    pred_e, pred_o = ahead(even, first_e, COARSE), ahead(odd, first_o, COARSE)
    second_e, second_o = rates(pred_e, pred_o, *sides, range(2), range(2))
    coarse_e = finish(even, first_e, second_e, COARSE, range(2))
    coarse_o = finish(odd, first_o, second_o, COARSE, range(2))

    row = row_ref[0]
    keep = jnp.where(row == 0, 0.0, 1.0).astype(F32)
    for comp in range(3):
        for parity, fine, coarse in ((0, fine_e, coarse_e), (1, fine_o, coarse_o)):
            moved = []
            for x in range(2):
                wide = fine[x][comp] - keep * coarse[x][comp]
                moved.append(tiles_of(pltpu.roll(wide, 16, axis=1)))
            count = len(moved[0])
            for q in range(count):
                a, b = moved[0][q], moved[1][q]
                after = (q + 1) % count
                c, d = (lane_select(128, 96, 128, m[q], m[after]) for m in moved)
                for i, (p, r) in enumerate(((a, b), (a, b), (a, b), (c, d))):
                    payload[4 * q + i, comp, parity] = lane_select(
                        128, 0, 64, turn(p, -32 * i), turn(r, 64 - 32 * i)
                    )

    for at in range(payload.shape[0]):

        @pl.when(row == at)
        def _():
            for parity, planes_used in ((0, range(-2, 3)), (1, range(-1, 4))):
                for k, x in enumerate(planes_used):
                    wide = 2.0 * load(3, x, parity)
                    windows[parity, k] = turn(wide, 16 - 32 * at)[:, :128]


def dense(even_pair, odd_pair):
    return lane_select(64, 0, 32, turn(even_pair, -16), turn(odd_pair, 16))


def chain(block, last, own, left, right, corr, windows, applied_ref, *rest):
    applied = [applied_ref[c] for c in range(3)]
    first_slice = 2 * block + 1

    def pair(ref, field, comp, parity):
        packed = ref[field, comp, parity]
        return packed, turn(packed, 64)

    def spread(field, parity, planes):
        out = {}
        for ref, base in ((left, -2), (own, 0), (right, 2)):
            pairs = [pair(ref, field, c, parity) for c in range(3)]
            for k in range(2):
                if base + k in planes:
                    out[base + k] = [p[k] for p in pairs]
        return out

    def aniso_even(x):
        return windows[0, x + 2]

    def aniso_odd(x):
        return windows[1, x + 1]

    sides = (aniso_even, aniso_odd, applied)
    reach = range(-1, 3) if last else range(-2, 4)
    inner = range(reach[0] + 1, reach[-1])
    even, odd = spread(0, 0, reach), spread(0, 1, reach)
    corr_e, corr_o = spread(1, 0, inner), spread(1, 1, inner)

    def add(spins, extra):
        return {x: [s + e for s, e in zip(spins[x], extra[x])] for x in extra}

    even, odd = heun(even, odd, *sides, COARSE, reach[0], reach[-1])
    even, odd = add(even, corr_e), add(odd, corr_o)

    def packed(spins):
        return [lane_select(128, 0, 64, spins[0][c], turn(spins[1][c], 64)) for c in range(3)]

    def emit(ref, at, packed_e, packed_o):
        for c in range(3):
            ref[at, c] = dense(packed_e[c], packed_o[c])

    if last:
        *earlier, sent = rest
        at = 0
        for ref in earlier:
            for k in range(ref.shape[0]):
                sent[at] = ref[k]
                at += 1
        emit(sent, at, packed(even), packed(odd))
        return

    message, ends = rest
    at = 0
    if block == 0:
        emit(ends, 0, [own[0, c, 0] for c in range(3)], [own[0, c, 1] for c in range(3)])
        at = 1
    emit(ends, at, packed(even), packed(odd))
    even, odd = heun(even, odd, *sides, COARSE, -1, 2)
    end_e = [s + corr[first_slice + 1, c, 0] for c, s in enumerate(packed(even))]
    end_o = [s + corr[first_slice + 1, c, 1] for c, s in enumerate(packed(odd))]
    emit(ends, at + 1, end_e, end_o)
    for c in range(3):
        message[0, c, 0] = end_e[c]
        message[0, c, 1] = end_o[c]
    message[1] = corr[first_slice + 2]


def assemble(sent, out, layers):
    for comp in range(3):
        for q in range(4):
            tiles = [sent[4 * q + i, comp] for i in range(4)]
            for k in range(4):
                whole = None
                for i in range(4):
                    part = turn(tiles[i], 32 * (i - k))
                    whole = part if whole is None else lane_select(128, 32 * i, 32 * i + 32, part, whole)
                layers[comp, k // 2, q, pl.ds(k % 2, 8, stride=2), :] = whole
            out[0, comp, :, :, 128 * q : 128 * (q + 1)] = layers[comp, :, q]


def both_sides(array):
    count = lax.axis_size("space")
    up = [(i, (i + 1) % count) for i in range(count)]
    down = [(j, i) for i, j in up]
    return lax.ppermute(array, "space", up), lax.ppermute(array, "space", down)


def call(kernel, shapes, in_specs, *args, scratch=()):
    return pl.pallas_call(
        kernel,
        out_shape=[jax.ShapeDtypeStruct(s, F32) for s in shapes],
        in_specs=in_specs,
        out_specs=[VMEM] * len(shapes),
        scratch_shapes=[pltpu.VMEM(s, F32) for s in scratch],
        compiler_params=pltpu.CompilerParams(vmem_limit_bytes=32 * 1024 * 1024),
    )(*args)


def per_device(starts, anisotropy, applied):
    slices = lax.axis_size("tm")
    row = lax.axis_index("tm").astype(jnp.int32)[None]
    own = jnp.concatenate([starts[0], anisotropy[None]], axis=0)
    left, right = both_sides(own)
    payload, windows = call(
        prologue,
        [(slices, 3, 2, 8, 128), (2, 5, 8, 128)],
        [VMEM] * 3 + [SMEM] * 2,
        *(own, left, right, applied, row),
        scratch=[(4, 6, starts.shape[-1] // 128, 16, 128)],
    )
    corr = lax.all_to_all(payload, "tm", 0, 0, tiled=True)
    message = corr[:2]
    done = []
    blocks = slices // 2
    for block in range(blocks):
        left, right = both_sides(message)
        last = block == blocks - 1
        kernel = functools.partial(chain, block, last)
        args = (message, left, right, corr, windows, applied)
        specs = [VMEM] * 5 + [SMEM]
        if last:
            (sent,) = call(kernel, [(slices, 3, 8, 128)], specs + [VMEM] * len(done), *args, *done)
        else:
            message, ends = call(kernel, [message.shape, (3 if block == 0 else 2, 3, 8, 128)], specs, *args)
            done.append(ends)
    sent = lax.all_to_all(sent, "tm", 0, 0, tiled=True)
    (out,) = call(assemble, [starts.shape], [VMEM], sent, scratch=[(3, 2, starts.shape[-1] // 128, 16, 128)])
    return out


def solution(mesh):
    placed = (P("tm", None, "space", None, None), P("space", None, None), P())
    return jax.shard_map(
        per_device,
        mesh=mesh,
        in_specs=placed,
        out_specs=P("tm", None, "space", None, None),
        check_vma=False,
    )
```

```python
import functools

import jax
import jax.numpy as jnp
from jax import lax
from jax.experimental import pallas as pl
from jax.experimental.pallas import tpu as pltpu
from jax.sharding import PartitionSpec as P

DAMPING = 0.1
STEP = 0.02
COARSE = 2 * STEP
GAIN = -1.0 / (1.0 + DAMPING * DAMPING)
F32 = jnp.float32
VMEM = pl.BlockSpec(memory_space=pltpu.VMEM)


def near_odd(even_below, even_here):
    out = []
    for below, here in zip(even_below, even_here):
        pair = below + here
        pair = pair + pltpu.roll(pair, 1, axis=1)
        row = lax.broadcasted_iota(jnp.int32, pair.shape, 0)
        out.append(pair + jnp.where(row < 7, pltpu.roll(pair, 7, axis=0), 0.0))
    return out


def near_even(odd_here, odd_above):
    out = []
    for here, above in zip(odd_here, odd_above):
        pair = here + above
        pair = pair + pltpu.roll(pair, pair.shape[1] - 1, axis=1)
        row = lax.broadcasted_iota(jnp.int32, pair.shape, 0)
        out.append(pair + jnp.where(row > 0, pltpu.roll(pair, 1, axis=0), 0.0))
    return out


def cross(a, b):
    return [a[1] * b[2] - a[2] * b[1], a[2] * b[0] - a[0] * b[2], a[0] * b[1] - a[1] * b[0]]


def bare_rate(spin, near, twice_aniso, applied):
    field = [n + h for n, h in zip(near, applied)]
    field[2] = field[2] + twice_aniso * spin[2]
    turn = cross(spin, field)
    return cross(spin, [f + DAMPING * c for f, c in zip(field, turn)])


def rates(even, odd, aniso_even, aniso_odd, applied, evens, odds):
    rate_even = {x: bare_rate(even[x], near_even(odd[x], odd[x + 1]), aniso_even(x), applied) for x in evens}
    rate_odd = {x: bare_rate(odd[x], near_odd(even[x - 1], even[x]), aniso_odd(x), applied) for x in odds}
    return rate_even, rate_odd


def ahead(spins, rate, length):
    return {x: [s + (length * GAIN) * r for s, r in zip(spins[x], rate[x])] for x in rate}


def finish(spins, first, second, length, planes):
    return {
        x: [s + (0.5 * length * GAIN) * (f + g) for s, f, g in zip(spins[x], first[x], second[x])]
        for x in planes
    }


def heun(even, odd, aniso_even, aniso_odd, applied, length, low, high):
    evens, odds, inner = range(low, high), range(low + 1, high + 1), range(low + 1, high)
    first_e, first_o = rates(even, odd, aniso_even, aniso_odd, applied, evens, odds)
    pred_e, pred_o = ahead(even, first_e, length), ahead(odd, first_o, length)
    second_e, second_o = rates(pred_e, pred_o, aniso_even, aniso_odd, applied, inner, inner)
    return finish(even, first_e, second_e, length, inner), finish(odd, first_o, second_o, length, inner)


def lane_select(tile, low, high, a, b):
    lane = lax.broadcasted_iota(jnp.int32, (8, 128), 1) % tile
    return jnp.where((lane >= low) & (lane < high), a, b)


def tiles_of(wide):
    return [wide[:, 128 * q : 128 * (q + 1)] for q in range(wide.shape[1] // 128)]


def turn(x, by):
    by = by % x.shape[1]
    return pltpu.roll(x, by, axis=1) if by else x


def laid(own, left, right):
    def load(comp, plane, parity):
        ref, at = (left, plane + 2) if plane < 0 else (own, plane) if plane < 2 else (right, plane - 2)
        return ref[comp, at, parity]

    return load


def prologue(own, left, right, field, payload):
    applied = [jnp.concatenate([field[c]] * (own.shape[-1] // 128), axis=1) for c in range(3)]
    load = laid(own, left, right)

    planes = range(-2, 4)
    even = {x: [load(c, x, 0) for c in range(3)] for x in planes}
    odd = {x: [load(c, x, 1) for c in range(3)] for x in planes}

    def aniso_even(x):
        return 2.0 * load(3, x, 0)

    def aniso_odd(x):
        return 2.0 * load(3, x, 1)

    sides = (aniso_even, aniso_odd, applied)
    first_e, first_o = rates(even, odd, *sides, range(-2, 3), range(-1, 4))
    pred_e, pred_o = ahead(even, first_e, STEP), ahead(odd, first_o, STEP)
    second_e, second_o = rates(pred_e, pred_o, *sides, range(-1, 3), range(-1, 3))
    fine_e = finish(even, first_e, second_e, STEP, range(-1, 3))
    fine_o = finish(odd, first_o, second_o, STEP, range(-1, 3))
    fine_e, fine_o = heun(fine_e, fine_o, *sides, STEP, -1, 2)
    pred_e, pred_o = ahead(even, first_e, COARSE), ahead(odd, first_o, COARSE)
    second_e, second_o = rates(pred_e, pred_o, *sides, range(2), range(2))
    coarse_e = finish(even, first_e, second_e, COARSE, range(2))
    coarse_o = finish(odd, first_o, second_o, COARSE, range(2))

    keep = jnp.where(lax.axis_index("tm") == 0, 0.0, 1.0).astype(F32)
    for comp in range(3):
        for parity, fine, coarse in ((0, fine_e, coarse_e), (1, fine_o, coarse_o)):
            moved = []
            for x in range(2):
                wide = fine[x][comp] - keep * coarse[x][comp]
                moved.append(tiles_of(pltpu.roll(wide, 16, axis=1)))
            count = len(moved[0])
            for q in range(count):
                a, b = moved[0][q], moved[1][q]
                after = (q + 1) % count
                c, d = (lane_select(128, 96, 128, m[q], m[after]) for m in moved)
                for i, (p, r) in enumerate(((a, b), (a, b), (a, b), (c, d))):
                    payload[4 * q + i, comp, parity] = lane_select(
                        128, 0, 64, turn(p, -32 * i), turn(r, 64 - 32 * i)
                    )


def window(own, left, right, windows):
    load = laid(own, left, right)
    row = lax.axis_index("tm")
    for at in range(own.shape[-1] // 32):

        @pl.when(row == at)
        def _():
            for parity, planes in ((0, range(-2, 3)), (1, range(-1, 4))):
                for k, x in enumerate(planes):
                    windows[parity, k] = turn(2.0 * load(3, x, parity), 16 - 32 * at)[:, :128]


def dense(even_pair, odd_pair):
    return lane_select(64, 0, 32, turn(even_pair, -16), turn(odd_pair, 16))


def chain(block, last, own, left, right, corr, windows, field, *rest):
    applied = [field[c] for c in range(3)]
    first_slice = 2 * block + 1
    start = block == 0
    reach = range(-1, 3) if last else range(-2, 4)
    inner = range(reach[0] + 1, reach[-1])

    def state(ref, comp, parity):
        return ref[0, comp, parity] if start else ref[parity, comp]

    def spread(parity):
        out = {}
        for ref, base in ((left, -2), (own, 0), (right, 2)):
            pairs = [state(ref, c, parity) for c in range(3)]
            for x, shift in ((base, 0), (base + 1, 64)):
                if x in reach:
                    out[x] = [turn(p, shift) for p in pairs]
        return out

    def extra(parity):
        pairs = [corr[first_slice, c, parity] for c in range(3)]
        out = {0: pairs, 1: [turn(p, 64) for p in pairs]}
        for ref, x, shift in ((left, -1, 64), (right, 2, 0)):
            if x in inner and start:
                out[x] = [turn(ref[1, c, parity], shift) for c in range(3)]
            elif x in inner:
                out[x] = [turn(ref[2, c], 64 * parity) for c in range(3)]
        return out

    def add(spins, more):
        return {x: [s + e for s, e in zip(spins[x], more[x])] for x in inner}

    def aniso_even(x):
        return windows[0, x + 2]

    def aniso_odd(x):
        return windows[1, x + 1]

    sides = (aniso_even, aniso_odd, applied)
    even, odd = heun(spread(0), spread(1), *sides, COARSE, reach[0], reach[-1])
    even, odd = add(even, extra(0)), add(odd, extra(1))

    def packed(spins):
        return [lane_select(128, 0, 64, spins[0][c], turn(spins[1][c], 64)) for c in range(3)]

    def emit(ref, at, packed_e, packed_o):
        for c in range(3):
            ref[at, c] = dense(packed_e[c], packed_o[c])

    if last:
        *earlier, sent = rest
        at = 0
        for ref in earlier:
            for k in range(ref.shape[0]):
                sent[at] = ref[k]
                at += 1
        emit(sent, at, packed(even), packed(odd))
        return

    up, down, ends = rest
    at = 0
    if start:
        emit(ends, 0, [own[0, c, 0] for c in range(3)], [own[0, c, 1] for c in range(3)])
        at = 1
    emit(ends, at, packed(even), packed(odd))
    even, odd = heun(even, odd, *sides, COARSE, -1, 2)
    end_e = [s + corr[first_slice + 1, c, 0] for c, s in enumerate(packed(even))]
    end_o = [s + corr[first_slice + 1, c, 1] for c, s in enumerate(packed(odd))]
    emit(ends, at + 1, end_e, end_o)
    for c in range(3):
        later_e, later_o = corr[first_slice + 2, c, 0], corr[first_slice + 2, c, 1]
        up[2, c] = lane_select(128, 0, 64, turn(later_e, 64), later_o)
        down[2, c] = lane_select(128, 0, 64, later_e, turn(later_o, 64))
        up[0, c], up[1, c] = end_e[c], end_o[c]
        down[0, c], down[1, c] = end_e[c], end_o[c]


def assemble(sent, out, layers):
    for comp in range(3):
        for q in range(4):
            tiles = [sent[4 * q + i, comp] for i in range(4)]
            for k in range(4):
                whole = None
                for i in range(4):
                    part = turn(tiles[i], 32 * (i - k))
                    whole = part if whole is None else lane_select(128, 32 * i, 32 * i + 32, part, whole)
                layers[comp, k // 2, q, pl.ds(k % 2, 8, stride=2), :] = whole
            out[0, comp, :, :, 128 * q : 128 * (q + 1)] = layers[comp, :, q]


def both_sides(to_above, to_below):
    count = lax.axis_size("space")
    up = [(i, (i + 1) % count) for i in range(count)]
    down = [(j, i) for i, j in up]
    return lax.ppermute(to_above, "space", up), lax.ppermute(to_below, "space", down)


def call(kernel, shapes, *args, scratch=()):
    return pl.pallas_call(
        kernel,
        out_shape=[jax.ShapeDtypeStruct(s, F32) for s in shapes],
        in_specs=[VMEM] * len(args),
        out_specs=[VMEM] * len(shapes),
        scratch_shapes=[pltpu.VMEM(s, F32) for s in scratch],
        compiler_params=pltpu.CompilerParams(vmem_limit_bytes=32 * 1024 * 1024),
    )(*args)


def per_device(starts, anisotropy, applied):
    slices = lax.axis_size("tm")
    width = starts.shape[-1]
    own = jnp.concatenate([starts[0], anisotropy[None]], axis=0)
    own = own.reshape(4, 2, 8, 2, width).swapaxes(2, 3)
    field = jnp.broadcast_to(applied[:, None, None], (3, 8, 128))
    slabs = (own, *both_sides(own, own))
    (payload,) = call(prologue, [(slices, 3, 2, 8, 128)], *slabs, field)
    (windows,) = call(window, [(2, 5, 8, 128)], *slabs)
    corr = lax.all_to_all(payload, "tm", 0, 0, tiled=True)
    up = down = corr[:2]
    done = []
    blocks = slices // 2
    for block in range(blocks):
        last = block == blocks - 1
        kernel = functools.partial(chain, block, last)
        args = (up, *both_sides(up, down), corr, windows, field)
        if last:
            (sent,) = call(kernel, [(slices, 3, 8, 128)], *args, *done)
        else:
            shapes = [(3, 3, 8, 128)] * 2 + [(3 if block == 0 else 2, 3, 8, 128)]
            up, down, ends = call(kernel, shapes, *args)
            done.append(ends)
    sent = lax.all_to_all(sent, "tm", 0, 0, tiled=True)
    (out,) = call(assemble, [starts.shape], sent, scratch=[(3, 2, width // 128, 16, 128)])
    return out


def solution(mesh):
    placed = (P("tm", None, "space", None, None), P("space", None, None), P())
    return jax.shard_map(
        per_device,
        mesh=mesh,
        in_specs=placed,
        out_specs=P("tm", None, "space", None, None),
        check_vma=False,
    )
```

```python
import functools

import jax
import jax.numpy as jnp
from jax import lax
from jax.experimental import pallas as pl
from jax.experimental.pallas import tpu as pltpu
from jax.sharding import PartitionSpec as P

DAMPING = 0.1
STEP = 0.02
COARSE = 2 * STEP
GAIN = -1.0 / (1.0 + DAMPING * DAMPING)
F32 = jnp.float32
VMEM = pl.BlockSpec(memory_space=pltpu.VMEM)


def near_odd(even_below, even_here):
    out = []
    for below, here in zip(even_below, even_here):
        pair = below + here
        pair = pair + pltpu.roll(pair, 1, axis=1)
        row = lax.broadcasted_iota(jnp.int32, pair.shape, 0)
        out.append(pair + jnp.where(row < 7, pltpu.roll(pair, 7, axis=0), 0.0))
    return out


def near_even(odd_here, odd_above):
    out = []
    for here, above in zip(odd_here, odd_above):
        pair = here + above
        pair = pair + pltpu.roll(pair, pair.shape[1] - 1, axis=1)
        row = lax.broadcasted_iota(jnp.int32, pair.shape, 0)
        out.append(pair + jnp.where(row > 0, pltpu.roll(pair, 1, axis=0), 0.0))
    return out


def cross(a, b):
    return [a[1] * b[2] - a[2] * b[1], a[2] * b[0] - a[0] * b[2], a[0] * b[1] - a[1] * b[0]]


def bare_rate(spin, near, twice_aniso, applied):
    field = [n + h for n, h in zip(near, applied)]
    field[2] = field[2] + twice_aniso * spin[2]
    turn = cross(spin, field)
    return cross(spin, [f + DAMPING * c for f, c in zip(field, turn)])


def rates(even, odd, aniso_even, aniso_odd, applied, evens, odds):
    rate_even = {x: bare_rate(even[x], near_even(odd[x], odd[x + 1]), aniso_even(x), applied) for x in evens}
    rate_odd = {x: bare_rate(odd[x], near_odd(even[x - 1], even[x]), aniso_odd(x), applied) for x in odds}
    return rate_even, rate_odd


def ahead(spins, rate, length):
    return {x: [s + (length * GAIN) * r for s, r in zip(spins[x], rate[x])] for x in rate}


def finish(spins, first, second, length, planes):
    return {
        x: [s + (0.5 * length * GAIN) * (f + g) for s, f, g in zip(spins[x], first[x], second[x])]
        for x in planes
    }


def heun(even, odd, aniso_even, aniso_odd, applied, length, low, high):
    evens, odds, inner = range(low, high), range(low + 1, high + 1), range(low + 1, high)
    first_e, first_o = rates(even, odd, aniso_even, aniso_odd, applied, evens, odds)
    pred_e, pred_o = ahead(even, first_e, length), ahead(odd, first_o, length)
    second_e, second_o = rates(pred_e, pred_o, aniso_even, aniso_odd, applied, inner, inner)
    return finish(even, first_e, second_e, length, inner), finish(odd, first_o, second_o, length, inner)


def lane_select(tile, low, high, a, b):
    lane = lax.broadcasted_iota(jnp.int32, (8, 128), 1) % tile
    return jnp.where((lane >= low) & (lane < high), a, b)


def tiles_of(wide):
    return [wide[:, 128 * q : 128 * (q + 1)] for q in range(wide.shape[1] // 128)]


def turn(x, by):
    by = by % x.shape[1]
    return pltpu.roll(x, by, axis=1) if by else x


def laid(own, left, right):
    def load(comp, plane, parity):
        ref, at = (left, plane + 2) if plane < 0 else (own, plane) if plane < 2 else (right, plane - 2)
        return ref[comp, at, parity]

    return load


def prologue(own, left, right, field, payload):
    applied = [jnp.concatenate([field[c]] * (own.shape[-1] // 128), axis=1) for c in range(3)]
    load = laid(own, left, right)

    planes = range(-2, 4)
    even = {x: [load(c, x, 0) for c in range(3)] for x in planes}
    odd = {x: [load(c, x, 1) for c in range(3)] for x in planes}

    def aniso_even(x):
        return 2.0 * load(3, x, 0)

    def aniso_odd(x):
        return 2.0 * load(3, x, 1)

    sides = (aniso_even, aniso_odd, applied)
    first_e, first_o = rates(even, odd, *sides, range(-2, 3), range(-1, 4))
    pred_e, pred_o = ahead(even, first_e, STEP), ahead(odd, first_o, STEP)
    second_e, second_o = rates(pred_e, pred_o, *sides, range(-1, 3), range(-1, 3))
    fine_e = finish(even, first_e, second_e, STEP, range(-1, 3))
    fine_o = finish(odd, first_o, second_o, STEP, range(-1, 3))
    fine_e, fine_o = heun(fine_e, fine_o, *sides, STEP, -1, 2)
    pred_e, pred_o = ahead(even, first_e, COARSE), ahead(odd, first_o, COARSE)
    second_e, second_o = rates(pred_e, pred_o, *sides, range(2), range(2))
    coarse_e = finish(even, first_e, second_e, COARSE, range(2))
    coarse_o = finish(odd, first_o, second_o, COARSE, range(2))

    keep = jnp.where(lax.axis_index("tm") == 0, 0.0, 1.0).astype(F32)
    for comp in range(3):
        for x in range(2):
            evens = tiles_of(fine_e[x][comp] - keep * coarse_e[x][comp])
            odds = [turn(t, 64) for t in tiles_of(fine_o[x][comp] - keep * coarse_o[x][comp])]
            for at in range(payload.shape[0]):
                payload[at, x, comp] = cut(evens, odds, at)


def cut(evens, odds, at):
    q, part = divmod(at, 4)
    if part == 0:
        return lanes(48, lanes(64, lanes(112, evens[q - 1], odds[q]), odds[q - 1]), evens[q])
    if part == 3:
        after = (q + 1) % len(evens)
        return lanes(16, lanes(64, lanes(80, evens[q], odds[after]), odds[q]), evens[after])
    first = 32 * part - 16
    return lanes(first, lanes(first + 64, odds[q], evens[q]), odds[q])


def lanes(count, here, before):
    return jnp.where(lax.broadcasted_iota(jnp.int32, (8, 128), 1) < count, before, here)


def logical_lane(row):
    return (lax.broadcasted_iota(jnp.int32, (8, 128), 1) + 16 - 32 * (row % 4)) & 127


def window(own, left, right, windows):
    load = laid(own, left, right)
    row = lax.axis_index("tm")
    windows[6] = logical_lane(row).astype(F32)
    for at in range(own.shape[-1] // 32):

        @pl.when(row == at)
        def _():
            for k in range(6):
                even, odd = (tiles_of(2.0 * load(3, k - 2, parity)) for parity in range(2))
                windows[k] = cut(even, [turn(t, 64) for t in odd], at)


def near_pair(pair, is_even):
    row = lax.broadcasted_iota(jnp.int32, (8, 128), 0)
    lane = lax.broadcasted_iota(jnp.int32, (8, 128), 1)
    source = (lane + jnp.where(is_even, 65, 63)) & 127
    out = []
    for p in pair:
        near = turn(p, 64) + jnp.take_along_axis(p, source, axis=1)
        lower = jnp.where(is_even & (row > 0), pltpu.roll(near, 1, axis=0), 0.0)
        out.append(near + jnp.where(~is_even & (row < 7), pltpu.roll(near, 7, axis=0), lower))
    return out


def pair_heun(spins, aniso, applied, is_even, length, low, high):
    def pick(a, b):
        return [jnp.where(is_even, p, r) for p, r in zip(a, b)]

    def plus(a, b):
        return [p + r for p, r in zip(a, b)]

    def rate(spins, x):
        pair = plus(spins[x], pick(spins[x - 1], spins[x + 1]))
        return bare_rate(spins[x], near_pair(pair, is_even), aniso(x), applied)

    inner = range(low + 1, high)
    first = {x: rate(spins, x) for x in inner}
    pair = pick(plus(spins[high - 1], spins[high]), plus(spins[low], spins[low + 1]))
    edge = pick(spins[low], spins[high])
    edge_aniso = jnp.where(is_even, aniso(low), aniso(high))
    edge_rate = bare_rate(edge, near_pair(pair, is_even), edge_aniso, applied)
    predicted = ahead(spins, first, length)
    predicted[low] = predicted[high] = ahead({0: edge}, {0: edge_rate}, length)[0]
    second = {x: rate(predicted, x) for x in inner}
    return finish(spins, first, second, length, inner)


def emit(ref, at, below, above, logical):
    inside = (logical & 63 >= 16) & (logical & 63 < 48)
    for c in range(3):
        ref[at, c] = jnp.where(inside, below[c], turn(above[c], 32))


def triple(ref, *at):
    return [ref[(*at, c)] for c in range(3)]


def chain(block, blocks, own, left, right, corr, windows, field, *rest):
    applied = [field[c] for c in range(3)]
    is_even = windows[6] < 64.0
    first_slice = 2 * block + 1
    start, last = block == 0, block == blocks - 1

    if last:
        below, above = own
        spins = {-1: triple(left, 0), 0: triple(below, 0), 1: triple(above, 0), 2: triple(right, 0)}
    elif start:
        spins = {base + k: triple(ref, 0, k) for ref, base in ((left, -2), (own, 0), (right, 2)) for k in range(2)}
        extra = {-1: triple(left, 1, 1), 2: triple(right, 1, 0)}
    else:
        spins = {base + k: triple(ref, k) for ref, base in ((left, -2), (own, 0), (right, 2)) for k in range(2)}
        extra = {-1: triple(left, 2), 2: triple(right, 2)}

    def added(spins, extra):
        return {x: [s + e for s, e in zip(spins[x], extra[x])] for x in spins}

    def aniso(x):
        return windows[x + 2]

    reach = (-1, 2) if last else (-2, 3)
    inside = {x: triple(corr, first_slice, x) for x in range(2)}
    ends = pair_heun(spins, aniso, applied, is_even, COARSE, *reach)
    if last:
        earlier, sent = rest
        ends = added(ends, inside)
        emit(sent, sent.shape[0] - 1, ends[0], ends[1], windows[6].astype(jnp.int32))
        return

    up, down, middle = rest
    ends = added(ends, inside | extra)
    for x in range(2):
        for c in range(3):
            middle[x, c] = ends[x][c]
    inside = {x: triple(corr, first_slice + 1, x) for x in range(2)}
    ends = added(pair_heun(ends, aniso, applied, is_even, COARSE, -1, 2), inside)
    for c in range(3):
        if block == blocks - 2:
            up[0, c], down[0, c] = ends[1][c], ends[0][c]
        else:
            for x in range(2):
                up[x, c] = down[x, c] = ends[x][c]
            up[2, c] = corr[first_slice + 2, 1, c]
            down[2, c] = corr[first_slice + 2, 0, c]


def final(block, blocks, below, above, *rest):
    chain(block, blocks, (below, above), *rest)


def pack(corr, windows, below, above, *rest):
    *kept, sent = rest
    logical = windows[6].astype(jnp.int32)
    emit(sent, 0, triple(corr, 0, 0), triple(corr, 0, 1), logical)
    for k, ref in enumerate(kept):
        emit(sent, k + 1, triple(ref, 0), triple(ref, 1), logical)
    emit(sent, len(kept) + 1, triple(below, 0), triple(above, 0), logical)


def assemble(sent, out, layers):
    for comp in range(3):
        for q in range(layers.shape[2]):
            tiles = [sent[4 * q + i, comp] for i in range(4)]
            for k in range(4):
                whole = tiles[0]
                for i in range(1, 4):
                    at = 32 * ((k + i) % 4)
                    whole = lane_select(128, at, at + 32, tiles[i], whole)
                layers[comp, k % 2, q, pl.ds(k // 2, 8, stride=2), :] = turn(whole, -32 * k)
            out[0, comp, :, :, 128 * q : 128 * (q + 1)] = layers[comp, :, q]


def both_sides(to_above, to_below):
    count = lax.axis_size("space")
    up = [(i, (i + 1) % count) for i in range(count)]
    down = [(j, i) for i, j in up]
    return lax.ppermute(to_above, "space", up), lax.ppermute(to_below, "space", down)


def call(kernel, shapes, *args, scratch=(), **more):
    return pl.pallas_call(
        kernel,
        out_shape=[jax.ShapeDtypeStruct(s, F32) for s in shapes],
        in_specs=[VMEM] * len(args),
        out_specs=[VMEM] * len(shapes),
        scratch_shapes=[pltpu.VMEM(s, F32) for s in scratch],
        **more,
        compiler_params=pltpu.CompilerParams(vmem_limit_bytes=32 * 1024 * 1024),
    )(*args)


def per_device(starts, anisotropy, applied):
    slices = lax.axis_size("tm")
    width = starts.shape[-1]
    own = jnp.concatenate([starts[0], anisotropy[None]], axis=0)
    own = own.reshape(4, 2, 8, 2, width).swapaxes(2, 3)
    field = jnp.broadcast_to(applied[:, None, None], (3, 8, 128))
    slabs = (own, *both_sides(own, own))
    (payload,) = call(prologue, [(slices, 2, 3, 8, 128)], *slabs, field)
    (windows,) = call(window, [(7, 8, 128)], *slabs)
    corr = lax.all_to_all(payload, "tm", 0, 0, tiled=True)
    up = down = corr[:2]
    kept = []
    blocks = slices // 2
    for block in range(blocks - 1):
        kernel = functools.partial(chain, block, blocks)
        ahead_of_last = block == blocks - 2
        shapes = [(1 if ahead_of_last else 3, 3, 8, 128)] * 2 + [(2, 3, 8, 128)]
        up, down, middle = call(kernel, shapes, up, *both_sides(up, down), corr, windows, field)
        kept += [middle] if ahead_of_last else [middle, up]
    left, right = both_sides(up, down)
    (sent,) = call(pack, [(slices, 3, 8, 128)], corr, windows, down, up, *kept)
    kernel = functools.partial(final, blocks - 1, blocks)
    (sent,) = call(
        kernel, [sent.shape], down, up, left, right, corr, windows, field, sent, input_output_aliases={7: 0}
    )
    sent = lax.all_to_all(sent, "tm", 0, 0, tiled=True)
    (out,) = call(assemble, [starts.shape], sent, scratch=[(3, 2, width // 128, 16, 128)])
    return out


def solution(mesh):
    placed = (P("tm", None, "space", None, None), P("space", None, None), P())
    return jax.shard_map(
        per_device,
        mesh=mesh,
        in_specs=placed,
        out_specs=P("tm", None, "space", None, None),
        check_vma=False,
    )
```

```python
import functools

import jax
import jax.numpy as jnp
from jax import lax
from jax.experimental import pallas as pl
from jax.experimental.pallas import tpu as pltpu
from jax.sharding import PartitionSpec as P

DAMPING = 0.1
STEP = 0.02
COARSE = 2 * STEP
GAIN = -1.0 / (1.0 + DAMPING * DAMPING)
F32 = jnp.float32
VMEM = pl.BlockSpec(memory_space=pltpu.VMEM)


def near_odd(even_below, even_here):
    out = []
    for below, here in zip(even_below, even_here):
        pair = below + here
        pair = pair + pltpu.roll(pair, 1, axis=1)
        row = lax.broadcasted_iota(jnp.int32, pair.shape, 0)
        out.append(pair + jnp.where(row < 7, pltpu.roll(pair, 7, axis=0), 0.0))
    return out


def near_even(odd_here, odd_above):
    out = []
    for here, above in zip(odd_here, odd_above):
        pair = here + above
        pair = pair + pltpu.roll(pair, pair.shape[1] - 1, axis=1)
        row = lax.broadcasted_iota(jnp.int32, pair.shape, 0)
        out.append(pair + jnp.where(row > 0, pltpu.roll(pair, 1, axis=0), 0.0))
    return out


def cross(a, b):
    return [a[1] * b[2] - a[2] * b[1], a[2] * b[0] - a[0] * b[2], a[0] * b[1] - a[1] * b[0]]


def bare_rate(spin, near, twice_aniso, applied):
    field = [n + h for n, h in zip(near, applied)]
    field[2] = field[2] + twice_aniso * spin[2]
    turn = cross(spin, field)
    return cross(spin, [f + DAMPING * c for f, c in zip(field, turn)])


def rates(even, odd, aniso_even, aniso_odd, applied, evens, odds):
    rate_even = {x: bare_rate(even[x], near_even(odd[x], odd[x + 1]), aniso_even(x), applied) for x in evens}
    rate_odd = {x: bare_rate(odd[x], near_odd(even[x - 1], even[x]), aniso_odd(x), applied) for x in odds}
    return rate_even, rate_odd


def ahead(spins, rate, length):
    return {x: [s + (length * GAIN) * r for s, r in zip(spins[x], rate[x])] for x in rate}


def finish(spins, first, second, length, planes):
    return {
        x: [s + (0.5 * length * GAIN) * (f + g) for s, f, g in zip(spins[x], first[x], second[x])]
        for x in planes
    }


def heun(even, odd, aniso_even, aniso_odd, applied, length, low, high):
    evens, odds, inner = range(low, high), range(low + 1, high + 1), range(low + 1, high)
    first_e, first_o = rates(even, odd, aniso_even, aniso_odd, applied, evens, odds)
    pred_e, pred_o = ahead(even, first_e, length), ahead(odd, first_o, length)
    second_e, second_o = rates(pred_e, pred_o, aniso_even, aniso_odd, applied, inner, inner)
    return finish(even, first_e, second_e, length, inner), finish(odd, first_o, second_o, length, inner)


def lane_select(tile, low, high, a, b):
    lane = lax.broadcasted_iota(jnp.int32, (8, 128), 1) % tile
    return jnp.where((lane >= low) & (lane < high), a, b)


def tiles_of(wide):
    return [wide[:, 128 * q : 128 * (q + 1)] for q in range(wide.shape[1] // 128)]


def turn(x, by):
    by = by % x.shape[1]
    return pltpu.roll(x, by, axis=1) if by else x


def by_parity(spins, aniso, out, layers):
    for comp in range(4):
        for x in range(2):
            for q in range(layers.shape[2]):
                at = slice(128 * q, 128 * (q + 1))
                layers[comp, x, q] = aniso[x, :, at] if comp == 3 else spins[comp, x, :, at]
                for parity in range(2):
                    out[comp, x, parity, :, at] = layers[comp, x, q, pl.ds(parity, 8, stride=2), :]


def prepare(spins, aniso, applied, out, field, layers):
    by_parity(spins, aniso, out, layers)
    for c in range(3):
        field[c] = jnp.full(field.shape[1:], applied[c], F32)


def beside(own, sides):
    def load(comp, plane, parity):
        ref, at = (sides.at[0], plane + 2) if plane < 0 else (own, plane) if plane < 2 else (sides.at[1], plane - 2)
        return ref[comp, at, parity]

    return load


def prologue(own, left, left_a, right, right_a, field, payload, sides, layers):
    by_parity(left, left_a, sides.at[0], layers.at[0])
    by_parity(right, right_a, sides.at[1], layers.at[1])
    load = beside(own, sides)
    applied = [jnp.concatenate([field[c]] * layers.shape[3], axis=1) for c in range(3)]

    planes = range(-2, 4)
    even = {x: [load(c, x, 0) for c in range(3)] for x in planes}
    odd = {x: [load(c, x, 1) for c in range(3)] for x in planes}

    def aniso_even(x):
        return 2.0 * load(3, x, 0)

    def aniso_odd(x):
        return 2.0 * load(3, x, 1)

    sides = (aniso_even, aniso_odd, applied)
    first_e, first_o = rates(even, odd, *sides, range(-2, 3), range(-1, 4))
    pred_e, pred_o = ahead(even, first_e, STEP), ahead(odd, first_o, STEP)
    second_e, second_o = rates(pred_e, pred_o, *sides, range(-1, 3), range(-1, 3))
    fine_e = finish(even, first_e, second_e, STEP, range(-1, 3))
    fine_o = finish(odd, first_o, second_o, STEP, range(-1, 3))
    fine_e, fine_o = heun(fine_e, fine_o, *sides, STEP, -1, 2)
    pred_e, pred_o = ahead(even, first_e, COARSE), ahead(odd, first_o, COARSE)
    second_e, second_o = rates(pred_e, pred_o, *sides, range(2), range(2))
    coarse_e = finish(even, first_e, second_e, COARSE, range(2))
    coarse_o = finish(odd, first_o, second_o, COARSE, range(2))

    keep = jnp.where(lax.axis_index("tm") == 0, 0.0, 1.0).astype(F32)
    for comp in range(3):
        for x in range(2):
            evens = tiles_of(fine_e[x][comp] - keep * coarse_e[x][comp])
            odds = [turn(t, 64) for t in tiles_of(fine_o[x][comp] - keep * coarse_o[x][comp])]
            for at in range(payload.shape[0]):
                payload[at, x, comp] = cut(evens, odds, at)


def cut(evens, odds, at):
    q, part = divmod(at, 4)
    if part == 0:
        return lanes(48, lanes(64, lanes(112, evens[q - 1], odds[q]), odds[q - 1]), evens[q])
    if part == 3:
        after = (q + 1) % len(evens)
        return lanes(16, lanes(64, lanes(80, evens[q], odds[after]), odds[q]), evens[after])
    first = 32 * part - 16
    return lanes(first, lanes(first + 64, odds[q], evens[q]), odds[q])


def lanes(count, here, before):
    return jnp.where(lax.broadcasted_iota(jnp.int32, (8, 128), 1) < count, before, here)


def logical_lane(row):
    return (lax.broadcasted_iota(jnp.int32, (8, 128), 1) + 16 - 32 * (row % 4)) & 127


def window(own, sides, windows):
    load = beside(own, sides)
    row = lax.axis_index("tm")
    windows[6] = logical_lane(row).astype(F32)
    for at in range(own.shape[-1] // 32):

        @pl.when(row == at)
        def _():
            for k in range(6):
                even, odd = (tiles_of(2.0 * load(3, k - 2, parity)) for parity in range(2))
                windows[k] = cut(even, [turn(t, 64) for t in odd], at)


def near_pair(pair, is_even):
    row = lax.broadcasted_iota(jnp.int32, (8, 128), 0)
    lane = lax.broadcasted_iota(jnp.int32, (8, 128), 1)
    source = (lane + jnp.where(is_even, 65, 63)) & 127
    out = []
    for p in pair:
        near = turn(p, 64) + jnp.take_along_axis(p, source, axis=1)
        lower = jnp.where(is_even & (row > 0), pltpu.roll(near, 1, axis=0), 0.0)
        out.append(near + jnp.where(~is_even & (row < 7), pltpu.roll(near, 7, axis=0), lower))
    return out


def pair_heun(spins, aniso, applied, is_even, length, low, high):
    def pick(a, b):
        return [jnp.where(is_even, p, r) for p, r in zip(a, b)]

    def plus(a, b):
        return [p + r for p, r in zip(a, b)]

    def rate(spins, x):
        pair = plus(spins[x], pick(spins[x - 1], spins[x + 1]))
        return bare_rate(spins[x], near_pair(pair, is_even), aniso(x), applied)

    inner = range(low + 1, high)
    first = {x: rate(spins, x) for x in inner}
    pair = pick(plus(spins[high - 1], spins[high]), plus(spins[low], spins[low + 1]))
    edge = pick(spins[low], spins[high])
    edge_aniso = jnp.where(is_even, aniso(low), aniso(high))
    edge_rate = bare_rate(edge, near_pair(pair, is_even), edge_aniso, applied)
    predicted = ahead(spins, first, length)
    predicted[low] = predicted[high] = ahead({0: edge}, {0: edge_rate}, length)[0]
    second = {x: rate(predicted, x) for x in inner}
    return finish(spins, first, second, length, inner)


def emit(ref, at, below, above, logical):
    inside = (logical & 63 >= 16) & (logical & 63 < 48)
    for c in range(3):
        ref[at, c] = jnp.where(inside, below[c], turn(above[c], 32))


def triple(ref, *at):
    return [ref[(*at, c)] for c in range(3)]


def chain(block, blocks, own, left, right, corr, windows, field, *rest):
    applied = [field[c] for c in range(3)]
    is_even = windows[6] < 64.0
    first_slice = 2 * block + 1
    start, last = block == 0, block == blocks - 1

    if last:
        below, above = own
        spins = {-1: triple(left, 0), 0: triple(below, 0), 1: triple(above, 0), 2: triple(right, 0)}
    elif start:
        spins = {base + k: triple(ref, 0, k) for ref, base in ((left, -2), (own, 0), (right, 2)) for k in range(2)}
        extra = {-1: triple(left, 1, 1), 2: triple(right, 1, 0)}
    else:
        spins = {base + k: triple(ref, k) for ref, base in ((left, -2), (own, 0), (right, 2)) for k in range(2)}
        extra = {-1: triple(left, 2), 2: triple(right, 2)}

    def added(spins, extra):
        return {x: [s + e for s, e in zip(spins[x], extra[x])] for x in spins}

    def aniso(x):
        return windows[x + 2]

    reach = (-1, 2) if last else (-2, 3)
    inside = {x: triple(corr, first_slice, x) for x in range(2)}
    ends = pair_heun(spins, aniso, applied, is_even, COARSE, *reach)
    if last:
        earlier, sent = rest
        ends = added(ends, inside)
        emit(sent, sent.shape[0] - 1, ends[0], ends[1], windows[6].astype(jnp.int32))
        return

    up, down, middle = rest
    ends = added(ends, inside | extra)
    for x in range(2):
        for c in range(3):
            middle[x, c] = ends[x][c]
    inside = {x: triple(corr, first_slice + 1, x) for x in range(2)}
    ends = added(pair_heun(ends, aniso, applied, is_even, COARSE, -1, 2), inside)
    for c in range(3):
        if block == blocks - 2:
            up[0, c], down[0, c] = ends[1][c], ends[0][c]
        else:
            for x in range(2):
                up[x, c] = down[x, c] = ends[x][c]
            up[2, c] = corr[first_slice + 2, 1, c]
            down[2, c] = corr[first_slice + 2, 0, c]


def final(block, blocks, below, above, *rest):
    chain(block, blocks, (below, above), *rest)


def pack(corr, windows, below, above, *rest):
    *kept, sent = rest
    logical = windows[6].astype(jnp.int32)
    emit(sent, 0, triple(corr, 0, 0), triple(corr, 0, 1), logical)
    for k, ref in enumerate(kept):
        emit(sent, k + 1, triple(ref, 0), triple(ref, 1), logical)
    emit(sent, len(kept) + 1, triple(below, 0), triple(above, 0), logical)


def assemble(sent, out, layers):
    for comp in range(3):
        for q in range(layers.shape[2]):
            tiles = [sent[4 * q + i, comp] for i in range(4)]
            for k in range(4):
                whole = tiles[0]
                for i in range(1, 4):
                    at = 32 * ((k + i) % 4)
                    whole = lane_select(128, at, at + 32, tiles[i], whole)
                layers[comp, k % 2, q, pl.ds(k // 2, 8, stride=2), :] = turn(whole, -32 * k)
            out[0, comp, :, :, 128 * q : 128 * (q + 1)] = layers[comp, :, q]


def both_sides(to_above, to_below):
    count = lax.axis_size("space")
    up = [(i, (i + 1) % count) for i in range(count)]
    down = [(j, i) for i, j in up]
    return lax.ppermute(to_above, "space", up), lax.ppermute(to_below, "space", down)


def call(kernel, shapes, *args, scratch=(), **more):
    return pl.pallas_call(
        kernel,
        out_shape=[jax.ShapeDtypeStruct(s, F32) for s in shapes],
        out_specs=[VMEM] * len(shapes),
        scratch_shapes=[pltpu.VMEM(s, F32) for s in scratch],
        **({"in_specs": [VMEM] * len(args)} | more),
        compiler_params=pltpu.CompilerParams(vmem_limit_bytes=32 * 1024 * 1024),
    )(*args)


def per_device(starts, anisotropy, applied):
    slices = lax.axis_size("tm")
    width = starts.shape[-1]
    layers = (4, 2, width // 128, 16, 128)
    left, right = both_sides(starts[0], starts[0])
    left_a, right_a = both_sides(anisotropy, anisotropy)
    own, field = call(
        prepare,
        [(4, 2, 2, 8, width), (3, 8, 128)],
        *(starts[0], anisotropy, applied),
        scratch=[layers],
        in_specs=[VMEM] * 2 + [pl.BlockSpec(memory_space=pltpu.SMEM)],
    )
    payload, sides = call(
        prologue,
        [(slices, 2, 3, 8, 128), (2, 4, 2, 2, 8, width)],
        *(own, left, left_a, right, right_a, field),
        scratch=[(2, *layers)],
    )
    (windows,) = call(window, [(7, 8, 128)], own, sides)
    corr = lax.all_to_all(payload, "tm", 0, 0, tiled=True)
    up = down = corr[:2]
    kept = []
    blocks = slices // 2
    for block in range(blocks - 1):
        kernel = functools.partial(chain, block, blocks)
        ahead_of_last = block == blocks - 2
        shapes = [(1 if ahead_of_last else 3, 3, 8, 128)] * 2 + [(2, 3, 8, 128)]
        up, down, middle = call(kernel, shapes, up, *both_sides(up, down), corr, windows, field)
        kept += [middle] if ahead_of_last else [middle, up]
    left, right = both_sides(up, down)
    (sent,) = call(pack, [(slices, 3, 8, 128)], corr, windows, down, up, *kept)
    kernel = functools.partial(final, blocks - 1, blocks)
    (sent,) = call(
        kernel, [sent.shape], down, up, left, right, corr, windows, field, sent, input_output_aliases={7: 0}
    )
    sent = lax.all_to_all(sent, "tm", 0, 0, tiled=True)
    (out,) = call(assemble, [starts.shape], sent, scratch=[(3, 2, width // 128, 16, 128)])
    return out


def solution(mesh):
    placed = (P("tm", None, "space", None, None), P("space", None, None), P())
    return jax.shard_map(
        per_device,
        mesh=mesh,
        in_specs=placed,
        out_specs=P("tm", None, "space", None, None),
        check_vma=False,
    )
```

```python
import functools

import jax
import jax.numpy as jnp
from jax import lax
from jax.experimental import pallas as pl
from jax.experimental.pallas import tpu as pltpu
from jax.sharding import PartitionSpec as P

DAMPING = 0.1
STEP = 0.02
COARSE = 2 * STEP
GAIN = -1.0 / (1.0 + DAMPING * DAMPING)
F32 = jnp.float32
VMEM = pl.BlockSpec(memory_space=pltpu.VMEM)


def near_odd(even_below, even_here):
    out = []
    for below, here in zip(even_below, even_here):
        pair = below + here
        pair = pair + pltpu.roll(pair, 1, axis=1)
        row = lax.broadcasted_iota(jnp.int32, pair.shape, 0)
        out.append(pair + jnp.where(row < 7, pltpu.roll(pair, 7, axis=0), 0.0))
    return out


def near_even(odd_here, odd_above):
    out = []
    for here, above in zip(odd_here, odd_above):
        pair = here + above
        pair = pair + pltpu.roll(pair, pair.shape[1] - 1, axis=1)
        row = lax.broadcasted_iota(jnp.int32, pair.shape, 0)
        out.append(pair + jnp.where(row > 0, pltpu.roll(pair, 1, axis=0), 0.0))
    return out


def cross(a, b):
    return [a[1] * b[2] - a[2] * b[1], a[2] * b[0] - a[0] * b[2], a[0] * b[1] - a[1] * b[0]]


def bare_rate(spin, near, twice_aniso, applied):
    field = [n + h for n, h in zip(near, applied)]
    field[2] = field[2] + twice_aniso * spin[2]
    turn = cross(spin, field)
    return cross(spin, [f + DAMPING * c for f, c in zip(field, turn)])


def rates(even, odd, aniso_even, aniso_odd, applied, evens, odds):
    rate_even = {x: bare_rate(even[x], near_even(odd[x], odd[x + 1]), aniso_even(x), applied) for x in evens}
    rate_odd = {x: bare_rate(odd[x], near_odd(even[x - 1], even[x]), aniso_odd(x), applied) for x in odds}
    return rate_even, rate_odd


def ahead(spins, rate, length):
    return {x: [s + (length * GAIN) * r for s, r in zip(spins[x], rate[x])] for x in rate}


def finish(spins, first, second, length, planes):
    return {
        x: [s + (0.5 * length * GAIN) * (f + g) for s, f, g in zip(spins[x], first[x], second[x])]
        for x in planes
    }


def heun(even, odd, aniso_even, aniso_odd, applied, length, low, high):
    evens, odds, inner = range(low, high), range(low + 1, high + 1), range(low + 1, high)
    first_e, first_o = rates(even, odd, aniso_even, aniso_odd, applied, evens, odds)
    pred_e, pred_o = ahead(even, first_e, length), ahead(odd, first_o, length)
    second_e, second_o = rates(pred_e, pred_o, aniso_even, aniso_odd, applied, inner, inner)
    return finish(even, first_e, second_e, length, inner), finish(odd, first_o, second_o, length, inner)


def lane_select(tile, low, high, a, b):
    lane = lax.broadcasted_iota(jnp.int32, (8, 128), 1) % tile
    return jnp.where((lane >= low) & (lane < high), a, b)


def tiles_of(wide):
    return [wide[:, 128 * q : 128 * (q + 1)] for q in range(wide.shape[1] // 128)]


def turn(x, by):
    by = by % x.shape[1]
    return pltpu.roll(x, by, axis=1) if by else x


def by_parity(slab, out, layers):
    for comp in range(4):
        for x in range(2):
            for q in range(layers.shape[2]):
                at = slice(128 * q, 128 * (q + 1))
                layers[comp, x, q] = slab[comp, x, :, at]
                for parity in range(2):
                    out[comp, x, parity, :, at] = layers[comp, x, q, pl.ds(parity, 8, stride=2), :]


def prepare(slab, applied, out, field, layers):
    by_parity(slab, out, layers)
    for c in range(3):
        field[c] = jnp.full(field.shape[1:], applied[c], F32)


def beside(own, sides):
    def load(comp, plane, parity):
        ref, at = (sides.at[0], plane + 2) if plane < 0 else (own, plane) if plane < 2 else (sides.at[1], plane - 2)
        return ref[comp, at, parity]

    return load


def prologue(own, left, right, field, payload, sides, layers):
    by_parity(left, sides.at[0], layers.at[0])
    by_parity(right, sides.at[1], layers.at[1])
    load = beside(own, sides)
    applied = [jnp.concatenate([field[c]] * layers.shape[3], axis=1) for c in range(3)]

    planes = range(-2, 4)
    even = {x: [load(c, x, 0) for c in range(3)] for x in planes}
    odd = {x: [load(c, x, 1) for c in range(3)] for x in planes}

    def aniso_even(x):
        return 2.0 * load(3, x, 0)

    def aniso_odd(x):
        return 2.0 * load(3, x, 1)

    sides = (aniso_even, aniso_odd, applied)
    first_e, first_o = rates(even, odd, *sides, range(-2, 3), range(-1, 4))
    pred_e, pred_o = ahead(even, first_e, STEP), ahead(odd, first_o, STEP)
    second_e, second_o = rates(pred_e, pred_o, *sides, range(-1, 3), range(-1, 3))
    fine_e = finish(even, first_e, second_e, STEP, range(-1, 3))
    fine_o = finish(odd, first_o, second_o, STEP, range(-1, 3))
    fine_e, fine_o = heun(fine_e, fine_o, *sides, STEP, -1, 2)
    pred_e, pred_o = ahead(even, first_e, COARSE), ahead(odd, first_o, COARSE)
    second_e, second_o = rates(pred_e, pred_o, *sides, range(2), range(2))
    coarse_e = finish(even, first_e, second_e, COARSE, range(2))
    coarse_o = finish(odd, first_o, second_o, COARSE, range(2))

    keep = jnp.where(lax.axis_index("tm") == 0, 0.0, 1.0).astype(F32)
    for comp in range(3):
        for x in range(2):
            evens = tiles_of(fine_e[x][comp] - keep * coarse_e[x][comp])
            odds = [turn(t, 64) for t in tiles_of(fine_o[x][comp] - keep * coarse_o[x][comp])]
            for at in range(payload.shape[0]):
                payload[at, x, comp] = cut(evens, odds, at)


def cut(evens, odds, at):
    q, part = divmod(at, 4)
    if part == 0:
        return lanes(48, lanes(64, lanes(112, evens[q - 1], odds[q]), odds[q - 1]), evens[q])
    if part == 3:
        after = (q + 1) % len(evens)
        return lanes(16, lanes(64, lanes(80, evens[q], odds[after]), odds[q]), evens[after])
    first = 32 * part - 16
    return lanes(first, lanes(first + 64, odds[q], evens[q]), odds[q])


def lanes(count, here, before):
    return jnp.where(lax.broadcasted_iota(jnp.int32, (8, 128), 1) < count, before, here)


def logical_lane(row):
    return (lax.broadcasted_iota(jnp.int32, (8, 128), 1) + 16 - 32 * (row % 4)) & 127


def window(own, sides, windows):
    load = beside(own, sides)
    row = lax.axis_index("tm")
    windows[6] = logical_lane(row).astype(F32)
    for at in range(own.shape[-1] // 32):

        @pl.when(row == at)
        def _():
            for k in range(6):
                even, odd = (tiles_of(2.0 * load(3, k - 2, parity)) for parity in range(2))
                windows[k] = cut(even, [turn(t, 64) for t in odd], at)


def near_pair(pair, is_even):
    row = lax.broadcasted_iota(jnp.int32, (8, 128), 0)
    lane = lax.broadcasted_iota(jnp.int32, (8, 128), 1)
    source = (lane + jnp.where(is_even, 65, 63)) & 127
    out = []
    for p in pair:
        near = turn(p, 64) + jnp.take_along_axis(p, source, axis=1)
        lower = jnp.where(is_even & (row > 0), pltpu.roll(near, 1, axis=0), 0.0)
        out.append(near + jnp.where(~is_even & (row < 7), pltpu.roll(near, 7, axis=0), lower))
    return out


def pair_heun(spins, aniso, applied, is_even, length, low, high):
    def pick(a, b):
        return [jnp.where(is_even, p, r) for p, r in zip(a, b)]

    def plus(a, b):
        return [p + r for p, r in zip(a, b)]

    def rate(spins, x):
        pair = plus(spins[x], pick(spins[x - 1], spins[x + 1]))
        return bare_rate(spins[x], near_pair(pair, is_even), aniso(x), applied)

    inner = range(low + 1, high)
    first = {x: rate(spins, x) for x in inner}
    pair = pick(plus(spins[high - 1], spins[high]), plus(spins[low], spins[low + 1]))
    edge = pick(spins[low], spins[high])
    edge_aniso = jnp.where(is_even, aniso(low), aniso(high))
    edge_rate = bare_rate(edge, near_pair(pair, is_even), edge_aniso, applied)
    predicted = ahead(spins, first, length)
    predicted[low] = predicted[high] = ahead({0: edge}, {0: edge_rate}, length)[0]
    second = {x: rate(predicted, x) for x in inner}
    return finish(spins, first, second, length, inner)


def emit(ref, at, below, above, logical):
    inside = (logical & 63 >= 16) & (logical & 63 < 48)
    for c in range(3):
        ref[at, c] = jnp.where(inside, below[c], turn(above[c], 32))


def triple(ref, *at):
    return [ref[(*at, c)] for c in range(3)]


def chain(block, blocks, own, left, right, corr, windows, field, *rest):
    applied = [field[c] for c in range(3)]
    is_even = windows[6] < 64.0
    first_slice = 2 * block + 1
    start, last = block == 0, block == blocks - 1

    if last:
        below, above = own
        spins = {-1: triple(left, 0), 0: triple(below, 0), 1: triple(above, 0), 2: triple(right, 0)}
    elif start:
        spins = {base + k: triple(ref, 0, k) for ref, base in ((left, -2), (own, 0), (right, 2)) for k in range(2)}
        extra = {-1: triple(left, 1, 1), 2: triple(right, 1, 0)}
    else:
        spins = {base + k: triple(ref, k) for ref, base in ((left, -2), (own, 0), (right, 2)) for k in range(2)}
        extra = {-1: triple(left, 2), 2: triple(right, 2)}

    def added(spins, extra):
        return {x: [s + e for s, e in zip(spins[x], extra[x])] for x in spins}

    def aniso(x):
        return windows[x + 2]

    reach = (-1, 2) if last else (-2, 3)
    inside = {x: triple(corr, first_slice, x) for x in range(2)}
    ends = pair_heun(spins, aniso, applied, is_even, COARSE, *reach)
    if last:
        earlier, sent = rest
        ends = added(ends, inside)
        emit(sent, sent.shape[0] - 1, ends[0], ends[1], windows[6].astype(jnp.int32))
        return

    up, down, middle = rest
    ends = added(ends, inside | extra)
    for x in range(2):
        for c in range(3):
            middle[x, c] = ends[x][c]
    inside = {x: triple(corr, first_slice + 1, x) for x in range(2)}
    ends = added(pair_heun(ends, aniso, applied, is_even, COARSE, -1, 2), inside)
    for c in range(3):
        if block == blocks - 2:
            up[0, c], down[0, c] = ends[1][c], ends[0][c]
        else:
            for x in range(2):
                up[x, c] = down[x, c] = ends[x][c]
            up[2, c] = corr[first_slice + 2, 1, c]
            down[2, c] = corr[first_slice + 2, 0, c]


def final(block, blocks, below, above, *rest):
    chain(block, blocks, (below, above), *rest)


def pack(corr, windows, below, above, *rest):
    *kept, sent = rest
    logical = windows[6].astype(jnp.int32)
    emit(sent, 0, triple(corr, 0, 0), triple(corr, 0, 1), logical)
    for k, ref in enumerate(kept):
        emit(sent, k + 1, triple(ref, 0), triple(ref, 1), logical)
    emit(sent, len(kept) + 1, triple(below, 0), triple(above, 0), logical)


def assemble(sent, out, layers):
    for comp in range(3):
        for q in range(layers.shape[2]):
            tiles = [sent[4 * q + i, comp] for i in range(4)]
            for k in range(4):
                whole = tiles[0]
                for i in range(1, 4):
                    at = 32 * ((k + i) % 4)
                    whole = lane_select(128, at, at + 32, tiles[i], whole)
                layers[comp, k % 2, q, pl.ds(k // 2, 8, stride=2), :] = turn(whole, -32 * k)
            out[0, comp, :, :, 128 * q : 128 * (q + 1)] = layers[comp, :, q]


def both_sides(to_above, to_below):
    count = lax.axis_size("space")
    up = [(i, (i + 1) % count) for i in range(count)]
    down = [(j, i) for i, j in up]
    return lax.ppermute(to_above, "space", up), lax.ppermute(to_below, "space", down)


def call(kernel, shapes, *args, scratch=(), **more):
    return pl.pallas_call(
        kernel,
        out_shape=[jax.ShapeDtypeStruct(s, F32) for s in shapes],
        out_specs=[VMEM] * len(shapes),
        scratch_shapes=[pltpu.VMEM(s, F32) for s in scratch],
        **({"in_specs": [VMEM] * len(args)} | more),
        compiler_params=pltpu.CompilerParams(vmem_limit_bytes=32 * 1024 * 1024),
    )(*args)


def per_device(starts, anisotropy, applied):
    slices = lax.axis_size("tm")
    width = starts.shape[-1]
    layers = (4, 2, width // 128, 16, 128)
    slab = jnp.concatenate([starts[0], anisotropy[None]], axis=0)
    left, right = both_sides(slab, slab)
    own, field = call(
        prepare,
        [(4, 2, 2, 8, width), (3, 8, 128)],
        *(slab, applied),
        scratch=[layers],
        in_specs=[VMEM, pl.BlockSpec(memory_space=pltpu.SMEM)],
    )
    payload, sides = call(
        prologue,
        [(slices, 2, 3, 8, 128), (2, 4, 2, 2, 8, width)],
        *(own, left, right, field),
        scratch=[(2, *layers)],
    )
    (windows,) = call(window, [(7, 8, 128)], own, sides)
    corr = lax.all_to_all(payload, "tm", 0, 0, tiled=True)
    up = down = corr[:2]
    kept = []
    blocks = slices // 2
    for block in range(blocks - 1):
        kernel = functools.partial(chain, block, blocks)
        ahead_of_last = block == blocks - 2
        shapes = [(1 if ahead_of_last else 3, 3, 8, 128)] * 2 + [(2, 3, 8, 128)]
        up, down, middle = call(kernel, shapes, up, *both_sides(up, down), corr, windows, field)
        kept += [middle] if ahead_of_last else [middle, up]
    left, right = both_sides(up, down)
    (sent,) = call(pack, [(slices, 3, 8, 128)], corr, windows, down, up, *kept)
    kernel = functools.partial(final, blocks - 1, blocks)
    (sent,) = call(
        kernel, [sent.shape], down, up, left, right, corr, windows, field, sent, input_output_aliases={7: 0}
    )
    sent = lax.all_to_all(sent, "tm", 0, 0, tiled=True)
    (out,) = call(assemble, [starts.shape], sent, scratch=[(3, 2, width // 128, 16, 128)])
    return out


def solution(mesh):
    placed = (P("tm", None, "space", None, None), P("space", None, None), P())
    return jax.shard_map(
        per_device,
        mesh=mesh,
        in_specs=placed,
        out_specs=P("tm", None, "space", None, None),
        check_vma=False,
    )
```

```python
import functools

import jax
import jax.numpy as jnp
from jax import lax
from jax.experimental import pallas as pl
from jax.experimental.pallas import tpu as pltpu
from jax.sharding import PartitionSpec as P

DAMPING = 0.1
STEP = 0.02
COARSE = 2 * STEP
GAIN = -1.0 / (1.0 + DAMPING * DAMPING)
F32 = jnp.float32
VMEM = pl.BlockSpec(memory_space=pltpu.VMEM)


def near_odd(even_below, even_here):
    out = []
    for below, here in zip(even_below, even_here):
        pair = below + here
        pair = pair + pltpu.roll(pair, 1, axis=1)
        row = lax.broadcasted_iota(jnp.int32, pair.shape, 0)
        out.append(pair + jnp.where(row < 7, pltpu.roll(pair, 7, axis=0), 0.0))
    return out


def near_even(odd_here, odd_above):
    out = []
    for here, above in zip(odd_here, odd_above):
        pair = here + above
        pair = pair + pltpu.roll(pair, pair.shape[1] - 1, axis=1)
        row = lax.broadcasted_iota(jnp.int32, pair.shape, 0)
        out.append(pair + jnp.where(row > 0, pltpu.roll(pair, 1, axis=0), 0.0))
    return out


def cross(a, b):
    return [a[1] * b[2] - a[2] * b[1], a[2] * b[0] - a[0] * b[2], a[0] * b[1] - a[1] * b[0]]


def bare_rate(spin, near, twice_aniso, applied):
    field = [n + h for n, h in zip(near, applied)]
    field[2] = field[2] + twice_aniso * spin[2]
    turn = cross(spin, field)
    return cross(spin, [f + DAMPING * c for f, c in zip(field, turn)])


def rates(even, odd, aniso_even, aniso_odd, applied, evens, odds):
    rate_even = {x: bare_rate(even[x], near_even(odd[x], odd[x + 1]), aniso_even(x), applied) for x in evens}
    rate_odd = {x: bare_rate(odd[x], near_odd(even[x - 1], even[x]), aniso_odd(x), applied) for x in odds}
    return rate_even, rate_odd


def ahead(spins, rate, length):
    return {x: [s + (length * GAIN) * r for s, r in zip(spins[x], rate[x])] for x in rate}


def finish(spins, first, second, length, planes):
    return {
        x: [s + (0.5 * length * GAIN) * (f + g) for s, f, g in zip(spins[x], first[x], second[x])]
        for x in planes
    }


def heun(even, odd, aniso_even, aniso_odd, applied, length, low, high):
    evens, odds, inner = range(low, high), range(low + 1, high + 1), range(low + 1, high)
    first_e, first_o = rates(even, odd, aniso_even, aniso_odd, applied, evens, odds)
    pred_e, pred_o = ahead(even, first_e, length), ahead(odd, first_o, length)
    second_e, second_o = rates(pred_e, pred_o, aniso_even, aniso_odd, applied, inner, inner)
    return finish(even, first_e, second_e, length, inner), finish(odd, first_o, second_o, length, inner)


def lane_select(tile, low, high, a, b):
    lane = lax.broadcasted_iota(jnp.int32, (8, 128), 1) % tile
    return jnp.where((lane >= low) & (lane < high), a, b)


def tiles_of(wide):
    return [wide[:, 128 * q : 128 * (q + 1)] for q in range(wide.shape[1] // 128)]


def turn(x, by):
    by = by % x.shape[1]
    return pltpu.roll(x, by, axis=1) if by else x


def by_parity(slab, out, layers):
    for comp in range(4):
        for x in range(2):
            for q in range(layers.shape[2]):
                at = slice(128 * q, 128 * (q + 1))
                layers[comp, x, q] = slab[comp, x, :, at]
                for parity in range(2):
                    out[comp, x, parity, :, at] = layers[comp, x, q, pl.ds(parity, 8, stride=2), :]


def prepare(slab, applied, out, field, layers):
    by_parity(slab, out, layers)
    for c in range(3):
        field[c] = jnp.full(field.shape[1:], applied[c], F32)


def beside(own, sides):
    def load(comp, plane, parity):
        ref, at = (sides.at[0], plane + 2) if plane < 0 else (own, plane) if plane < 2 else (sides.at[1], plane - 2)
        return ref[comp, at, parity]

    return load


def prologue(own, right, left, field, payload, sides, layers):
    by_parity(left, sides.at[0], layers.at[0])
    by_parity(right, sides.at[1], layers.at[1])
    load = beside(own, sides)
    applied = [jnp.concatenate([field[c]] * layers.shape[3], axis=1) for c in range(3)]

    planes = range(-2, 4)
    even = {x: [load(c, x, 0) for c in range(3)] for x in planes}
    odd = {x: [load(c, x, 1) for c in range(3)] for x in planes}

    def aniso_even(x):
        return 2.0 * load(3, x, 0)

    def aniso_odd(x):
        return 2.0 * load(3, x, 1)

    sides = (aniso_even, aniso_odd, applied)
    first_e, first_o = rates(even, odd, *sides, range(-2, 3), range(-1, 4))
    pred_e, pred_o = ahead(even, first_e, STEP), ahead(odd, first_o, STEP)
    second_e, second_o = rates(pred_e, pred_o, *sides, range(-1, 3), range(-1, 3))
    fine_e = finish(even, first_e, second_e, STEP, range(-1, 3))
    fine_o = finish(odd, first_o, second_o, STEP, range(-1, 3))
    fine_e, fine_o = heun(fine_e, fine_o, *sides, STEP, -1, 2)
    pred_e, pred_o = ahead(even, first_e, COARSE), ahead(odd, first_o, COARSE)
    second_e, second_o = rates(pred_e, pred_o, *sides, range(2), range(2))
    coarse_e = finish(even, first_e, second_e, COARSE, range(2))
    coarse_o = finish(odd, first_o, second_o, COARSE, range(2))

    keep = jnp.where(lax.axis_index("tm") == 0, 0.0, 1.0).astype(F32)
    for comp in range(3):
        for x in range(2):
            evens = tiles_of(fine_e[x][comp] - keep * coarse_e[x][comp])
            odds = [turn(t, 64) for t in tiles_of(fine_o[x][comp] - keep * coarse_o[x][comp])]
            for at in range(payload.shape[0]):
                payload[at, x, comp] = cut(evens, odds, at)


def cut(evens, odds, at):
    q, part = divmod(at, 4)
    if part == 0:
        return lanes(48, lanes(64, lanes(112, evens[q - 1], odds[q]), odds[q - 1]), evens[q])
    if part == 3:
        after = (q + 1) % len(evens)
        return lanes(16, lanes(64, lanes(80, evens[q], odds[after]), odds[q]), evens[after])
    first = 32 * part - 16
    return lanes(first, lanes(first + 64, odds[q], evens[q]), odds[q])


def lanes(count, here, before):
    return jnp.where(lax.broadcasted_iota(jnp.int32, (8, 128), 1) < count, before, here)


def logical_lane(row):
    return (lax.broadcasted_iota(jnp.int32, (8, 128), 1) + 16 - 32 * (row % 4)) & 127


def window(own, sides, windows):
    load = beside(own, sides)
    row = lax.axis_index("tm")
    windows[6] = logical_lane(row).astype(F32)
    for at in range(own.shape[-1] // 32):

        @pl.when(row == at)
        def _():
            for k in range(6):
                even, odd = (tiles_of(2.0 * load(3, k - 2, parity)) for parity in range(2))
                windows[k] = cut(even, [turn(t, 64) for t in odd], at)


def near_pair(pair, is_even):
    row = lax.broadcasted_iota(jnp.int32, (8, 128), 0)
    lane = lax.broadcasted_iota(jnp.int32, (8, 128), 1)
    source = (lane + jnp.where(is_even, 65, 63)) & 127
    out = []
    for p in pair:
        near = turn(p, 64) + jnp.take_along_axis(p, source, axis=1)
        lower = jnp.where(is_even & (row > 0), pltpu.roll(near, 1, axis=0), 0.0)
        out.append(near + jnp.where(~is_even & (row < 7), pltpu.roll(near, 7, axis=0), lower))
    return out


def pair_heun(spins, aniso, applied, is_even, length, low, high):
    def pick(a, b):
        return [jnp.where(is_even, p, r) for p, r in zip(a, b)]

    def plus(a, b):
        return [p + r for p, r in zip(a, b)]

    def rate(spins, x):
        pair = plus(spins[x], pick(spins[x - 1], spins[x + 1]))
        return bare_rate(spins[x], near_pair(pair, is_even), aniso(x), applied)

    inner = range(low + 1, high)
    first = {x: rate(spins, x) for x in inner}
    pair = pick(plus(spins[high - 1], spins[high]), plus(spins[low], spins[low + 1]))
    edge = pick(spins[low], spins[high])
    edge_aniso = jnp.where(is_even, aniso(low), aniso(high))
    edge_rate = bare_rate(edge, near_pair(pair, is_even), edge_aniso, applied)
    predicted = ahead(spins, first, length)
    predicted[low] = predicted[high] = ahead({0: edge}, {0: edge_rate}, length)[0]
    second = {x: rate(predicted, x) for x in inner}
    return finish(spins, first, second, length, inner)


def emit(ref, at, below, above, logical):
    inside = (logical & 63 >= 16) & (logical & 63 < 48)
    for c in range(3):
        ref[at, c] = jnp.where(inside, below[c], turn(above[c], 32))


def triple(ref, *at):
    return [ref[(*at, c)] for c in range(3)]


def chain(block, blocks, own, right, left, corr, windows, field, *rest):
    applied = [field[c] for c in range(3)]
    is_even = windows[6] < 64.0
    first_slice = 2 * block + 1
    start, last = block == 0, block == blocks - 1

    if last:
        below, above = own
        spins = {-1: triple(left, 0), 0: triple(below, 0), 1: triple(above, 0), 2: triple(right, 0)}
    elif start:
        spins = {base + k: triple(ref, 0, k) for ref, base in ((left, -2), (own, 0), (right, 2)) for k in range(2)}
        extra = {-1: triple(left, 1, 1), 2: triple(right, 1, 0)}
    else:
        spins = {base + k: triple(ref, k) for ref, base in ((left, -2), (own, 0), (right, 2)) for k in range(2)}
        extra = {-1: triple(left, 2), 2: triple(right, 2)}

    def added(spins, extra):
        return {x: [s + e for s, e in zip(spins[x], extra[x])] for x in spins}

    def aniso(x):
        return windows[x + 2]

    reach = (-1, 2) if last else (-2, 3)
    inside = {x: triple(corr, first_slice, x) for x in range(2)}
    ends = pair_heun(spins, aniso, applied, is_even, COARSE, *reach)
    if last:
        earlier, sent = rest
        ends = added(ends, inside)
        emit(sent, sent.shape[0] - 1, ends[0], ends[1], windows[6].astype(jnp.int32))
        return

    up, down, middle = rest
    ends = added(ends, inside | extra)
    for x in range(2):
        for c in range(3):
            middle[x, c] = ends[x][c]
    inside = {x: triple(corr, first_slice + 1, x) for x in range(2)}
    ends = added(pair_heun(ends, aniso, applied, is_even, COARSE, -1, 2), inside)
    for c in range(3):
        if block == blocks - 2:
            up[0, c], down[0, c] = ends[1][c], ends[0][c]
        else:
            for x in range(2):
                up[x, c] = down[x, c] = ends[x][c]
            up[2, c] = corr[first_slice + 2, 1, c]
            down[2, c] = corr[first_slice + 2, 0, c]


def final(block, blocks, below, above, *rest):
    chain(block, blocks, (below, above), *rest)


def pack(corr, windows, below, above, *rest):
    *kept, sent = rest
    logical = windows[6].astype(jnp.int32)
    emit(sent, 0, triple(corr, 0, 0), triple(corr, 0, 1), logical)
    for k, ref in enumerate(kept):
        emit(sent, k + 1, triple(ref, 0), triple(ref, 1), logical)
    emit(sent, len(kept) + 1, triple(below, 0), triple(above, 0), logical)


def assemble(sent, out, layers):
    for comp in range(3):
        for q in range(layers.shape[2]):
            tiles = [sent[4 * q + i, comp] for i in range(4)]
            for k in range(4):
                whole = tiles[0]
                for i in range(1, 4):
                    at = 32 * ((k + i) % 4)
                    whole = lane_select(128, at, at + 32, tiles[i], whole)
                layers[comp, k % 2, q, pl.ds(k // 2, 8, stride=2), :] = turn(whole, -32 * k)
            out[0, comp, :, :, 128 * q : 128 * (q + 1)] = layers[comp, :, q]


def both_sides(to_above, to_below):
    count = lax.axis_size("space")
    up = [(i, (i + 1) % count) for i in range(count)]
    down = [(j, i) for i, j in up]
    from_above = lax.ppermute(to_below, "space", down)
    return from_above, lax.ppermute(to_above, "space", up)


def call(kernel, shapes, *args, scratch=(), **more):
    return pl.pallas_call(
        kernel,
        out_shape=[jax.ShapeDtypeStruct(s, F32) for s in shapes],
        out_specs=[VMEM] * len(shapes),
        scratch_shapes=[pltpu.VMEM(s, F32) for s in scratch],
        **({"in_specs": [VMEM] * len(args)} | more),
        compiler_params=pltpu.CompilerParams(vmem_limit_bytes=32 * 1024 * 1024),
    )(*args)


def per_device(starts, anisotropy, applied):
    slices = lax.axis_size("tm")
    width = starts.shape[-1]
    layers = (4, 2, width // 128, 16, 128)
    slab = jnp.concatenate([starts[0], anisotropy[None]], axis=0)
    right, left = both_sides(slab, slab)
    own, field = call(
        prepare,
        [(4, 2, 2, 8, width), (3, 8, 128)],
        *(slab, applied),
        scratch=[layers],
        in_specs=[VMEM, pl.BlockSpec(memory_space=pltpu.SMEM)],
    )
    payload, sides = call(
        prologue,
        [(slices, 2, 3, 8, 128), (2, 4, 2, 2, 8, width)],
        *(own, right, left, field),
        scratch=[(2, *layers)],
    )
    (windows,) = call(window, [(7, 8, 128)], own, sides)
    corr = lax.all_to_all(payload, "tm", 0, 0, tiled=True)
    up = down = corr[:2]
    kept = []
    blocks = slices // 2
    for block in range(blocks - 1):
        kernel = functools.partial(chain, block, blocks)
        ahead_of_last = block == blocks - 2
        shapes = [(1 if ahead_of_last else 3, 3, 8, 128)] * 2 + [(2, 3, 8, 128)]
        up, down, middle = call(kernel, shapes, up, *both_sides(up, down), corr, windows, field)
        kept += [middle] if ahead_of_last else [middle, up]
    right, left = both_sides(up, down)
    (sent,) = call(pack, [(slices, 3, 8, 128)], corr, windows, down, up, *kept)
    kernel = functools.partial(final, blocks - 1, blocks)
    (sent,) = call(
        kernel, [sent.shape], down, up, right, left, corr, windows, field, sent, input_output_aliases={7: 0}
    )
    sent = lax.all_to_all(sent, "tm", 0, 0, tiled=True)
    (out,) = call(assemble, [starts.shape], sent, scratch=[(3, 2, width // 128, 16, 128)])
    return out


def solution(mesh):
    placed = (P("tm", None, "space", None, None), P("space", None, None), P())
    return jax.shard_map(
        per_device,
        mesh=mesh,
        in_specs=placed,
        out_specs=P("tm", None, "space", None, None),
        check_vma=False,
    )
```

```python
import functools

import jax
import jax.numpy as jnp
from jax import lax
from jax.experimental import pallas as pl
from jax.experimental.pallas import tpu as pltpu
from jax.sharding import PartitionSpec as P

DAMPING = 0.1
STEP = 0.02
COARSE = 2 * STEP
GAIN = -1.0 / (1.0 + DAMPING * DAMPING)
F32 = jnp.float32
VMEM = pl.BlockSpec(memory_space=pltpu.VMEM)


def near_odd(even_below, even_here):
    out = []
    for below, here in zip(even_below, even_here):
        pair = below + here
        pair = pair + pltpu.roll(pair, 1, axis=1)
        row = lax.broadcasted_iota(jnp.int32, pair.shape, 0)
        out.append(pair + jnp.where(row < 7, pltpu.roll(pair, 7, axis=0), 0.0))
    return out


def near_even(odd_here, odd_above):
    out = []
    for here, above in zip(odd_here, odd_above):
        pair = here + above
        pair = pair + pltpu.roll(pair, pair.shape[1] - 1, axis=1)
        row = lax.broadcasted_iota(jnp.int32, pair.shape, 0)
        out.append(pair + jnp.where(row > 0, pltpu.roll(pair, 1, axis=0), 0.0))
    return out


def cross(a, b):
    return [a[1] * b[2] - a[2] * b[1], a[2] * b[0] - a[0] * b[2], a[0] * b[1] - a[1] * b[0]]


def bare_rate(spin, near, twice_aniso, applied):
    field = [n + h for n, h in zip(near, applied)]
    field[2] = field[2] + twice_aniso * spin[2]
    turn = cross(spin, field)
    return cross(spin, [f + DAMPING * c for f, c in zip(field, turn)])


def rates(even, odd, aniso_even, aniso_odd, applied, evens, odds):
    rate_even = {x: bare_rate(even[x], near_even(odd[x], odd[x + 1]), aniso_even(x), applied) for x in evens}
    rate_odd = {x: bare_rate(odd[x], near_odd(even[x - 1], even[x]), aniso_odd(x), applied) for x in odds}
    return rate_even, rate_odd


def ahead(spins, rate, length):
    return {x: [s + (length * GAIN) * r for s, r in zip(spins[x], rate[x])] for x in rate}


def finish(spins, first, second, length, planes):
    return {
        x: [s + (0.5 * length * GAIN) * (f + g) for s, f, g in zip(spins[x], first[x], second[x])]
        for x in planes
    }


def heun(even, odd, aniso_even, aniso_odd, applied, length, low, high):
    evens, odds, inner = range(low, high), range(low + 1, high + 1), range(low + 1, high)
    first_e, first_o = rates(even, odd, aniso_even, aniso_odd, applied, evens, odds)
    pred_e, pred_o = ahead(even, first_e, length), ahead(odd, first_o, length)
    second_e, second_o = rates(pred_e, pred_o, aniso_even, aniso_odd, applied, inner, inner)
    return finish(even, first_e, second_e, length, inner), finish(odd, first_o, second_o, length, inner)


def lane_select(tile, low, high, a, b):
    lane = lax.broadcasted_iota(jnp.int32, (8, 128), 1) % tile
    return jnp.where((lane >= low) & (lane < high), a, b)


def tiles_of(wide):
    return [wide[:, 128 * q : 128 * (q + 1)] for q in range(wide.shape[1] // 128)]


def turn(x, by):
    by = by % x.shape[1]
    return pltpu.roll(x, by, axis=1) if by else x


def by_parity(slab, out, layers):
    for comp in range(4):
        for x in range(2):
            for q in range(layers.shape[2]):
                at = slice(128 * q, 128 * (q + 1))
                layers[comp, x, q] = slab[comp, x, :, at]
                for parity in range(2):
                    out[comp, x, parity, :, at] = layers[comp, x, q, pl.ds(parity, 8, stride=2), :]


def prepare(slab, applied, out, field, layers):
    by_parity(slab, out, layers)
    for c in range(3):
        field[c] = jnp.full(field.shape[1:], applied[c], F32)


def beside(own, sides):
    def load(comp, plane, parity):
        ref, at = (sides.at[0], plane + 2) if plane < 0 else (own, plane) if plane < 2 else (sides.at[1], plane - 2)
        return ref[comp, at, parity]

    return load


def prologue(own, right, left, field, payload, sides, layers):
    by_parity(left, sides.at[0], layers.at[0])
    by_parity(right, sides.at[1], layers.at[1])
    load = beside(own, sides)
    applied = [jnp.concatenate([field[c]] * layers.shape[3], axis=1) for c in range(3)]

    planes = range(-2, 4)
    even = {x: [load(c, x, 0) for c in range(3)] for x in planes}
    odd = {x: [load(c, x, 1) for c in range(3)] for x in planes}

    def aniso_even(x):
        return 2.0 * load(3, x, 0)

    def aniso_odd(x):
        return 2.0 * load(3, x, 1)

    sides = (aniso_even, aniso_odd, applied)
    first_e, first_o = rates(even, odd, *sides, range(-2, 3), range(-1, 4))
    pred_e, pred_o = ahead(even, first_e, STEP), ahead(odd, first_o, STEP)
    second_e, second_o = rates(pred_e, pred_o, *sides, range(-1, 3), range(-1, 3))
    fine_e = finish(even, first_e, second_e, STEP, range(-1, 3))
    fine_o = finish(odd, first_o, second_o, STEP, range(-1, 3))
    fine_e, fine_o = heun(fine_e, fine_o, *sides, STEP, -1, 2)
    pred_e, pred_o = ahead(even, first_e, COARSE), ahead(odd, first_o, COARSE)
    second_e, second_o = rates(pred_e, pred_o, *sides, range(2), range(2))
    coarse_e = finish(even, first_e, second_e, COARSE, range(2))
    coarse_o = finish(odd, first_o, second_o, COARSE, range(2))

    keep = jnp.where(lax.axis_index("tm") == 0, 0.0, 1.0).astype(F32)
    for comp in range(3):
        for x in range(2):
            evens = tiles_of(fine_e[x][comp] - keep * coarse_e[x][comp])
            odds = [turn(t, 64) for t in tiles_of(fine_o[x][comp] - keep * coarse_o[x][comp])]
            for at in range(payload.shape[0]):
                payload[at, x, comp] = cut(evens, odds, at)


def cut(evens, odds, at):
    q, part = divmod(at, 4)
    if part == 0:
        return lanes(48, lanes(64, lanes(112, evens[q - 1], odds[q]), odds[q - 1]), evens[q])
    if part == 3:
        after = (q + 1) % len(evens)
        return lanes(16, lanes(64, lanes(80, evens[q], odds[after]), odds[q]), evens[after])
    first = 32 * part - 16
    return lanes(first, lanes(first + 64, odds[q], evens[q]), odds[q])


def lanes(count, here, before):
    return jnp.where(lax.broadcasted_iota(jnp.int32, (8, 128), 1) < count, before, here)


def logical_lane(row):
    return (lax.broadcasted_iota(jnp.int32, (8, 128), 1) + 16 - 32 * (row % 4)) & 127


def window(own, sides, windows):
    load = beside(own, sides)
    row = lax.axis_index("tm")
    windows[6] = logical_lane(row).astype(F32)
    for at in range(own.shape[-1] // 32):

        @pl.when(row == at)
        def _():
            for k in range(6):
                even, odd = (tiles_of(2.0 * load(3, k - 2, parity)) for parity in range(2))
                windows[k] = cut(even, [turn(t, 64) for t in odd], at)


def near_pair(pair, is_even):
    row = lax.broadcasted_iota(jnp.int32, (8, 128), 0)
    lane = lax.broadcasted_iota(jnp.int32, (8, 128), 1)
    source = (lane + jnp.where(is_even, 65, 63)) & 127
    out = []
    for p in pair:
        near = turn(p, 64) + jnp.take_along_axis(p, source, axis=1)
        lower = jnp.where(is_even & (row > 0), pltpu.roll(near, 1, axis=0), 0.0)
        out.append(near + jnp.where(~is_even & (row < 7), pltpu.roll(near, 7, axis=0), lower))
    return out


def pair_heun(spins, aniso, applied, is_even, length, low, high):
    def pick(a, b):
        return [jnp.where(is_even, p, r) for p, r in zip(a, b)]

    def plus(a, b):
        return [p + r for p, r in zip(a, b)]

    def rate(spins, x):
        pair = plus(spins[x], pick(spins[x - 1], spins[x + 1]))
        return bare_rate(spins[x], near_pair(pair, is_even), aniso(x), applied)

    inner = range(low + 1, high)
    first = {x: rate(spins, x) for x in inner}
    pair = pick(plus(spins[high - 1], spins[high]), plus(spins[low], spins[low + 1]))
    edge = pick(spins[low], spins[high])
    edge_aniso = jnp.where(is_even, aniso(low), aniso(high))
    edge_rate = bare_rate(edge, near_pair(pair, is_even), edge_aniso, applied)
    predicted = ahead(spins, first, length)
    predicted[low] = predicted[high] = ahead({0: edge}, {0: edge_rate}, length)[0]
    second = {x: rate(predicted, x) for x in inner}
    return finish(spins, first, second, length, inner)


def emit(ref, at, below, above, logical):
    inside = (logical & 63 >= 16) & (logical & 63 < 48)
    for c in range(3):
        ref[at, c] = jnp.where(inside, below[c], turn(above[c], 32))


def triple(ref, *at):
    return [ref[(*at, c)] for c in range(3)]


def chain(block, blocks, own, right, left, corr, windows, field, *rest):
    applied = [field[c] for c in range(3)]
    is_even = windows[6] < 64.0
    first_slice = 2 * block + 1
    start, last = block == 0, block == blocks - 1

    if last:
        below, above = own
        spins = {-1: triple(left, 0), 0: triple(below, 0), 1: triple(above, 0), 2: triple(right, 0)}
    elif start:
        spins = {base + k: triple(ref, 0, k) for ref, base in ((left, -2), (own, 0), (right, 2)) for k in range(2)}
        extra = {-1: triple(left, 1, 1), 2: triple(right, 1, 0)}
    else:
        spins = {base + k: triple(ref, k) for ref, base in ((left, -2), (own, 0), (right, 2)) for k in range(2)}
        extra = {-1: triple(left, 2), 2: triple(right, 2)}

    def added(spins, extra):
        return {x: [s + e for s, e in zip(spins[x], extra[x])] for x in spins}

    def aniso(x):
        return windows[x + 2]

    reach = (-1, 2) if last else (-2, 3)
    inside = {x: triple(corr, first_slice, x) for x in range(2)}
    ends = pair_heun(spins, aniso, applied, is_even, COARSE, *reach)
    if last:
        earlier, sent = rest
        ends = added(ends, inside)
        emit(sent, sent.shape[0] - 1, ends[0], ends[1], windows[6].astype(jnp.int32))
        return

    up, down, middle = rest
    ends = added(ends, inside | extra)
    for x in range(2):
        for c in range(3):
            middle[x, c] = ends[x][c]
    inside = {x: triple(corr, first_slice + 1, x) for x in range(2)}
    ends = added(pair_heun(ends, aniso, applied, is_even, COARSE, -1, 2), inside)
    for c in range(3):
        if block == blocks - 2:
            up[0, c], down[0, c] = ends[1][c], ends[0][c]
        else:
            for x in range(2):
                up[x, c] = down[x, c] = ends[x][c]
            up[2, c] = corr[first_slice + 2, 1, c]
            down[2, c] = corr[first_slice + 2, 0, c]


def final(block, blocks, above, below, *rest):
    chain(block, blocks, (below, above), *rest)


def pack(corr, windows, below, above, *rest):
    *kept, sent = rest
    logical = windows[6].astype(jnp.int32)
    emit(sent, 0, triple(corr, 0, 0), triple(corr, 0, 1), logical)
    for k, ref in enumerate(kept):
        emit(sent, k + 1, triple(ref, 0), triple(ref, 1), logical)
    emit(sent, len(kept) + 1, triple(below, 0), triple(above, 0), logical)


def assemble(sent, out, layers):
    for comp in range(3):
        for q in range(layers.shape[2]):
            tiles = [sent[4 * q + i, comp] for i in range(4)]
            for k in range(4):
                whole = tiles[0]
                for i in range(1, 4):
                    at = 32 * ((k + i) % 4)
                    whole = lane_select(128, at, at + 32, tiles[i], whole)
                layers[comp, k % 2, q, pl.ds(k // 2, 8, stride=2), :] = turn(whole, -32 * k)
            out[0, comp, :, :, 128 * q : 128 * (q + 1)] = layers[comp, :, q]


def both_sides(to_above, to_below):
    count = lax.axis_size("space")
    up = [(i, (i + 1) % count) for i in range(count)]
    down = [(j, i) for i, j in up]
    from_above = lax.ppermute(to_below, "space", down)
    return from_above, lax.ppermute(to_above, "space", up)


def call(kernel, shapes, *args, scratch=(), **more):
    return pl.pallas_call(
        kernel,
        out_shape=[jax.ShapeDtypeStruct(s, F32) for s in shapes],
        out_specs=[VMEM] * len(shapes),
        scratch_shapes=[pltpu.VMEM(s, F32) for s in scratch],
        **({"in_specs": [VMEM] * len(args)} | more),
        compiler_params=pltpu.CompilerParams(vmem_limit_bytes=32 * 1024 * 1024),
    )(*args)


def per_device(starts, anisotropy, applied):
    slices = lax.axis_size("tm")
    width = starts.shape[-1]
    layers = (4, 2, width // 128, 16, 128)
    slab = jnp.concatenate([starts[0], anisotropy[None]], axis=0)
    right, left = both_sides(slab, slab)
    own, field = call(
        prepare,
        [(4, 2, 2, 8, width), (3, 8, 128)],
        *(slab, applied),
        scratch=[layers],
        in_specs=[VMEM, pl.BlockSpec(memory_space=pltpu.SMEM)],
    )
    payload, sides = call(
        prologue,
        [(slices, 2, 3, 8, 128), (2, 4, 2, 2, 8, width)],
        *(own, right, left, field),
        scratch=[(2, *layers)],
    )
    (windows,) = call(window, [(7, 8, 128)], own, sides)
    corr = lax.all_to_all(payload, "tm", 0, 0, tiled=True)
    up = down = corr[:2]
    kept = []
    blocks = slices // 2
    for block in range(blocks - 1):
        kernel = functools.partial(chain, block, blocks)
        ahead_of_last = block == blocks - 2
        shapes = [(1 if ahead_of_last else 3, 3, 8, 128)] * 2 + [(2, 3, 8, 128)]
        up, down, middle = call(kernel, shapes, down, *both_sides(up, down), corr, windows, field)
        kept += [middle] if ahead_of_last else [middle, down]
    right, left = both_sides(up, down)
    (sent,) = call(pack, [(slices, 3, 8, 128)], corr, windows, down, up, *kept)
    kernel = functools.partial(final, blocks - 1, blocks)
    (sent,) = call(
        kernel, [sent.shape], up, down, right, left, corr, windows, field, sent, input_output_aliases={7: 0}
    )
    sent = lax.all_to_all(sent, "tm", 0, 0, tiled=True)
    (out,) = call(assemble, [starts.shape], sent, scratch=[(3, 2, width // 128, 16, 128)])
    return out


def solution(mesh):
    placed = (P("tm", None, "space", None, None), P("space", None, None), P())
    return jax.shard_map(
        per_device,
        mesh=mesh,
        in_specs=placed,
        out_specs=P("tm", None, "space", None, None),
        check_vma=False,
    )
```

```python
import functools

import jax
import jax.numpy as jnp
from jax import lax
from jax.experimental import pallas as pl
from jax.experimental.pallas import tpu as pltpu
from jax.sharding import PartitionSpec as P

DAMPING = 0.1
STEP = 0.02
COARSE = 2 * STEP
GAIN = -1.0 / (1.0 + DAMPING * DAMPING)
F32 = jnp.float32
VMEM = pl.BlockSpec(memory_space=pltpu.VMEM)


def near_odd(even_below, even_here):
    out = []
    for below, here in zip(even_below, even_here):
        pair = below + here
        pair = pair + pltpu.roll(pair, 1, axis=1)
        row = lax.broadcasted_iota(jnp.int32, pair.shape, 0)
        out.append(pair + jnp.where(row < 7, pltpu.roll(pair, 7, axis=0), 0.0))
    return out


def near_even(odd_here, odd_above):
    out = []
    for here, above in zip(odd_here, odd_above):
        pair = here + above
        pair = pair + pltpu.roll(pair, pair.shape[1] - 1, axis=1)
        row = lax.broadcasted_iota(jnp.int32, pair.shape, 0)
        out.append(pair + jnp.where(row > 0, pltpu.roll(pair, 1, axis=0), 0.0))
    return out


def cross(a, b):
    return [a[1] * b[2] - a[2] * b[1], a[2] * b[0] - a[0] * b[2], a[0] * b[1] - a[1] * b[0]]


def bare_rate(spin, near, twice_aniso, applied):
    field = [n + h for n, h in zip(near, applied)]
    field[2] = field[2] + twice_aniso * spin[2]
    turn = cross(spin, field)
    return cross(spin, [f + DAMPING * c for f, c in zip(field, turn)])


def rates(even, odd, aniso_even, aniso_odd, applied, evens, odds):
    rate_even = {x: bare_rate(even[x], near_even(odd[x], odd[x + 1]), aniso_even(x), applied) for x in evens}
    rate_odd = {x: bare_rate(odd[x], near_odd(even[x - 1], even[x]), aniso_odd(x), applied) for x in odds}
    return rate_even, rate_odd


def ahead(spins, rate, length):
    return {x: [s + (length * GAIN) * r for s, r in zip(spins[x], rate[x])] for x in rate}


def finish(spins, first, second, length, planes):
    return {
        x: [s + (0.5 * length * GAIN) * (f + g) for s, f, g in zip(spins[x], first[x], second[x])]
        for x in planes
    }


def heun(even, odd, aniso_even, aniso_odd, applied, length, low, high):
    evens, odds, inner = range(low, high), range(low + 1, high + 1), range(low + 1, high)
    first_e, first_o = rates(even, odd, aniso_even, aniso_odd, applied, evens, odds)
    pred_e, pred_o = ahead(even, first_e, length), ahead(odd, first_o, length)
    second_e, second_o = rates(pred_e, pred_o, aniso_even, aniso_odd, applied, inner, inner)
    return finish(even, first_e, second_e, length, inner), finish(odd, first_o, second_o, length, inner)


def lane_select(tile, low, high, a, b):
    lane = lax.broadcasted_iota(jnp.int32, (8, 128), 1) % tile
    return jnp.where((lane >= low) & (lane < high), a, b)


def tiles_of(wide):
    return [wide[:, 128 * q : 128 * (q + 1)] for q in range(wide.shape[1] // 128)]


def turn(x, by):
    by = by % x.shape[1]
    return pltpu.roll(x, by, axis=1) if by else x


def by_parity(spins, aniso, out, layers):
    for comp in range(4):
        for x in range(2):
            for q in range(layers.shape[2]):
                at = slice(128 * q, 128 * (q + 1))
                layers[comp, x, q] = aniso[x, :, at] if comp == 3 else spins[comp, x, :, at]
                for parity in range(2):
                    out[comp, x, parity, :, at] = layers[comp, x, q, pl.ds(parity, 8, stride=2), :]


def prepare(spins, aniso, applied, out, field, layers):
    by_parity(spins, aniso, out, layers)
    for c in range(3):
        field[c] = jnp.full(field.shape[1:], applied[c], F32)


def beside(own, sides):
    def load(comp, plane, parity):
        ref, at = (sides.at[0], plane + 2) if plane < 0 else (own, plane) if plane < 2 else (sides.at[1], plane - 2)
        return ref[comp, at, parity]

    return load


def prologue(own, right, left, right_a, left_a, field, payload, sides, layers):
    by_parity(left, left_a, sides.at[0], layers.at[0])
    by_parity(right, right_a, sides.at[1], layers.at[1])
    load = beside(own, sides)
    applied = [jnp.concatenate([field[c]] * layers.shape[3], axis=1) for c in range(3)]

    planes = range(-2, 4)
    even = {x: [load(c, x, 0) for c in range(3)] for x in planes}
    odd = {x: [load(c, x, 1) for c in range(3)] for x in planes}

    def aniso_even(x):
        return 2.0 * load(3, x, 0)

    def aniso_odd(x):
        return 2.0 * load(3, x, 1)

    sides = (aniso_even, aniso_odd, applied)
    first_e, first_o = rates(even, odd, *sides, range(-2, 3), range(-1, 4))
    pred_e, pred_o = ahead(even, first_e, STEP), ahead(odd, first_o, STEP)
    second_e, second_o = rates(pred_e, pred_o, *sides, range(-1, 3), range(-1, 3))
    fine_e = finish(even, first_e, second_e, STEP, range(-1, 3))
    fine_o = finish(odd, first_o, second_o, STEP, range(-1, 3))
    fine_e, fine_o = heun(fine_e, fine_o, *sides, STEP, -1, 2)
    pred_e, pred_o = ahead(even, first_e, COARSE), ahead(odd, first_o, COARSE)
    second_e, second_o = rates(pred_e, pred_o, *sides, range(2), range(2))
    coarse_e = finish(even, first_e, second_e, COARSE, range(2))
    coarse_o = finish(odd, first_o, second_o, COARSE, range(2))

    keep = jnp.where(lax.axis_index("tm") == 0, 0.0, 1.0).astype(F32)
    for comp in range(3):
        for x in range(2):
            evens = tiles_of(fine_e[x][comp] - keep * coarse_e[x][comp])
            odds = [turn(t, 64) for t in tiles_of(fine_o[x][comp] - keep * coarse_o[x][comp])]
            for at in range(payload.shape[0]):
                payload[at, x, comp] = cut(evens, odds, at)


def cut(evens, odds, at):
    q, part = divmod(at, 4)
    if part == 0:
        return lanes(48, lanes(64, lanes(112, evens[q - 1], odds[q]), odds[q - 1]), evens[q])
    if part == 3:
        after = (q + 1) % len(evens)
        return lanes(16, lanes(64, lanes(80, evens[q], odds[after]), odds[q]), evens[after])
    first = 32 * part - 16
    return lanes(first, lanes(first + 64, odds[q], evens[q]), odds[q])


def lanes(count, here, before):
    return jnp.where(lax.broadcasted_iota(jnp.int32, (8, 128), 1) < count, before, here)


def logical_lane(row):
    return (lax.broadcasted_iota(jnp.int32, (8, 128), 1) + 16 - 32 * (row % 4)) & 127


def window(own, sides, windows):
    load = beside(own, sides)
    row = lax.axis_index("tm")
    windows[6] = logical_lane(row).astype(F32)
    for at in range(own.shape[-1] // 32):

        @pl.when(row == at)
        def _():
            for k in range(6):
                even, odd = (tiles_of(2.0 * load(3, k - 2, parity)) for parity in range(2))
                windows[k] = cut(even, [turn(t, 64) for t in odd], at)


def near_pair(pair, is_even):
    row = lax.broadcasted_iota(jnp.int32, (8, 128), 0)
    lane = lax.broadcasted_iota(jnp.int32, (8, 128), 1)
    source = (lane + jnp.where(is_even, 65, 63)) & 127
    out = []
    for p in pair:
        near = turn(p, 64) + jnp.take_along_axis(p, source, axis=1)
        lower = jnp.where(is_even & (row > 0), pltpu.roll(near, 1, axis=0), 0.0)
        out.append(near + jnp.where(~is_even & (row < 7), pltpu.roll(near, 7, axis=0), lower))
    return out


def pair_heun(spins, aniso, applied, is_even, length, low, high):
    def pick(a, b):
        return [jnp.where(is_even, p, r) for p, r in zip(a, b)]

    def plus(a, b):
        return [p + r for p, r in zip(a, b)]

    def rate(spins, x):
        pair = plus(spins[x], pick(spins[x - 1], spins[x + 1]))
        return bare_rate(spins[x], near_pair(pair, is_even), aniso(x), applied)

    inner = range(low + 1, high)
    first = {x: rate(spins, x) for x in inner}
    pair = pick(plus(spins[high - 1], spins[high]), plus(spins[low], spins[low + 1]))
    edge = pick(spins[low], spins[high])
    edge_aniso = jnp.where(is_even, aniso(low), aniso(high))
    edge_rate = bare_rate(edge, near_pair(pair, is_even), edge_aniso, applied)
    predicted = ahead(spins, first, length)
    predicted[low] = predicted[high] = ahead({0: edge}, {0: edge_rate}, length)[0]
    second = {x: rate(predicted, x) for x in inner}
    return finish(spins, first, second, length, inner)


def emit(ref, at, below, above, logical):
    inside = (logical & 63 >= 16) & (logical & 63 < 48)
    for c in range(3):
        ref[at, c] = jnp.where(inside, below[c], turn(above[c], 32))


def triple(ref, *at):
    return [ref[(*at, c)] for c in range(3)]


def chain(block, blocks, own, right, left, corr, windows, field, *rest):
    applied = [field[c] for c in range(3)]
    is_even = windows[6] < 64.0
    first_slice = 2 * block + 1
    start, last = block == 0, block == blocks - 1

    if last:
        below, above = own
        spins = {-1: triple(left, 0), 0: triple(below, 0), 1: triple(above, 0), 2: triple(right, 0)}
    elif start:
        spins = {base + k: triple(ref, 0, k) for ref, base in ((left, -2), (own, 0), (right, 2)) for k in range(2)}
        extra = {-1: triple(left, 1, 1), 2: triple(right, 1, 0)}
    else:
        spins = {base + k: triple(ref, k) for ref, base in ((left, -2), (own, 0), (right, 2)) for k in range(2)}
        extra = {-1: triple(left, 2), 2: triple(right, 2)}

    def added(spins, extra):
        return {x: [s + e for s, e in zip(spins[x], extra[x])] for x in spins}

    def aniso(x):
        return windows[x + 2]

    reach = (-1, 2) if last else (-2, 3)
    inside = {x: triple(corr, first_slice, x) for x in range(2)}
    ends = pair_heun(spins, aniso, applied, is_even, COARSE, *reach)
    if last:
        earlier, sent = rest
        ends = added(ends, inside)
        emit(sent, sent.shape[0] - 1, ends[0], ends[1], windows[6].astype(jnp.int32))
        return

    up, down, middle = rest
    ends = added(ends, inside | extra)
    for x in range(2):
        for c in range(3):
            middle[x, c] = ends[x][c]
    inside = {x: triple(corr, first_slice + 1, x) for x in range(2)}
    ends = added(pair_heun(ends, aniso, applied, is_even, COARSE, -1, 2), inside)
    for c in range(3):
        if block == blocks - 2:
            up[0, c], down[0, c] = ends[1][c], ends[0][c]
        else:
            for x in range(2):
                up[x, c] = down[x, c] = ends[x][c]
            up[2, c] = corr[first_slice + 2, 1, c]
            down[2, c] = corr[first_slice + 2, 0, c]


def final(block, blocks, above, below, *rest):
    chain(block, blocks, (below, above), *rest)


def pack(corr, windows, below, above, *rest):
    *kept, sent = rest
    logical = windows[6].astype(jnp.int32)
    emit(sent, 0, triple(corr, 0, 0), triple(corr, 0, 1), logical)
    for k, ref in enumerate(kept):
        emit(sent, k + 1, triple(ref, 0), triple(ref, 1), logical)
    emit(sent, len(kept) + 1, triple(below, 0), triple(above, 0), logical)


def assemble(sent, out, layers):
    for comp in range(3):
        for q in range(layers.shape[2]):
            tiles = [sent[4 * q + i, comp] for i in range(4)]
            for k in range(4):
                whole = tiles[0]
                for i in range(1, 4):
                    at = 32 * ((k + i) % 4)
                    whole = lane_select(128, at, at + 32, tiles[i], whole)
                layers[comp, k % 2, q, pl.ds(k // 2, 8, stride=2), :] = turn(whole, -32 * k)
            out[0, comp, :, :, 128 * q : 128 * (q + 1)] = layers[comp, :, q]


def both_sides(to_above, to_below):
    count = lax.axis_size("space")
    up = [(i, (i + 1) % count) for i in range(count)]
    down = [(j, i) for i, j in up]
    from_above = lax.ppermute(to_below, "space", down)
    return from_above, lax.ppermute(to_above, "space", up)


def call(kernel, shapes, *args, scratch=(), **more):
    return pl.pallas_call(
        kernel,
        out_shape=[jax.ShapeDtypeStruct(s, F32) for s in shapes],
        out_specs=[VMEM] * len(shapes),
        scratch_shapes=[pltpu.VMEM(s, F32) for s in scratch],
        **({"in_specs": [VMEM] * len(args)} | more),
        compiler_params=pltpu.CompilerParams(vmem_limit_bytes=32 * 1024 * 1024),
    )(*args)


def per_device(starts, anisotropy, applied):
    slices = lax.axis_size("tm")
    width = starts.shape[-1]
    layers = (4, 2, width // 128, 16, 128)
    right, left = both_sides(starts[0], starts[0])
    right_a, left_a = both_sides(anisotropy, anisotropy)
    own, field = call(
        prepare,
        [(4, 2, 2, 8, width), (3, 8, 128)],
        *(starts[0], anisotropy, applied),
        scratch=[layers],
        in_specs=[VMEM] * 2 + [pl.BlockSpec(memory_space=pltpu.SMEM)],
    )
    payload, sides = call(
        prologue,
        [(slices, 2, 3, 8, 128), (2, 4, 2, 2, 8, width)],
        *(own, right, left, right_a, left_a, field),
        scratch=[(2, *layers)],
    )
    (windows,) = call(window, [(7, 8, 128)], own, sides)
    corr = lax.all_to_all(payload, "tm", 0, 0, tiled=True)
    up = down = corr[:2]
    kept = []
    blocks = slices // 2
    for block in range(blocks - 1):
        kernel = functools.partial(chain, block, blocks)
        ahead_of_last = block == blocks - 2
        shapes = [(1 if ahead_of_last else 3, 3, 8, 128)] * 2 + [(2, 3, 8, 128)]
        up, down, middle = call(kernel, shapes, down, *both_sides(up, down), corr, windows, field)
        kept += [middle] if ahead_of_last else [middle, down]
    right, left = both_sides(up, down)
    (sent,) = call(pack, [(slices, 3, 8, 128)], corr, windows, down, up, *kept)
    kernel = functools.partial(final, blocks - 1, blocks)
    (sent,) = call(
        kernel, [sent.shape], up, down, right, left, corr, windows, field, sent, input_output_aliases={7: 0}
    )
    sent = lax.all_to_all(sent, "tm", 0, 0, tiled=True)
    (out,) = call(assemble, [starts.shape], sent, scratch=[(3, 2, width // 128, 16, 128)])
    return out


def solution(mesh):
    placed = (P("tm", None, "space", None, None), P("space", None, None), P())
    return jax.shard_map(
        per_device,
        mesh=mesh,
        in_specs=placed,
        out_specs=P("tm", None, "space", None, None),
        check_vma=False,
    )
```

```python
import functools

import jax
import jax.numpy as jnp
from jax import lax
from jax.experimental import pallas as pl
from jax.experimental.pallas import tpu as pltpu
from jax.sharding import PartitionSpec as P

DAMPING = 0.1
STEP = 0.02
COARSE = 2 * STEP
GAIN = -1.0 / (1.0 + DAMPING * DAMPING)
F32 = jnp.float32
VMEM = pl.BlockSpec(memory_space=pltpu.VMEM)


def near_odd(even_below, even_here):
    out = []
    for below, here in zip(even_below, even_here):
        pair = below + here
        pair = pair + pltpu.roll(pair, 1, axis=1)
        row = lax.broadcasted_iota(jnp.int32, pair.shape, 0)
        out.append(pair + jnp.where(row < 7, pltpu.roll(pair, 7, axis=0), 0.0))
    return out


def near_even(odd_here, odd_above):
    out = []
    for here, above in zip(odd_here, odd_above):
        pair = here + above
        pair = pair + pltpu.roll(pair, pair.shape[1] - 1, axis=1)
        row = lax.broadcasted_iota(jnp.int32, pair.shape, 0)
        out.append(pair + jnp.where(row > 0, pltpu.roll(pair, 1, axis=0), 0.0))
    return out


def cross(a, b):
    return [a[1] * b[2] - a[2] * b[1], a[2] * b[0] - a[0] * b[2], a[0] * b[1] - a[1] * b[0]]


def bare_rate(spin, near, twice_aniso, applied):
    field = [n + h for n, h in zip(near, applied)]
    field[2] = field[2] + twice_aniso * spin[2]
    turn = cross(spin, field)
    return cross(spin, [f + DAMPING * c for f, c in zip(field, turn)])


def rates(even, odd, aniso_even, aniso_odd, applied, evens, odds):
    rate_even = {x: bare_rate(even[x], near_even(odd[x], odd[x + 1]), aniso_even(x), applied) for x in evens}
    rate_odd = {x: bare_rate(odd[x], near_odd(even[x - 1], even[x]), aniso_odd(x), applied) for x in odds}
    return rate_even, rate_odd


def ahead(spins, rate, length):
    return {x: [s + (length * GAIN) * r for s, r in zip(spins[x], rate[x])] for x in rate}


def finish(spins, first, second, length, planes):
    return {
        x: [s + (0.5 * length * GAIN) * (f + g) for s, f, g in zip(spins[x], first[x], second[x])]
        for x in planes
    }


def heun(even, odd, aniso_even, aniso_odd, applied, length, low, high):
    evens, odds, inner = range(low, high), range(low + 1, high + 1), range(low + 1, high)
    first_e, first_o = rates(even, odd, aniso_even, aniso_odd, applied, evens, odds)
    pred_e, pred_o = ahead(even, first_e, length), ahead(odd, first_o, length)
    second_e, second_o = rates(pred_e, pred_o, aniso_even, aniso_odd, applied, inner, inner)
    return finish(even, first_e, second_e, length, inner), finish(odd, first_o, second_o, length, inner)


def lane_select(tile, low, high, a, b):
    lane = lax.broadcasted_iota(jnp.int32, (8, 128), 1) % tile
    return jnp.where((lane >= low) & (lane < high), a, b)


def tiles_of(wide):
    return [wide[:, 128 * q : 128 * (q + 1)] for q in range(wide.shape[1] // 128)]


def turn(x, by):
    by = by % x.shape[1]
    return pltpu.roll(x, by, axis=1) if by else x


def by_parity(spins, aniso, out, layers):
    for comp in range(4):
        for x in range(2):
            for q in range(layers.shape[2]):
                at = slice(128 * q, 128 * (q + 1))
                layers[comp, x, q] = aniso[x, :, at] if comp == 3 else spins[comp, x, :, at]
                for parity in range(2):
                    out[comp, x, parity, :, at] = layers[comp, x, q, pl.ds(parity, 8, stride=2), :]


def prepare(slab, applied, out, field, layers):
    by_parity(slab, slab.at[3], out, layers)
    for c in range(3):
        field[c] = jnp.full(field.shape[1:], applied[c], F32)


def beside(own, sides):
    def load(comp, plane, parity):
        ref, at = (sides.at[0], plane + 2) if plane < 0 else (own, plane) if plane < 2 else (sides.at[1], plane - 2)
        return ref[comp, at, parity]

    return load


def prologue(own, right, left, right_a, left_a, field, payload, sides, layers):
    by_parity(left, left_a, sides.at[0], layers.at[0])
    by_parity(right, right_a, sides.at[1], layers.at[1])
    load = beside(own, sides)
    applied = [jnp.concatenate([field[c]] * layers.shape[3], axis=1) for c in range(3)]

    planes = range(-2, 4)
    even = {x: [load(c, x, 0) for c in range(3)] for x in planes}
    odd = {x: [load(c, x, 1) for c in range(3)] for x in planes}

    def aniso_even(x):
        return 2.0 * load(3, x, 0)

    def aniso_odd(x):
        return 2.0 * load(3, x, 1)

    sides = (aniso_even, aniso_odd, applied)
    first_e, first_o = rates(even, odd, *sides, range(-2, 3), range(-1, 4))
    pred_e, pred_o = ahead(even, first_e, STEP), ahead(odd, first_o, STEP)
    second_e, second_o = rates(pred_e, pred_o, *sides, range(-1, 3), range(-1, 3))
    fine_e = finish(even, first_e, second_e, STEP, range(-1, 3))
    fine_o = finish(odd, first_o, second_o, STEP, range(-1, 3))
    fine_e, fine_o = heun(fine_e, fine_o, *sides, STEP, -1, 2)
    pred_e, pred_o = ahead(even, first_e, COARSE), ahead(odd, first_o, COARSE)
    second_e, second_o = rates(pred_e, pred_o, *sides, range(2), range(2))
    coarse_e = finish(even, first_e, second_e, COARSE, range(2))
    coarse_o = finish(odd, first_o, second_o, COARSE, range(2))

    keep = jnp.where(lax.axis_index("tm") == 0, 0.0, 1.0).astype(F32)
    for comp in range(3):
        for x in range(2):
            evens = tiles_of(fine_e[x][comp] - keep * coarse_e[x][comp])
            odds = [turn(t, 64) for t in tiles_of(fine_o[x][comp] - keep * coarse_o[x][comp])]
            for at in range(payload.shape[0]):
                payload[at, x, comp] = cut(evens, odds, at)


def cut(evens, odds, at):
    q, part = divmod(at, 4)
    if part == 0:
        return lanes(48, lanes(64, lanes(112, evens[q - 1], odds[q]), odds[q - 1]), evens[q])
    if part == 3:
        after = (q + 1) % len(evens)
        return lanes(16, lanes(64, lanes(80, evens[q], odds[after]), odds[q]), evens[after])
    first = 32 * part - 16
    return lanes(first, lanes(first + 64, odds[q], evens[q]), odds[q])


def lanes(count, here, before):
    return jnp.where(lax.broadcasted_iota(jnp.int32, (8, 128), 1) < count, before, here)


def logical_lane(row):
    return (lax.broadcasted_iota(jnp.int32, (8, 128), 1) + 16 - 32 * (row % 4)) & 127


def window(own, sides, windows):
    load = beside(own, sides)
    row = lax.axis_index("tm")
    windows[6] = logical_lane(row).astype(F32)
    for at in range(own.shape[-1] // 32):

        @pl.when(row == at)
        def _():
            for k in range(6):
                even, odd = (tiles_of(2.0 * load(3, k - 2, parity)) for parity in range(2))
                windows[k] = cut(even, [turn(t, 64) for t in odd], at)


def near_pair(pair, is_even):
    row = lax.broadcasted_iota(jnp.int32, (8, 128), 0)
    lane = lax.broadcasted_iota(jnp.int32, (8, 128), 1)
    source = (lane + jnp.where(is_even, 65, 63)) & 127
    out = []
    for p in pair:
        near = turn(p, 64) + jnp.take_along_axis(p, source, axis=1)
        lower = jnp.where(is_even & (row > 0), pltpu.roll(near, 1, axis=0), 0.0)
        out.append(near + jnp.where(~is_even & (row < 7), pltpu.roll(near, 7, axis=0), lower))
    return out


def pair_heun(spins, aniso, applied, is_even, length, low, high):
    def pick(a, b):
        return [jnp.where(is_even, p, r) for p, r in zip(a, b)]

    def plus(a, b):
        return [p + r for p, r in zip(a, b)]

    def rate(spins, x):
        pair = plus(spins[x], pick(spins[x - 1], spins[x + 1]))
        return bare_rate(spins[x], near_pair(pair, is_even), aniso(x), applied)

    inner = range(low + 1, high)
    first = {x: rate(spins, x) for x in inner}
    pair = pick(plus(spins[high - 1], spins[high]), plus(spins[low], spins[low + 1]))
    edge = pick(spins[low], spins[high])
    edge_aniso = jnp.where(is_even, aniso(low), aniso(high))
    edge_rate = bare_rate(edge, near_pair(pair, is_even), edge_aniso, applied)
    predicted = ahead(spins, first, length)
    predicted[low] = predicted[high] = ahead({0: edge}, {0: edge_rate}, length)[0]
    second = {x: rate(predicted, x) for x in inner}
    return finish(spins, first, second, length, inner)


def emit(ref, at, below, above, logical):
    inside = (logical & 63 >= 16) & (logical & 63 < 48)
    for c in range(3):
        ref[at, c] = jnp.where(inside, below[c], turn(above[c], 32))


def triple(ref, *at):
    return [ref[(*at, c)] for c in range(3)]


def chain(block, blocks, own, right, left, corr, windows, field, *rest):
    applied = [field[c] for c in range(3)]
    is_even = windows[6] < 64.0
    first_slice = 2 * block + 1
    start, last = block == 0, block == blocks - 1

    if last:
        below, above = own
        spins = {-1: triple(left, 0), 0: triple(below, 0), 1: triple(above, 0), 2: triple(right, 0)}
    elif start:
        spins = {base + k: triple(ref, 0, k) for ref, base in ((left, -2), (own, 0), (right, 2)) for k in range(2)}
        extra = {-1: triple(left, 1, 1), 2: triple(right, 1, 0)}
    else:
        spins = {base + k: triple(ref, k) for ref, base in ((left, -2), (own, 0), (right, 2)) for k in range(2)}
        extra = {-1: triple(left, 2), 2: triple(right, 2)}

    def added(spins, extra):
        return {x: [s + e for s, e in zip(spins[x], extra[x])] for x in spins}

    def aniso(x):
        return windows[x + 2]

    reach = (-1, 2) if last else (-2, 3)
    inside = {x: triple(corr, first_slice, x) for x in range(2)}
    ends = pair_heun(spins, aniso, applied, is_even, COARSE, *reach)
    if last:
        earlier, sent = rest
        ends = added(ends, inside)
        emit(sent, sent.shape[0] - 1, ends[0], ends[1], windows[6].astype(jnp.int32))
        return

    up, down, middle = rest
    ends = added(ends, inside | extra)
    for x in range(2):
        for c in range(3):
            middle[x, c] = ends[x][c]
    inside = {x: triple(corr, first_slice + 1, x) for x in range(2)}
    ends = added(pair_heun(ends, aniso, applied, is_even, COARSE, -1, 2), inside)
    for c in range(3):
        if block == blocks - 2:
            up[0, c], down[0, c] = ends[1][c], ends[0][c]
        else:
            for x in range(2):
                up[x, c] = down[x, c] = ends[x][c]
            up[2, c] = corr[first_slice + 2, 1, c]
            down[2, c] = corr[first_slice + 2, 0, c]


def final(block, blocks, above, below, *rest):
    chain(block, blocks, (below, above), *rest)


def pack(corr, windows, below, above, *rest):
    *kept, sent = rest
    logical = windows[6].astype(jnp.int32)
    emit(sent, 0, triple(corr, 0, 0), triple(corr, 0, 1), logical)
    for k, ref in enumerate(kept):
        emit(sent, k + 1, triple(ref, 0), triple(ref, 1), logical)
    emit(sent, len(kept) + 1, triple(below, 0), triple(above, 0), logical)


def assemble(sent, out, layers):
    for comp in range(3):
        for q in range(layers.shape[2]):
            tiles = [sent[4 * q + i, comp] for i in range(4)]
            for k in range(4):
                whole = tiles[0]
                for i in range(1, 4):
                    at = 32 * ((k + i) % 4)
                    whole = lane_select(128, at, at + 32, tiles[i], whole)
                layers[comp, k % 2, q, pl.ds(k // 2, 8, stride=2), :] = turn(whole, -32 * k)
            out[0, comp, :, :, 128 * q : 128 * (q + 1)] = layers[comp, :, q]


def both_sides(to_above, to_below):
    count = lax.axis_size("space")
    up = [(i, (i + 1) % count) for i in range(count)]
    down = [(j, i) for i, j in up]
    from_above = lax.ppermute(to_below, "space", down)
    return from_above, lax.ppermute(to_above, "space", up)


def call(kernel, shapes, *args, scratch=(), **more):
    return pl.pallas_call(
        kernel,
        out_shape=[jax.ShapeDtypeStruct(s, F32) for s in shapes],
        out_specs=[VMEM] * len(shapes),
        scratch_shapes=[pltpu.VMEM(s, F32) for s in scratch],
        **({"in_specs": [VMEM] * len(args)} | more),
        compiler_params=pltpu.CompilerParams(vmem_limit_bytes=32 * 1024 * 1024),
    )(*args)


def per_device(starts, anisotropy, applied):
    slices = lax.axis_size("tm")
    width = starts.shape[-1]
    layers = (4, 2, width // 128, 16, 128)
    slab = jnp.concatenate([starts[0], anisotropy[None]], axis=0)
    right, left = both_sides(starts[0], starts[0])
    right_a, left_a = both_sides(anisotropy, anisotropy)
    own, field = call(
        prepare,
        [(4, 2, 2, 8, width), (3, 8, 128)],
        *(slab, applied),
        scratch=[layers],
        in_specs=[VMEM, pl.BlockSpec(memory_space=pltpu.SMEM)],
    )
    payload, sides = call(
        prologue,
        [(slices, 2, 3, 8, 128), (2, 4, 2, 2, 8, width)],
        *(own, right, left, right_a, left_a, field),
        scratch=[(2, *layers)],
    )
    (windows,) = call(window, [(7, 8, 128)], own, sides)
    corr = lax.all_to_all(payload, "tm", 0, 0, tiled=True)
    up = down = corr[:2]
    kept = []
    blocks = slices // 2
    for block in range(blocks - 1):
        kernel = functools.partial(chain, block, blocks)
        ahead_of_last = block == blocks - 2
        shapes = [(1 if ahead_of_last else 3, 3, 8, 128)] * 2 + [(2, 3, 8, 128)]
        up, down, middle = call(kernel, shapes, down, *both_sides(up, down), corr, windows, field)
        kept += [middle] if ahead_of_last else [middle, down]
    right, left = both_sides(up, down)
    (sent,) = call(pack, [(slices, 3, 8, 128)], corr, windows, down, up, *kept)
    kernel = functools.partial(final, blocks - 1, blocks)
    (sent,) = call(
        kernel, [sent.shape], up, down, right, left, corr, windows, field, sent, input_output_aliases={7: 0}
    )
    sent = lax.all_to_all(sent, "tm", 0, 0, tiled=True)
    (out,) = call(assemble, [starts.shape], sent, scratch=[(3, 2, width // 128, 16, 128)])
    return out


def solution(mesh):
    placed = (P("tm", None, "space", None, None), P("space", None, None), P())
    return jax.shard_map(
        per_device,
        mesh=mesh,
        in_specs=placed,
        out_specs=P("tm", None, "space", None, None),
        check_vma=False,
    )
```

```python
import functools

import jax
import jax.numpy as jnp
from jax import lax
from jax.experimental import pallas as pl
from jax.experimental.pallas import tpu as pltpu
from jax.sharding import PartitionSpec as P

DAMPING = 0.1
STEP = 0.02
COARSE = 2 * STEP
GAIN = -1.0 / (1.0 + DAMPING * DAMPING)
F32 = jnp.float32
VMEM = pl.BlockSpec(memory_space=pltpu.VMEM)


def near_odd(even_below, even_here):
    out = []
    for below, here in zip(even_below, even_here):
        pair = below + here
        pair = pair + pltpu.roll(pair, 1, axis=1)
        row = lax.broadcasted_iota(jnp.int32, pair.shape, 0)
        out.append(pair + jnp.where(row < 7, pltpu.roll(pair, 7, axis=0), 0.0))
    return out


def near_even(odd_here, odd_above):
    out = []
    for here, above in zip(odd_here, odd_above):
        pair = here + above
        pair = pair + pltpu.roll(pair, pair.shape[1] - 1, axis=1)
        row = lax.broadcasted_iota(jnp.int32, pair.shape, 0)
        out.append(pair + jnp.where(row > 0, pltpu.roll(pair, 1, axis=0), 0.0))
    return out


def cross(a, b):
    return [a[1] * b[2] - a[2] * b[1], a[2] * b[0] - a[0] * b[2], a[0] * b[1] - a[1] * b[0]]


def bare_rate(spin, near, twice_aniso, applied):
    field = [n + h for n, h in zip(near, applied)]
    field[2] = field[2] + twice_aniso * spin[2]
    turn = cross(spin, field)
    return cross(spin, [f + DAMPING * c for f, c in zip(field, turn)])


def rates(even, odd, aniso_even, aniso_odd, applied, evens, odds):
    rate_even = {x: bare_rate(even[x], near_even(odd[x], odd[x + 1]), aniso_even(x), applied) for x in evens}
    rate_odd = {x: bare_rate(odd[x], near_odd(even[x - 1], even[x]), aniso_odd(x), applied) for x in odds}
    return rate_even, rate_odd


def ahead(spins, rate, length):
    return {x: [s + (length * GAIN) * r for s, r in zip(spins[x], rate[x])] for x in rate}


def finish(spins, first, second, length, planes):
    return {
        x: [s + (0.5 * length * GAIN) * (f + g) for s, f, g in zip(spins[x], first[x], second[x])]
        for x in planes
    }


def heun(even, odd, aniso_even, aniso_odd, applied, length, low, high):
    evens, odds, inner = range(low, high), range(low + 1, high + 1), range(low + 1, high)
    first_e, first_o = rates(even, odd, aniso_even, aniso_odd, applied, evens, odds)
    pred_e, pred_o = ahead(even, first_e, length), ahead(odd, first_o, length)
    second_e, second_o = rates(pred_e, pred_o, aniso_even, aniso_odd, applied, inner, inner)
    return finish(even, first_e, second_e, length, inner), finish(odd, first_o, second_o, length, inner)


def lane_select(tile, low, high, a, b):
    lane = lax.broadcasted_iota(jnp.int32, (8, 128), 1) % tile
    return jnp.where((lane >= low) & (lane < high), a, b)


def tiles_of(wide):
    return [wide[:, 128 * q : 128 * (q + 1)] for q in range(wide.shape[1] // 128)]


def turn(x, by):
    by = by % x.shape[1]
    return pltpu.roll(x, by, axis=1) if by else x


def by_parity(spins, aniso, out, layers):
    for comp in range(4):
        for x in range(2):
            for q in range(layers.shape[2]):
                at = slice(128 * q, 128 * (q + 1))
                layers[comp, x, q] = aniso[x, :, at] if comp == 3 else spins[comp][x, :, at]
                for parity in range(2):
                    out[comp, x, parity, :, at] = layers[comp, x, q, pl.ds(parity, 8, stride=2), :]


def prepare(slab, applied, out, field, layers):
    by_parity([slab.at[c] for c in range(3)], slab.at[3], out, layers)
    for c in range(3):
        field[c] = jnp.full(field.shape[1:], applied[c], F32)


def beside(own, sides):
    def load(comp, plane, parity):
        ref, at = (sides.at[0], plane + 2) if plane < 0 else (own, plane) if plane < 2 else (sides.at[1], plane - 2)
        return ref[comp, at, parity]

    return load


def prologue(own, right_x, right_y, right_z, right_a, left, left_a, field, payload, sides, layers):
    by_parity([left.at[c] for c in range(3)], left_a, sides.at[0], layers.at[0])
    by_parity((right_x, right_y, right_z), right_a, sides.at[1], layers.at[1])
    load = beside(own, sides)
    applied = [jnp.concatenate([field[c]] * layers.shape[3], axis=1) for c in range(3)]

    planes = range(-2, 4)
    even = {x: [load(c, x, 0) for c in range(3)] for x in planes}
    odd = {x: [load(c, x, 1) for c in range(3)] for x in planes}

    def aniso_even(x):
        return 2.0 * load(3, x, 0)

    def aniso_odd(x):
        return 2.0 * load(3, x, 1)

    sides = (aniso_even, aniso_odd, applied)
    first_e, first_o = rates(even, odd, *sides, range(-2, 3), range(-1, 4))
    pred_e, pred_o = ahead(even, first_e, STEP), ahead(odd, first_o, STEP)
    second_e, second_o = rates(pred_e, pred_o, *sides, range(-1, 3), range(-1, 3))
    fine_e = finish(even, first_e, second_e, STEP, range(-1, 3))
    fine_o = finish(odd, first_o, second_o, STEP, range(-1, 3))
    fine_e, fine_o = heun(fine_e, fine_o, *sides, STEP, -1, 2)
    pred_e, pred_o = ahead(even, first_e, COARSE), ahead(odd, first_o, COARSE)
    second_e, second_o = rates(pred_e, pred_o, *sides, range(2), range(2))
    coarse_e = finish(even, first_e, second_e, COARSE, range(2))
    coarse_o = finish(odd, first_o, second_o, COARSE, range(2))

    keep = jnp.where(lax.axis_index("tm") == 0, 0.0, 1.0).astype(F32)
    for comp in range(3):
        for x in range(2):
            evens = tiles_of(fine_e[x][comp] - keep * coarse_e[x][comp])
            odds = [turn(t, 64) for t in tiles_of(fine_o[x][comp] - keep * coarse_o[x][comp])]
            for at in range(payload.shape[0]):
                payload[at, x, comp] = cut(evens, odds, at)


def cut(evens, odds, at):
    q, part = divmod(at, 4)
    if part == 0:
        return lanes(48, lanes(64, lanes(112, evens[q - 1], odds[q]), odds[q - 1]), evens[q])
    if part == 3:
        after = (q + 1) % len(evens)
        return lanes(16, lanes(64, lanes(80, evens[q], odds[after]), odds[q]), evens[after])
    first = 32 * part - 16
    return lanes(first, lanes(first + 64, odds[q], evens[q]), odds[q])


def lanes(count, here, before):
    return jnp.where(lax.broadcasted_iota(jnp.int32, (8, 128), 1) < count, before, here)


def logical_lane(row):
    return (lax.broadcasted_iota(jnp.int32, (8, 128), 1) + 16 - 32 * (row % 4)) & 127


def window(own, sides, windows):
    load = beside(own, sides)
    row = lax.axis_index("tm")
    windows[6] = logical_lane(row).astype(F32)
    for at in range(own.shape[-1] // 32):

        @pl.when(row == at)
        def _():
            for k in range(6):
                even, odd = (tiles_of(2.0 * load(3, k - 2, parity)) for parity in range(2))
                windows[k] = cut(even, [turn(t, 64) for t in odd], at)


def near_pair(pair, is_even):
    row = lax.broadcasted_iota(jnp.int32, (8, 128), 0)
    lane = lax.broadcasted_iota(jnp.int32, (8, 128), 1)
    source = (lane + jnp.where(is_even, 65, 63)) & 127
    out = []
    for p in pair:
        near = turn(p, 64) + jnp.take_along_axis(p, source, axis=1)
        lower = jnp.where(is_even & (row > 0), pltpu.roll(near, 1, axis=0), 0.0)
        out.append(near + jnp.where(~is_even & (row < 7), pltpu.roll(near, 7, axis=0), lower))
    return out


def pair_heun(spins, aniso, applied, is_even, length, low, high):
    def pick(a, b):
        return [jnp.where(is_even, p, r) for p, r in zip(a, b)]

    def plus(a, b):
        return [p + r for p, r in zip(a, b)]

    def rate(spins, x):
        pair = plus(spins[x], pick(spins[x - 1], spins[x + 1]))
        return bare_rate(spins[x], near_pair(pair, is_even), aniso(x), applied)

    inner = range(low + 1, high)
    first = {x: rate(spins, x) for x in inner}
    pair = pick(plus(spins[high - 1], spins[high]), plus(spins[low], spins[low + 1]))
    edge = pick(spins[low], spins[high])
    edge_aniso = jnp.where(is_even, aniso(low), aniso(high))
    edge_rate = bare_rate(edge, near_pair(pair, is_even), edge_aniso, applied)
    predicted = ahead(spins, first, length)
    predicted[low] = predicted[high] = ahead({0: edge}, {0: edge_rate}, length)[0]
    second = {x: rate(predicted, x) for x in inner}
    return finish(spins, first, second, length, inner)


def emit(ref, at, below, above, logical):
    inside = (logical & 63 >= 16) & (logical & 63 < 48)
    for c in range(3):
        ref[at, c] = jnp.where(inside, below[c], turn(above[c], 32))


def triple(ref, *at):
    return [ref[(*at, c)] for c in range(3)]


def chain(block, blocks, own, right, left, corr, windows, field, *rest):
    applied = [field[c] for c in range(3)]
    is_even = windows[6] < 64.0
    first_slice = 2 * block + 1
    start, last = block == 0, block == blocks - 1

    if last:
        below, above = own
        spins = {-1: triple(left, 0), 0: triple(below, 0), 1: triple(above, 0), 2: triple(right, 0)}
    elif start:
        spins = {base + k: triple(ref, 0, k) for ref, base in ((left, -2), (own, 0), (right, 2)) for k in range(2)}
        extra = {-1: triple(left, 1, 1), 2: triple(right, 1, 0)}
    else:
        spins = {base + k: triple(ref, k) for ref, base in ((left, -2), (own, 0), (right, 2)) for k in range(2)}
        extra = {-1: triple(left, 2), 2: triple(right, 2)}

    def added(spins, extra):
        return {x: [s + e for s, e in zip(spins[x], extra[x])] for x in spins}

    def aniso(x):
        return windows[x + 2]

    reach = (-1, 2) if last else (-2, 3)
    inside = {x: triple(corr, first_slice, x) for x in range(2)}
    ends = pair_heun(spins, aniso, applied, is_even, COARSE, *reach)
    if last:
        earlier, sent = rest
        ends = added(ends, inside)
        emit(sent, sent.shape[0] - 1, ends[0], ends[1], windows[6].astype(jnp.int32))
        return

    up, down, middle = rest
    ends = added(ends, inside | extra)
    for x in range(2):
        for c in range(3):
            middle[x, c] = ends[x][c]
    inside = {x: triple(corr, first_slice + 1, x) for x in range(2)}
    ends = added(pair_heun(ends, aniso, applied, is_even, COARSE, -1, 2), inside)
    for c in range(3):
        if block == blocks - 2:
            up[0, c], down[0, c] = ends[1][c], ends[0][c]
        else:
            for x in range(2):
                up[x, c] = down[x, c] = ends[x][c]
            up[2, c] = corr[first_slice + 2, 1, c]
            down[2, c] = corr[first_slice + 2, 0, c]


def final(block, blocks, above, below, *rest):
    chain(block, blocks, (below, above), *rest)


def pack(corr, windows, below, above, *rest):
    *kept, sent = rest
    logical = windows[6].astype(jnp.int32)
    emit(sent, 0, triple(corr, 0, 0), triple(corr, 0, 1), logical)
    for k, ref in enumerate(kept):
        emit(sent, k + 1, triple(ref, 0), triple(ref, 1), logical)
    emit(sent, len(kept) + 1, triple(below, 0), triple(above, 0), logical)


def assemble(sent, out, layers):
    for comp in range(3):
        for q in range(layers.shape[2]):
            tiles = [sent[4 * q + i, comp] for i in range(4)]
            for k in range(4):
                whole = tiles[0]
                for i in range(1, 4):
                    at = 32 * ((k + i) % 4)
                    whole = lane_select(128, at, at + 32, tiles[i], whole)
                layers[comp, k % 2, q, pl.ds(k // 2, 8, stride=2), :] = turn(whole, -32 * k)
            out[0, comp, :, :, 128 * q : 128 * (q + 1)] = layers[comp, :, q]


def from_below(array):
    count = lax.axis_size("space")
    return lax.ppermute(array, "space", [(i, (i + 1) % count) for i in range(count)])


def from_above(array):
    count = lax.axis_size("space")
    return lax.ppermute(array, "space", [((i + 1) % count, i) for i in range(count)])


def both_sides(to_above, to_below):
    right = from_above(to_below)
    return right, from_below(to_above)


def call(kernel, shapes, *args, scratch=(), **more):
    return pl.pallas_call(
        kernel,
        out_shape=[jax.ShapeDtypeStruct(s, F32) for s in shapes],
        out_specs=[VMEM] * len(shapes),
        scratch_shapes=[pltpu.VMEM(s, F32) for s in scratch],
        **({"in_specs": [VMEM] * len(args)} | more),
        compiler_params=pltpu.CompilerParams(vmem_limit_bytes=32 * 1024 * 1024),
    )(*args)


def per_device(starts, anisotropy, applied):
    slices = lax.axis_size("tm")
    width = starts.shape[-1]
    layers = (4, 2, width // 128, 16, 128)
    (slab,) = lax.optimization_barrier((jnp.concatenate([starts[0], anisotropy[None]], axis=0),))
    parts = [slab[c] for c in range(4)]
    rights = [from_above(part) for part in parts]
    left, left_a = from_below(starts[0]), from_below(anisotropy)
    own, field = call(
        prepare,
        [(4, 2, 2, 8, width), (3, 8, 128)],
        *(slab, applied),
        scratch=[layers],
        in_specs=[VMEM, pl.BlockSpec(memory_space=pltpu.SMEM)],
    )
    payload, sides = call(
        prologue,
        [(slices, 2, 3, 8, 128), (2, 4, 2, 2, 8, width)],
        *(own, *rights, left, left_a, field),
        scratch=[(2, *layers)],
    )
    (windows,) = call(window, [(7, 8, 128)], own, sides)
    corr = lax.all_to_all(payload, "tm", 0, 0, tiled=True)
    up = down = corr[:2]
    kept = []
    blocks = slices // 2
    for block in range(blocks - 1):
        kernel = functools.partial(chain, block, blocks)
        ahead_of_last = block == blocks - 2
        shapes = [(1 if ahead_of_last else 3, 3, 8, 128)] * 2 + [(2, 3, 8, 128)]
        up, down, middle = call(kernel, shapes, down, *both_sides(up, down), corr, windows, field)
        kept += [middle] if ahead_of_last else [middle, down]
    right, left = both_sides(up, down)
    (sent,) = call(pack, [(slices, 3, 8, 128)], corr, windows, down, up, *kept)
    kernel = functools.partial(final, blocks - 1, blocks)
    (sent,) = call(
        kernel, [sent.shape], up, down, right, left, corr, windows, field, sent, input_output_aliases={7: 0}
    )
    sent = lax.all_to_all(sent, "tm", 0, 0, tiled=True)
    (out,) = call(assemble, [starts.shape], sent, scratch=[(3, 2, width // 128, 16, 128)])
    return out


def solution(mesh):
    placed = (P("tm", None, "space", None, None), P("space", None, None), P())
    return jax.shard_map(
        per_device,
        mesh=mesh,
        in_specs=placed,
        out_specs=P("tm", None, "space", None, None),
        check_vma=False,
    )
```

```python
import functools

import jax
import jax.numpy as jnp
from jax import lax
from jax.experimental import pallas as pl
from jax.experimental.pallas import tpu as pltpu
from jax.sharding import PartitionSpec as P

DAMPING = 0.1
STEP = 0.02
COARSE = 2 * STEP
GAIN = -1.0 / (1.0 + DAMPING * DAMPING)
F32 = jnp.float32
VMEM = pl.BlockSpec(memory_space=pltpu.VMEM)


def near_odd(even_below, even_here):
    out = []
    for below, here in zip(even_below, even_here):
        pair = below + here
        pair = pair + pltpu.roll(pair, 1, axis=1)
        row = lax.broadcasted_iota(jnp.int32, pair.shape, 0)
        out.append(pair + jnp.where(row < 7, pltpu.roll(pair, 7, axis=0), 0.0))
    return out


def near_even(odd_here, odd_above):
    out = []
    for here, above in zip(odd_here, odd_above):
        pair = here + above
        pair = pair + pltpu.roll(pair, pair.shape[1] - 1, axis=1)
        row = lax.broadcasted_iota(jnp.int32, pair.shape, 0)
        out.append(pair + jnp.where(row > 0, pltpu.roll(pair, 1, axis=0), 0.0))
    return out


def cross(a, b):
    return [a[1] * b[2] - a[2] * b[1], a[2] * b[0] - a[0] * b[2], a[0] * b[1] - a[1] * b[0]]


def bare_rate(spin, near, twice_aniso, applied):
    field = [n + h for n, h in zip(near, applied)]
    field[2] = field[2] + twice_aniso * spin[2]
    turn = cross(spin, field)
    return cross(spin, [f + DAMPING * c for f, c in zip(field, turn)])


def rates(even, odd, aniso_even, aniso_odd, applied, evens, odds):
    rate_even = {x: bare_rate(even[x], near_even(odd[x], odd[x + 1]), aniso_even(x), applied) for x in evens}
    rate_odd = {x: bare_rate(odd[x], near_odd(even[x - 1], even[x]), aniso_odd(x), applied) for x in odds}
    return rate_even, rate_odd


def ahead(spins, rate, length):
    return {x: [s + (length * GAIN) * r for s, r in zip(spins[x], rate[x])] for x in rate}


def finish(spins, first, second, length, planes):
    return {
        x: [s + (0.5 * length * GAIN) * (f + g) for s, f, g in zip(spins[x], first[x], second[x])]
        for x in planes
    }


def heun(even, odd, aniso_even, aniso_odd, applied, length, low, high):
    evens, odds, inner = range(low, high), range(low + 1, high + 1), range(low + 1, high)
    first_e, first_o = rates(even, odd, aniso_even, aniso_odd, applied, evens, odds)
    pred_e, pred_o = ahead(even, first_e, length), ahead(odd, first_o, length)
    second_e, second_o = rates(pred_e, pred_o, aniso_even, aniso_odd, applied, inner, inner)
    return finish(even, first_e, second_e, length, inner), finish(odd, first_o, second_o, length, inner)


def lane_select(tile, low, high, a, b):
    lane = lax.broadcasted_iota(jnp.int32, (8, 128), 1) % tile
    return jnp.where((lane >= low) & (lane < high), a, b)


def tiles_of(wide):
    return [wide[:, 128 * q : 128 * (q + 1)] for q in range(wide.shape[1] // 128)]


def turn(x, by):
    by = by % x.shape[1]
    return pltpu.roll(x, by, axis=1) if by else x


def by_parity(spins, aniso, out, layers):
    for comp in range(4):
        for x in range(2):
            for q in range(layers.shape[2]):
                at = slice(128 * q, 128 * (q + 1))
                layers[comp, x, q] = aniso[x, :, at] if comp == 3 else spins[comp, x, :, at]
                for parity in range(2):
                    out[comp, x, parity, :, at] = layers[comp, x, q, pl.ds(parity, 8, stride=2), :]


def prepare(slab, applied, out, field, layers):
    by_parity(slab, slab.at[3], out, layers)
    for c in range(3):
        field[c] = jnp.full(field.shape[1:], applied[c], F32)


def beside(own, sides):
    def load(comp, plane, parity):
        ref, at = (sides.at[0], plane + 2) if plane < 0 else (own, plane) if plane < 2 else (sides.at[1], plane - 2)
        return ref[comp, at, parity]

    return load


def prologue(own, right, left_a, right_a, left, field, payload, sides, layers):
    by_parity(left, left_a, sides.at[0], layers.at[0])
    by_parity(right, right_a, sides.at[1], layers.at[1])
    load = beside(own, sides)
    applied = [jnp.concatenate([field[c]] * layers.shape[3], axis=1) for c in range(3)]

    planes = range(-2, 4)
    even = {x: [load(c, x, 0) for c in range(3)] for x in planes}
    odd = {x: [load(c, x, 1) for c in range(3)] for x in planes}

    def aniso_even(x):
        return 2.0 * load(3, x, 0)

    def aniso_odd(x):
        return 2.0 * load(3, x, 1)

    sides = (aniso_even, aniso_odd, applied)
    first_e, first_o = rates(even, odd, *sides, range(-2, 3), range(-1, 4))
    pred_e, pred_o = ahead(even, first_e, STEP), ahead(odd, first_o, STEP)
    second_e, second_o = rates(pred_e, pred_o, *sides, range(-1, 3), range(-1, 3))
    fine_e = finish(even, first_e, second_e, STEP, range(-1, 3))
    fine_o = finish(odd, first_o, second_o, STEP, range(-1, 3))
    fine_e, fine_o = heun(fine_e, fine_o, *sides, STEP, -1, 2)
    pred_e, pred_o = ahead(even, first_e, COARSE), ahead(odd, first_o, COARSE)
    second_e, second_o = rates(pred_e, pred_o, *sides, range(2), range(2))
    coarse_e = finish(even, first_e, second_e, COARSE, range(2))
    coarse_o = finish(odd, first_o, second_o, COARSE, range(2))

    keep = jnp.where(lax.axis_index("tm") == 0, 0.0, 1.0).astype(F32)
    for comp in range(3):
        for x in range(2):
            evens = tiles_of(fine_e[x][comp] - keep * coarse_e[x][comp])
            odds = [turn(t, 64) for t in tiles_of(fine_o[x][comp] - keep * coarse_o[x][comp])]
            for at in range(payload.shape[0]):
                payload[at, x, comp] = cut(evens, odds, at)


def cut(evens, odds, at):
    q, part = divmod(at, 4)
    if part == 0:
        return lanes(48, lanes(64, lanes(112, evens[q - 1], odds[q]), odds[q - 1]), evens[q])
    if part == 3:
        after = (q + 1) % len(evens)
        return lanes(16, lanes(64, lanes(80, evens[q], odds[after]), odds[q]), evens[after])
    first = 32 * part - 16
    return lanes(first, lanes(first + 64, odds[q], evens[q]), odds[q])


def lanes(count, here, before):
    return jnp.where(lax.broadcasted_iota(jnp.int32, (8, 128), 1) < count, before, here)


def logical_lane(row):
    return (lax.broadcasted_iota(jnp.int32, (8, 128), 1) + 16 - 32 * (row % 4)) & 127


def window(own, sides, windows):
    load = beside(own, sides)
    row = lax.axis_index("tm")
    windows[6] = logical_lane(row).astype(F32)
    for at in range(own.shape[-1] // 32):

        @pl.when(row == at)
        def _():
            for k in range(6):
                even, odd = (tiles_of(2.0 * load(3, k - 2, parity)) for parity in range(2))
                windows[k] = cut(even, [turn(t, 64) for t in odd], at)


def near_pair(pair, is_even):
    row = lax.broadcasted_iota(jnp.int32, (8, 128), 0)
    lane = lax.broadcasted_iota(jnp.int32, (8, 128), 1)
    source = (lane + jnp.where(is_even, 65, 63)) & 127
    out = []
    for p in pair:
        near = turn(p, 64) + jnp.take_along_axis(p, source, axis=1)
        lower = jnp.where(is_even & (row > 0), pltpu.roll(near, 1, axis=0), 0.0)
        out.append(near + jnp.where(~is_even & (row < 7), pltpu.roll(near, 7, axis=0), lower))
    return out


def pair_heun(spins, aniso, applied, is_even, length, low, high):
    def pick(a, b):
        return [jnp.where(is_even, p, r) for p, r in zip(a, b)]

    def plus(a, b):
        return [p + r for p, r in zip(a, b)]

    def rate(spins, x):
        pair = plus(spins[x], pick(spins[x - 1], spins[x + 1]))
        return bare_rate(spins[x], near_pair(pair, is_even), aniso(x), applied)

    inner = range(low + 1, high)
    first = {x: rate(spins, x) for x in inner}
    pair = pick(plus(spins[high - 1], spins[high]), plus(spins[low], spins[low + 1]))
    edge = pick(spins[low], spins[high])
    edge_aniso = jnp.where(is_even, aniso(low), aniso(high))
    edge_rate = bare_rate(edge, near_pair(pair, is_even), edge_aniso, applied)
    predicted = ahead(spins, first, length)
    predicted[low] = predicted[high] = ahead({0: edge}, {0: edge_rate}, length)[0]
    second = {x: rate(predicted, x) for x in inner}
    return finish(spins, first, second, length, inner)


def emit(ref, at, below, above, logical):
    inside = (logical & 63 >= 16) & (logical & 63 < 48)
    for c in range(3):
        ref[at, c] = jnp.where(inside, below[c], turn(above[c], 32))


def triple(ref, *at):
    return [ref[(*at, c)] for c in range(3)]


def chain(block, blocks, own, right, left, corr, windows, field, *rest):
    applied = [field[c] for c in range(3)]
    is_even = windows[6] < 64.0
    first_slice = 2 * block + 1
    start, last = block == 0, block == blocks - 1

    if last:
        below, above = own
        spins = {-1: triple(left, 0), 0: triple(below, 0), 1: triple(above, 0), 2: triple(right, 0)}
    elif start:
        spins = {base + k: triple(ref, 0, k) for ref, base in ((left, -2), (own, 0), (right, 2)) for k in range(2)}
        extra = {-1: triple(left, 1, 1), 2: triple(right, 1, 0)}
    else:
        spins = {base + k: triple(ref, k) for ref, base in ((left, -2), (own, 0), (right, 2)) for k in range(2)}
        extra = {-1: triple(left, 2), 2: triple(right, 2)}

    def added(spins, extra):
        return {x: [s + e for s, e in zip(spins[x], extra[x])] for x in spins}

    def aniso(x):
        return windows[x + 2]

    reach = (-1, 2) if last else (-2, 3)
    inside = {x: triple(corr, first_slice, x) for x in range(2)}
    ends = pair_heun(spins, aniso, applied, is_even, COARSE, *reach)
    if last:
        earlier, sent = rest
        ends = added(ends, inside)
        emit(sent, sent.shape[0] - 1, ends[0], ends[1], windows[6].astype(jnp.int32))
        return

    up, down, middle = rest
    ends = added(ends, inside | extra)
    for x in range(2):
        for c in range(3):
            middle[x, c] = ends[x][c]
    inside = {x: triple(corr, first_slice + 1, x) for x in range(2)}
    ends = added(pair_heun(ends, aniso, applied, is_even, COARSE, -1, 2), inside)
    for c in range(3):
        if block == blocks - 2:
            up[0, c], down[0, c] = ends[1][c], ends[0][c]
        else:
            for x in range(2):
                up[x, c] = down[x, c] = ends[x][c]
            up[2, c] = corr[first_slice + 2, 1, c]
            down[2, c] = corr[first_slice + 2, 0, c]


def final(block, blocks, above, below, *rest):
    chain(block, blocks, (below, above), *rest)


def pack(corr, windows, below, above, *rest):
    *kept, sent = rest
    logical = windows[6].astype(jnp.int32)
    emit(sent, 0, triple(corr, 0, 0), triple(corr, 0, 1), logical)
    for k, ref in enumerate(kept):
        emit(sent, k + 1, triple(ref, 0), triple(ref, 1), logical)
    emit(sent, len(kept) + 1, triple(below, 0), triple(above, 0), logical)


def assemble(sent, out, layers):
    for comp in range(3):
        for q in range(layers.shape[2]):
            tiles = [sent[4 * q + i, comp] for i in range(4)]
            for k in range(4):
                whole = tiles[0]
                for i in range(1, 4):
                    at = 32 * ((k + i) % 4)
                    whole = lane_select(128, at, at + 32, tiles[i], whole)
                layers[comp, k % 2, q, pl.ds(k // 2, 8, stride=2), :] = turn(whole, -32 * k)
            out[0, comp, :, :, 128 * q : 128 * (q + 1)] = layers[comp, :, q]


def both_sides(to_above, to_below):
    count = lax.axis_size("space")
    up = [(i, (i + 1) % count) for i in range(count)]
    down = [(j, i) for i, j in up]
    from_above = lax.ppermute(to_below, "space", down)
    return from_above, lax.ppermute(to_above, "space", up)


def call(kernel, shapes, *args, scratch=(), **more):
    return pl.pallas_call(
        kernel,
        out_shape=[jax.ShapeDtypeStruct(s, F32) for s in shapes],
        out_specs=[VMEM] * len(shapes),
        scratch_shapes=[pltpu.VMEM(s, F32) for s in scratch],
        **({"in_specs": [VMEM] * len(args)} | more),
        compiler_params=pltpu.CompilerParams(vmem_limit_bytes=32 * 1024 * 1024),
    )(*args)


def per_device(starts, anisotropy, applied):
    slices = lax.axis_size("tm")
    width = starts.shape[-1]
    layers = (4, 2, width // 128, 16, 128)
    slab = jnp.concatenate([starts[0], anisotropy[None]], axis=0)
    right, left = both_sides(starts[0], starts[0])
    right_a, left_a = both_sides(anisotropy, anisotropy)
    own, field = call(
        prepare,
        [(4, 2, 2, 8, width), (3, 8, 128)],
        *(slab, applied),
        scratch=[layers],
        in_specs=[VMEM, pl.BlockSpec(memory_space=pltpu.SMEM)],
    )
    payload, sides = call(
        prologue,
        [(slices, 2, 3, 8, 128), (2, 4, 2, 2, 8, width)],
        *(own, right, left_a, right_a, left, field),
        scratch=[(2, *layers)],
    )
    (windows,) = call(window, [(7, 8, 128)], own, sides)
    corr = lax.all_to_all(payload, "tm", 0, 0, tiled=True)
    up = down = corr[:2]
    kept = []
    blocks = slices // 2
    for block in range(blocks - 1):
        kernel = functools.partial(chain, block, blocks)
        ahead_of_last = block == blocks - 2
        shapes = [(1 if ahead_of_last else 3, 3, 8, 128)] * 2 + [(2, 3, 8, 128)]
        up, down, middle = call(kernel, shapes, down, *both_sides(up, down), corr, windows, field)
        kept += [middle] if ahead_of_last else [middle, down]
    right, left = both_sides(up, down)
    (sent,) = call(pack, [(slices, 3, 8, 128)], corr, windows, down, up, *kept)
    kernel = functools.partial(final, blocks - 1, blocks)
    (sent,) = call(
        kernel, [sent.shape], up, down, right, left, corr, windows, field, sent, input_output_aliases={7: 0}
    )
    sent = lax.all_to_all(sent, "tm", 0, 0, tiled=True)
    (out,) = call(assemble, [starts.shape], sent, scratch=[(3, 2, width // 128, 16, 128)])
    return out


def solution(mesh):
    placed = (P("tm", None, "space", None, None), P("space", None, None), P())
    return jax.shard_map(
        per_device,
        mesh=mesh,
        in_specs=placed,
        out_specs=P("tm", None, "space", None, None),
        check_vma=False,
    )
```

```python
import functools

import jax
import jax.numpy as jnp
from jax import lax
from jax.experimental import pallas as pl
from jax.experimental.pallas import tpu as pltpu
from jax.sharding import PartitionSpec as P

DAMPING = 0.1
STEP = 0.02
COARSE = 2 * STEP
GAIN = -1.0 / (1.0 + DAMPING * DAMPING)
F32 = jnp.float32
VMEM = pl.BlockSpec(memory_space=pltpu.VMEM)


def near_odd(even_below, even_here):
    out = []
    for below, here in zip(even_below, even_here):
        pair = below + here
        pair = pair + pltpu.roll(pair, 1, axis=1)
        row = lax.broadcasted_iota(jnp.int32, pair.shape, 0)
        out.append(pair + jnp.where(row < 7, pltpu.roll(pair, 7, axis=0), 0.0))
    return out


def near_even(odd_here, odd_above):
    out = []
    for here, above in zip(odd_here, odd_above):
        pair = here + above
        pair = pair + pltpu.roll(pair, pair.shape[1] - 1, axis=1)
        row = lax.broadcasted_iota(jnp.int32, pair.shape, 0)
        out.append(pair + jnp.where(row > 0, pltpu.roll(pair, 1, axis=0), 0.0))
    return out


def cross(a, b):
    return [a[1] * b[2] - a[2] * b[1], a[2] * b[0] - a[0] * b[2], a[0] * b[1] - a[1] * b[0]]


def bare_rate(spin, near, twice_aniso, applied):
    field = [n + h for n, h in zip(near, applied)]
    field[2] = field[2] + twice_aniso * spin[2]
    turn = cross(spin, field)
    return cross(spin, [f + DAMPING * c for f, c in zip(field, turn)])


def rates(even, odd, aniso_even, aniso_odd, applied, evens, odds):
    rate_even = {x: bare_rate(even[x], near_even(odd[x], odd[x + 1]), aniso_even(x), applied) for x in evens}
    rate_odd = {x: bare_rate(odd[x], near_odd(even[x - 1], even[x]), aniso_odd(x), applied) for x in odds}
    return rate_even, rate_odd


def ahead(spins, rate, length):
    return {x: [s + (length * GAIN) * r for s, r in zip(spins[x], rate[x])] for x in rate}


def finish(spins, first, second, length, planes):
    return {
        x: [s + (0.5 * length * GAIN) * (f + g) for s, f, g in zip(spins[x], first[x], second[x])]
        for x in planes
    }


def heun(even, odd, aniso_even, aniso_odd, applied, length, low, high):
    evens, odds, inner = range(low, high), range(low + 1, high + 1), range(low + 1, high)
    first_e, first_o = rates(even, odd, aniso_even, aniso_odd, applied, evens, odds)
    pred_e, pred_o = ahead(even, first_e, length), ahead(odd, first_o, length)
    second_e, second_o = rates(pred_e, pred_o, aniso_even, aniso_odd, applied, inner, inner)
    return finish(even, first_e, second_e, length, inner), finish(odd, first_o, second_o, length, inner)


def lane_select(tile, low, high, a, b):
    lane = lax.broadcasted_iota(jnp.int32, (8, 128), 1) % tile
    return jnp.where((lane >= low) & (lane < high), a, b)


def tiles_of(wide):
    return [wide[:, 128 * q : 128 * (q + 1)] for q in range(wide.shape[1] // 128)]


def turn(x, by):
    by = by % x.shape[1]
    return pltpu.roll(x, by, axis=1) if by else x


def by_parity(spins, aniso, out, layers):
    for comp in range(4):
        for x in range(2):
            for q in range(layers.shape[2]):
                at = slice(128 * q, 128 * (q + 1))
                layers[comp, x, q] = aniso[x, :, at] if comp == 3 else spins[comp, x, :, at]
                for parity in range(2):
                    tile = layers[comp, x, q, pl.ds(parity, 8, stride=2), :]
                    out[comp, x, parity, :, at] = 2.0 * tile if comp == 3 else tile


def prepare(slab, applied, out, field, layers):
    by_parity(slab, slab.at[3], out, layers)
    for c in range(3):
        field[c] = jnp.full(field.shape[1:], applied[c], F32)


def beside(own, sides):
    def load(comp, plane, parity):
        ref, at = (sides.at[0], plane + 2) if plane < 0 else (own, plane) if plane < 2 else (sides.at[1], plane - 2)
        return ref[comp, at, parity]

    return load


def prologue(own, right, left, right_a, left_a, field, payload, sides, layers):
    by_parity(left, left_a, sides.at[0], layers.at[0])
    by_parity(right, right_a, sides.at[1], layers.at[1])
    load = beside(own, sides)
    applied = [jnp.concatenate([field[c]] * layers.shape[3], axis=1) for c in range(3)]

    planes = range(-2, 4)
    even = {x: [load(c, x, 0) for c in range(3)] for x in planes}
    odd = {x: [load(c, x, 1) for c in range(3)] for x in planes}

    def aniso_even(x):
        return load(3, x, 0)

    def aniso_odd(x):
        return load(3, x, 1)

    sides = (aniso_even, aniso_odd, applied)
    first_e, first_o = rates(even, odd, *sides, range(-2, 3), range(-1, 4))
    pred_e, pred_o = ahead(even, first_e, STEP), ahead(odd, first_o, STEP)
    second_e, second_o = rates(pred_e, pred_o, *sides, range(-1, 3), range(-1, 3))
    fine_e = finish(even, first_e, second_e, STEP, range(-1, 3))
    fine_o = finish(odd, first_o, second_o, STEP, range(-1, 3))
    fine_e, fine_o = heun(fine_e, fine_o, *sides, STEP, -1, 2)
    pred_e, pred_o = ahead(even, first_e, COARSE), ahead(odd, first_o, COARSE)
    second_e, second_o = rates(pred_e, pred_o, *sides, range(2), range(2))
    coarse_e = finish(even, first_e, second_e, COARSE, range(2))
    coarse_o = finish(odd, first_o, second_o, COARSE, range(2))

    keep = jnp.where(lax.axis_index("tm") == 0, 0.0, 1.0).astype(F32)
    for comp in range(3):
        for x in range(2):
            evens = tiles_of(fine_e[x][comp] - keep * coarse_e[x][comp])
            odds = [turn(t, 64) for t in tiles_of(fine_o[x][comp] - keep * coarse_o[x][comp])]
            for at in range(payload.shape[0]):
                payload[at, x, comp] = cut(evens, odds, at)


def cut(evens, odds, at):
    q, part = divmod(at, 4)
    if part == 0:
        return lanes(48, lanes(64, lanes(112, evens[q - 1], odds[q]), odds[q - 1]), evens[q])
    if part == 3:
        after = (q + 1) % len(evens)
        return lanes(16, lanes(64, lanes(80, evens[q], odds[after]), odds[q]), evens[after])
    first = 32 * part - 16
    return lanes(first, lanes(first + 64, odds[q], evens[q]), odds[q])


def lanes(count, here, before):
    return jnp.where(lax.broadcasted_iota(jnp.int32, (8, 128), 1) < count, before, here)


def logical_lane(row):
    return (lax.broadcasted_iota(jnp.int32, (8, 128), 1) + 16 - 32 * (row % 4)) & 127


def window(own, sides, windows):
    load = beside(own, sides)
    row = lax.axis_index("tm")
    windows[6] = logical_lane(row).astype(F32)
    for at in range(own.shape[-1] // 32):

        @pl.when(row == at)
        def _():
            for k in range(6):
                even, odd = (tiles_of(load(3, k - 2, parity)) for parity in range(2))
                windows[k] = cut(even, [turn(t, 64) for t in odd], at)


def near_pair(pair, is_even):
    row = lax.broadcasted_iota(jnp.int32, (8, 128), 0)
    lane = lax.broadcasted_iota(jnp.int32, (8, 128), 1)
    source = (lane + jnp.where(is_even, 65, 63)) & 127
    out = []
    for p in pair:
        near = turn(p, 64) + jnp.take_along_axis(p, source, axis=1)
        lower = jnp.where(is_even & (row > 0), pltpu.roll(near, 1, axis=0), 0.0)
        out.append(near + jnp.where(~is_even & (row < 7), pltpu.roll(near, 7, axis=0), lower))
    return out


def pair_heun(spins, aniso, applied, is_even, length, low, high):
    def pick(a, b):
        return [jnp.where(is_even, p, r) for p, r in zip(a, b)]

    def plus(a, b):
        return [p + r for p, r in zip(a, b)]

    def rate(spins, x):
        pair = plus(spins[x], pick(spins[x - 1], spins[x + 1]))
        return bare_rate(spins[x], near_pair(pair, is_even), aniso(x), applied)

    inner = range(low + 1, high)
    first = {x: rate(spins, x) for x in inner}
    pair = pick(plus(spins[high - 1], spins[high]), plus(spins[low], spins[low + 1]))
    edge = pick(spins[low], spins[high])
    edge_aniso = jnp.where(is_even, aniso(low), aniso(high))
    edge_rate = bare_rate(edge, near_pair(pair, is_even), edge_aniso, applied)
    predicted = ahead(spins, first, length)
    predicted[low] = predicted[high] = ahead({0: edge}, {0: edge_rate}, length)[0]
    second = {x: rate(predicted, x) for x in inner}
    return finish(spins, first, second, length, inner)


def emit(ref, at, below, above, logical):
    inside = (logical & 63 >= 16) & (logical & 63 < 48)
    for c in range(3):
        ref[at, c] = jnp.where(inside, below[c], turn(above[c], 32))


def triple(ref, *at):
    return [ref[(*at, c)] for c in range(3)]


def chain(block, blocks, own, right, left, corr, windows, field, *rest):
    applied = [field[c] for c in range(3)]
    is_even = windows[6] < 64.0
    first_slice = 2 * block + 1
    start, last = block == 0, block == blocks - 1

    if last:
        below, above = own
        spins = {-1: triple(left, 0), 0: triple(below, 0), 1: triple(above, 0), 2: triple(right, 0)}
    elif start:
        spins = {base + k: triple(ref, k) for ref, base in ((own, 0), (right, 2)) for k in range(2)}
        spins |= {k - 2: triple(left, 0, k) for k in range(2)}
        extra = {-1: triple(left, 1, 1), 2: triple(right, 2)}
    else:
        spins = {base + k: triple(ref, k) for ref, base in ((left, -2), (own, 0), (right, 2)) for k in range(2)}
        extra = {-1: triple(left, 2), 2: triple(right, 2)}

    def added(spins, extra):
        return {x: [s + e for s, e in zip(spins[x], extra[x])] for x in spins}

    def aniso(x):
        return windows[x + 2]

    reach = (-1, 2) if last else (-2, 3)
    inside = {x: triple(corr, first_slice, x) for x in range(2)}
    ends = pair_heun(spins, aniso, applied, is_even, COARSE, *reach)
    if last:
        earlier, sent = rest
        ends = added(ends, inside)
        emit(sent, sent.shape[0] - 1, ends[0], ends[1], windows[6].astype(jnp.int32))
        return

    up, down, middle = rest
    ends = added(ends, inside | extra)
    for x in range(2):
        for c in range(3):
            middle[x, c] = ends[x][c]
    inside = {x: triple(corr, first_slice + 1, x) for x in range(2)}
    ends = added(pair_heun(ends, aniso, applied, is_even, COARSE, -1, 2), inside)
    for c in range(3):
        if block == blocks - 2:
            up[0, c], down[0, c] = ends[1][c], ends[0][c]
        else:
            for x in range(2):
                up[x, c] = down[x, c] = ends[x][c]
            up[2, c] = corr[first_slice + 2, 1, c]
            down[2, c] = corr[first_slice + 2, 0, c]


def final(block, blocks, above, below, *rest):
    chain(block, blocks, (below, above), *rest)


def pack(corr, windows, below, above, *rest):
    *kept, sent = rest
    logical = windows[6].astype(jnp.int32)
    emit(sent, 0, triple(corr, 0, 0), triple(corr, 0, 1), logical)
    for k, ref in enumerate(kept):
        emit(sent, k + 1, triple(ref, 0), triple(ref, 1), logical)
    emit(sent, len(kept) + 1, triple(below, 0), triple(above, 0), logical)


def assemble(sent, out, layers):
    for comp in range(3):
        for q in range(layers.shape[2]):
            tiles = [sent[4 * q + i, comp] for i in range(4)]
            for k in range(4):
                whole = tiles[0]
                for i in range(1, 4):
                    at = 32 * ((k + i) % 4)
                    whole = lane_select(128, at, at + 32, tiles[i], whole)
                layers[comp, k % 2, q, pl.ds(k // 2, 8, stride=2), :] = turn(whole, -32 * k)
            out[0, comp, :, :, 128 * q : 128 * (q + 1)] = layers[comp, :, q]


def both_sides(to_above, to_below):
    count = lax.axis_size("space")
    up = [(i, (i + 1) % count) for i in range(count)]
    down = [(j, i) for i, j in up]
    from_above = lax.ppermute(to_below, "space", down)
    return from_above, lax.ppermute(to_above, "space", up)


def call(kernel, shapes, *args, scratch=(), **more):
    return pl.pallas_call(
        kernel,
        out_shape=[jax.ShapeDtypeStruct(s, F32) for s in shapes],
        out_specs=[VMEM] * len(shapes),
        scratch_shapes=[pltpu.VMEM(s, F32) for s in scratch],
        **({"in_specs": [VMEM] * len(args)} | more),
        compiler_params=pltpu.CompilerParams(vmem_limit_bytes=32 * 1024 * 1024),
    )(*args)


def per_device(starts, anisotropy, applied):
    slices = lax.axis_size("tm")
    width = starts.shape[-1]
    layers = (4, 2, width // 128, 16, 128)
    slab = jnp.concatenate([starts[0], anisotropy[None]], axis=0)
    right, left = both_sides(starts[0], starts[0])
    right_a, left_a = both_sides(anisotropy, anisotropy)
    own, field = call(
        prepare,
        [(4, 2, 2, 8, width), (3, 8, 128)],
        *(slab, applied),
        scratch=[layers],
        in_specs=[VMEM, pl.BlockSpec(memory_space=pltpu.SMEM)],
    )
    payload, sides = call(
        prologue,
        [(slices, 2, 3, 8, 128), (2, 4, 2, 2, 8, width)],
        *(own, right, left, right_a, left_a, field),
        scratch=[(2, *layers)],
    )
    (windows,) = call(window, [(7, 8, 128)], own, sides)
    corr = lax.all_to_all(payload, "tm", 0, 0, tiled=True)
    up, down = corr[:2], corr.reshape(-1, *corr.shape[2:])[:3]
    kept = []
    blocks = slices // 2
    for block in range(blocks - 1):
        kernel = functools.partial(chain, block, blocks)
        ahead_of_last = block == blocks - 2
        shapes = [(1 if ahead_of_last else 3, 3, 8, 128)] * 2 + [(2, 3, 8, 128)]
        up, down, middle = call(kernel, shapes, down, *both_sides(up, down), corr, windows, field)
        kept += [middle] if ahead_of_last else [middle, down]
    right, left = both_sides(up, down)
    (sent,) = call(pack, [(slices, 3, 8, 128)], corr, windows, down, up, *kept)
    kernel = functools.partial(final, blocks - 1, blocks)
    (sent,) = call(
        kernel, [sent.shape], up, down, right, left, corr, windows, field, sent, input_output_aliases={7: 0}
    )
    sent = lax.all_to_all(sent, "tm", 0, 0, tiled=True)
    (out,) = call(assemble, [starts.shape], sent, scratch=[(3, 2, width // 128, 16, 128)])
    return out


def solution(mesh):
    placed = (P("tm", None, "space", None, None), P("space", None, None), P())
    return jax.shard_map(
        per_device,
        mesh=mesh,
        in_specs=placed,
        out_specs=P("tm", None, "space", None, None),
        check_vma=False,
    )
```

```python
import functools

import jax
import jax.numpy as jnp
from jax import lax
from jax.experimental import pallas as pl
from jax.experimental.pallas import tpu as pltpu
from jax.sharding import PartitionSpec as P

DAMPING = 0.1
STEP = 0.02
COARSE = 2 * STEP
GAIN = -1.0 / (1.0 + DAMPING * DAMPING)
F32 = jnp.float32
VMEM = pl.BlockSpec(memory_space=pltpu.VMEM)


def near_odd(even_below, even_here):
    out = []
    for below, here in zip(even_below, even_here):
        pair = below + here
        pair = pair + pltpu.roll(pair, 1, axis=1)
        row = lax.broadcasted_iota(jnp.int32, pair.shape, 0)
        out.append(pair + jnp.where(row < 7, pltpu.roll(pair, 7, axis=0), 0.0))
    return out


def near_even(odd_here, odd_above):
    out = []
    for here, above in zip(odd_here, odd_above):
        pair = here + above
        pair = pair + pltpu.roll(pair, pair.shape[1] - 1, axis=1)
        row = lax.broadcasted_iota(jnp.int32, pair.shape, 0)
        out.append(pair + jnp.where(row > 0, pltpu.roll(pair, 1, axis=0), 0.0))
    return out


def cross(a, b):
    return [a[1] * b[2] - a[2] * b[1], a[2] * b[0] - a[0] * b[2], a[0] * b[1] - a[1] * b[0]]


def bare_rate(spin, near, twice_aniso, applied):
    field = [n + h for n, h in zip(near, applied)]
    field[2] = field[2] + twice_aniso * spin[2]
    turn = cross(spin, field)
    return cross(spin, [f + DAMPING * c for f, c in zip(field, turn)])


def rates(even, odd, aniso_even, aniso_odd, applied, evens, odds):
    rate_even = {x: bare_rate(even[x], near_even(odd[x], odd[x + 1]), aniso_even(x), applied) for x in evens}
    rate_odd = {x: bare_rate(odd[x], near_odd(even[x - 1], even[x]), aniso_odd(x), applied) for x in odds}
    return rate_even, rate_odd


def ahead(spins, rate, length):
    return {x: [s + (length * GAIN) * r for s, r in zip(spins[x], rate[x])] for x in rate}


def finish(spins, first, second, length, planes):
    return {
        x: [s + (0.5 * length * GAIN) * (f + g) for s, f, g in zip(spins[x], first[x], second[x])]
        for x in planes
    }


def heun(even, odd, aniso_even, aniso_odd, applied, length, low, high):
    evens, odds, inner = range(low, high), range(low + 1, high + 1), range(low + 1, high)
    first_e, first_o = rates(even, odd, aniso_even, aniso_odd, applied, evens, odds)
    pred_e, pred_o = ahead(even, first_e, length), ahead(odd, first_o, length)
    second_e, second_o = rates(pred_e, pred_o, aniso_even, aniso_odd, applied, inner, inner)
    return finish(even, first_e, second_e, length, inner), finish(odd, first_o, second_o, length, inner)


def lane_select(tile, low, high, a, b):
    lane = lax.broadcasted_iota(jnp.int32, (8, 128), 1) % tile
    return jnp.where((lane >= low) & (lane < high), a, b)


def tiles_of(wide):
    return [wide[:, 128 * q : 128 * (q + 1)] for q in range(wide.shape[1] // 128)]


def turn(x, by):
    by = by % x.shape[1]
    return pltpu.roll(x, by, axis=1) if by else x


def by_parity(planes, out, layers, scale=None):
    for x in range(2):
        for q in range(layers.shape[1]):
            at = slice(128 * q, 128 * (q + 1))
            layers[x, q] = planes[x, :, at]
            for parity in range(2):
                tile = layers[x, q, pl.ds(parity, 8, stride=2), :]
                out[x, parity, :, at] = tile if scale is None else scale * tile


def prepare(slab, applied, out, field, layers):
    for comp in range(4):
        by_parity(slab.at[comp], out.at[comp], layers.at[comp], 2.0 if comp == 3 else None)
    for c in range(3):
        field[c] = jnp.full(field.shape[1:], applied[c], F32)


def beside(own, sides, first=0):
    def load(comp, plane, parity):
        if 0 <= plane < 2:
            return own[comp, plane, parity]
        return sides[int(plane > 1), comp - first, plane % 2, parity]

    return load


def first_sums(own, right, left, sides, near, layers):
    for side, spins in enumerate((left, right)):
        for comp in range(3):
            by_parity(spins.at[comp], sides.at[side, comp], layers.at[side, comp])
    load = beside(own, sides)
    even = {x: [load(c, x, 0) for c in range(3)] for x in range(-2, 4)}
    odd = {x: [load(c, x, 1) for c in range(3)] for x in range(-2, 4)}
    for k in range(5):
        for c, value in enumerate(near_even(odd[k - 2], odd[k - 1])):
            near[0, k, c] = value
        for c, value in enumerate(near_odd(even[k - 2], even[k - 1])):
            near[1, k, c] = value


def prologue(own, sides, near, right_a, left_a, field, payload, aniso, layers):
    by_parity(left_a, aniso.at[0, 0], layers.at[0], 2.0)
    by_parity(right_a, aniso.at[1, 0], layers.at[1], 2.0)
    load, load_a = beside(own, sides), beside(own, aniso, 3)
    applied = [jnp.concatenate([field[c]] * layers.shape[2], axis=1) for c in range(3)]

    planes = range(-2, 4)
    even = {x: [load(c, x, 0) for c in range(3)] for x in planes}
    odd = {x: [load(c, x, 1) for c in range(3)] for x in planes}

    def aniso_even(x):
        return load_a(3, x, 0)

    def aniso_odd(x):
        return load_a(3, x, 1)

    sides = (aniso_even, aniso_odd, applied)
    first_e = {x: bare_rate(even[x], [near[0, x + 2, c] for c in range(3)], aniso_even(x), applied) for x in range(-2, 3)}
    first_o = {x: bare_rate(odd[x], [near[1, x + 1, c] for c in range(3)], aniso_odd(x), applied) for x in range(-1, 4)}
    pred_e, pred_o = ahead(even, first_e, STEP), ahead(odd, first_o, STEP)
    second_e, second_o = rates(pred_e, pred_o, *sides, range(-1, 3), range(-1, 3))
    fine_e = finish(even, first_e, second_e, STEP, range(-1, 3))
    fine_o = finish(odd, first_o, second_o, STEP, range(-1, 3))
    fine_e, fine_o = heun(fine_e, fine_o, *sides, STEP, -1, 2)
    pred_e, pred_o = ahead(even, first_e, COARSE), ahead(odd, first_o, COARSE)
    second_e, second_o = rates(pred_e, pred_o, *sides, range(2), range(2))
    coarse_e = finish(even, first_e, second_e, COARSE, range(2))
    coarse_o = finish(odd, first_o, second_o, COARSE, range(2))

    keep = jnp.where(lax.axis_index("tm") == 0, 0.0, 1.0).astype(F32)
    for comp in range(3):
        for x in range(2):
            evens = tiles_of(fine_e[x][comp] - keep * coarse_e[x][comp])
            odds = [turn(t, 64) for t in tiles_of(fine_o[x][comp] - keep * coarse_o[x][comp])]
            for at in range(payload.shape[0]):
                payload[at, x, comp] = cut(evens, odds, at)


def cut(evens, odds, at):
    q, part = divmod(at, 4)
    if part == 0:
        return lanes(48, lanes(64, lanes(112, evens[q - 1], odds[q]), odds[q - 1]), evens[q])
    if part == 3:
        after = (q + 1) % len(evens)
        return lanes(16, lanes(64, lanes(80, evens[q], odds[after]), odds[q]), evens[after])
    first = 32 * part - 16
    return lanes(first, lanes(first + 64, odds[q], evens[q]), odds[q])


def lanes(count, here, before):
    return jnp.where(lax.broadcasted_iota(jnp.int32, (8, 128), 1) < count, before, here)


def logical_lane(row):
    return (lax.broadcasted_iota(jnp.int32, (8, 128), 1) + 16 - 32 * (row % 4)) & 127


def window(own, aniso, windows):
    load = beside(own, aniso, 3)
    row = lax.axis_index("tm")
    windows[6] = logical_lane(row).astype(F32)
    for at in range(own.shape[-1] // 32):

        @pl.when(row == at)
        def _():
            for k in range(6):
                even, odd = (tiles_of(load(3, k - 2, parity)) for parity in range(2))
                windows[k] = cut(even, [turn(t, 64) for t in odd], at)


def near_pair(pair, is_even):
    row = lax.broadcasted_iota(jnp.int32, (8, 128), 0)
    lane = lax.broadcasted_iota(jnp.int32, (8, 128), 1)
    source = (lane + jnp.where(is_even, 65, 63)) & 127
    out = []
    for p in pair:
        near = turn(p, 64) + jnp.take_along_axis(p, source, axis=1)
        lower = jnp.where(is_even & (row > 0), pltpu.roll(near, 1, axis=0), 0.0)
        out.append(near + jnp.where(~is_even & (row < 7), pltpu.roll(near, 7, axis=0), lower))
    return out


def pair_heun(spins, aniso, applied, is_even, length, low, high):
    def pick(a, b):
        return [jnp.where(is_even, p, r) for p, r in zip(a, b)]

    def plus(a, b):
        return [p + r for p, r in zip(a, b)]

    def rate(spins, x):
        pair = plus(spins[x], pick(spins[x - 1], spins[x + 1]))
        return bare_rate(spins[x], near_pair(pair, is_even), aniso(x), applied)

    inner = range(low + 1, high)
    first = {x: rate(spins, x) for x in inner}
    pair = pick(plus(spins[high - 1], spins[high]), plus(spins[low], spins[low + 1]))
    edge = pick(spins[low], spins[high])
    edge_aniso = jnp.where(is_even, aniso(low), aniso(high))
    edge_rate = bare_rate(edge, near_pair(pair, is_even), edge_aniso, applied)
    predicted = ahead(spins, first, length)
    predicted[low] = predicted[high] = ahead({0: edge}, {0: edge_rate}, length)[0]
    second = {x: rate(predicted, x) for x in inner}
    return finish(spins, first, second, length, inner)


def emit(ref, at, below, above, logical):
    inside = (logical & 63 >= 16) & (logical & 63 < 48)
    for c in range(3):
        ref[at, c] = jnp.where(inside, below[c], turn(above[c], 32))


def triple(ref, *at):
    return [ref[(*at, c)] for c in range(3)]


def chain(block, blocks, own, right, left, corr, windows, field, *rest):
    applied = [field[c] for c in range(3)]
    is_even = windows[6] < 64.0
    first_slice = 2 * block + 1
    start, last = block == 0, block == blocks - 1

    if last:
        below, above = own
        spins = {-1: triple(left, 0), 0: triple(below, 0), 1: triple(above, 0), 2: triple(right, 0)}
    elif start:
        spins = {base + k: triple(ref, k) for ref, base in ((own, 0), (right, 2)) for k in range(2)}
        spins |= {k - 2: triple(left, 0, k) for k in range(2)}
        extra = {-1: triple(left, 1, 1), 2: triple(right, 2)}
    else:
        spins = {base + k: triple(ref, k) for ref, base in ((left, -2), (own, 0), (right, 2)) for k in range(2)}
        extra = {-1: triple(left, 2), 2: triple(right, 2)}

    def added(spins, extra):
        return {x: [s + e for s, e in zip(spins[x], extra[x])] for x in spins}

    def aniso(x):
        return windows[x + 2]

    reach = (-1, 2) if last else (-2, 3)
    inside = {x: triple(corr, first_slice, x) for x in range(2)}
    ends = pair_heun(spins, aniso, applied, is_even, COARSE, *reach)
    if last:
        earlier, sent = rest
        ends = added(ends, inside)
        emit(sent, sent.shape[0] - 1, ends[0], ends[1], windows[6].astype(jnp.int32))
        return

    up, down, middle = rest
    ends = added(ends, inside | extra)
    for x in range(2):
        for c in range(3):
            middle[x, c] = ends[x][c]
    inside = {x: triple(corr, first_slice + 1, x) for x in range(2)}
    ends = added(pair_heun(ends, aniso, applied, is_even, COARSE, -1, 2), inside)
    for c in range(3):
        if block == blocks - 2:
            up[0, c], down[0, c] = ends[1][c], ends[0][c]
        else:
            for x in range(2):
                up[x, c] = down[x, c] = ends[x][c]
            up[2, c] = corr[first_slice + 2, 1, c]
            down[2, c] = corr[first_slice + 2, 0, c]


def final(block, blocks, above, below, *rest):
    chain(block, blocks, (below, above), *rest)


def pack(corr, windows, below, above, *rest):
    *kept, sent = rest
    logical = windows[6].astype(jnp.int32)
    emit(sent, 0, triple(corr, 0, 0), triple(corr, 0, 1), logical)
    for k, ref in enumerate(kept):
        emit(sent, k + 1, triple(ref, 0), triple(ref, 1), logical)
    emit(sent, len(kept) + 1, triple(below, 0), triple(above, 0), logical)


def assemble(sent, out, layers):
    for comp in range(3):
        for q in range(layers.shape[2]):
            tiles = [sent[4 * q + i, comp] for i in range(4)]
            for k in range(4):
                whole = tiles[0]
                for i in range(1, 4):
                    at = 32 * ((k + i) % 4)
                    whole = lane_select(128, at, at + 32, tiles[i], whole)
                layers[comp, k % 2, q, pl.ds(k // 2, 8, stride=2), :] = turn(whole, -32 * k)
            out[0, comp, :, :, 128 * q : 128 * (q + 1)] = layers[comp, :, q]


def both_sides(to_above, to_below):
    count = lax.axis_size("space")
    up = [(i, (i + 1) % count) for i in range(count)]
    down = [(j, i) for i, j in up]
    from_above = lax.ppermute(to_below, "space", down)
    return from_above, lax.ppermute(to_above, "space", up)


def call(kernel, shapes, *args, scratch=(), **more):
    return pl.pallas_call(
        kernel,
        out_shape=[jax.ShapeDtypeStruct(s, F32) for s in shapes],
        out_specs=[VMEM] * len(shapes),
        scratch_shapes=[pltpu.VMEM(s, F32) for s in scratch],
        **({"in_specs": [VMEM] * len(args)} | more),
        compiler_params=pltpu.CompilerParams(vmem_limit_bytes=32 * 1024 * 1024),
    )(*args)


def per_device(starts, anisotropy, applied):
    slices = lax.axis_size("tm")
    width = starts.shape[-1]
    layers = (4, 2, width // 128, 16, 128)
    slab = jnp.concatenate([starts[0], anisotropy[None]], axis=0)
    right, left = both_sides(starts[0], starts[0])
    right_a, left_a = both_sides(anisotropy, anisotropy)
    own, field = call(
        prepare,
        [(4, 2, 2, 8, width), (3, 8, 128)],
        *(slab, applied),
        scratch=[layers],
        in_specs=[VMEM, pl.BlockSpec(memory_space=pltpu.SMEM)],
    )
    sides, near = call(
        first_sums,
        [(2, 3, 2, 2, 8, width), (2, 5, 3, 8, width)],
        *(own, right, left),
        scratch=[(2, *layers)],
    )
    payload, aniso = call(
        prologue,
        [(slices, 2, 3, 8, 128), (2, 1, 2, 2, 8, width)],
        *(own, sides, near, right_a, left_a, field),
        scratch=[(2, *layers[1:])],
    )
    (windows,) = call(window, [(7, 8, 128)], own, aniso)
    corr = lax.all_to_all(payload, "tm", 0, 0, tiled=True)
    up, down = corr[:2], corr.reshape(-1, *corr.shape[2:])[:3]
    kept = []
    blocks = slices // 2
    for block in range(blocks - 1):
        kernel = functools.partial(chain, block, blocks)
        ahead_of_last = block == blocks - 2
        shapes = [(1 if ahead_of_last else 3, 3, 8, 128)] * 2 + [(2, 3, 8, 128)]
        up, down, middle = call(kernel, shapes, down, *both_sides(up, down), corr, windows, field)
        kept += [middle] if ahead_of_last else [middle, down]
    right, left = both_sides(up, down)
    (sent,) = call(pack, [(slices, 3, 8, 128)], corr, windows, down, up, *kept)
    kernel = functools.partial(final, blocks - 1, blocks)
    (sent,) = call(
        kernel, [sent.shape], up, down, right, left, corr, windows, field, sent, input_output_aliases={7: 0}
    )
    sent = lax.all_to_all(sent, "tm", 0, 0, tiled=True)
    (out,) = call(assemble, [starts.shape], sent, scratch=[(3, 2, width // 128, 16, 128)])
    return out


def solution(mesh):
    placed = (P("tm", None, "space", None, None), P("space", None, None), P())
    return jax.shard_map(
        per_device,
        mesh=mesh,
        in_specs=placed,
        out_specs=P("tm", None, "space", None, None),
        check_vma=False,
    )
```

```python
import functools

import jax
import jax.numpy as jnp
from jax import lax
from jax.experimental import pallas as pl
from jax.experimental.pallas import tpu as pltpu
from jax.sharding import PartitionSpec as P

DAMPING = 0.1
STEP = 0.02
COARSE = 2 * STEP
GAIN = -1.0 / (1.0 + DAMPING * DAMPING)
F32 = jnp.float32
VMEM = pl.BlockSpec(memory_space=pltpu.VMEM)


def near_odd(even_below, even_here):
    out = []
    for below, here in zip(even_below, even_here):
        pair = below + here
        pair = pair + pltpu.roll(pair, 1, axis=1)
        row = lax.broadcasted_iota(jnp.int32, pair.shape, 0)
        out.append(pair + jnp.where(row < 7, pltpu.roll(pair, 7, axis=0), 0.0))
    return out


def near_even(odd_here, odd_above):
    out = []
    for here, above in zip(odd_here, odd_above):
        pair = here + above
        pair = pair + pltpu.roll(pair, pair.shape[1] - 1, axis=1)
        row = lax.broadcasted_iota(jnp.int32, pair.shape, 0)
        out.append(pair + jnp.where(row > 0, pltpu.roll(pair, 1, axis=0), 0.0))
    return out


def cross(a, b):
    return [a[1] * b[2] - a[2] * b[1], a[2] * b[0] - a[0] * b[2], a[0] * b[1] - a[1] * b[0]]


def bare_rate(spin, near, twice_aniso, applied):
    field = [n + h for n, h in zip(near, applied)]
    field[2] = field[2] + twice_aniso * spin[2]
    turn = cross(spin, field)
    return cross(spin, [f + DAMPING * c for f, c in zip(field, turn)])


def rates(even, odd, aniso_even, aniso_odd, applied, evens, odds):
    rate_even = {x: bare_rate(even[x], near_even(odd[x], odd[x + 1]), aniso_even(x), applied) for x in evens}
    rate_odd = {x: bare_rate(odd[x], near_odd(even[x - 1], even[x]), aniso_odd(x), applied) for x in odds}
    return rate_even, rate_odd


def ahead(spins, rate, length):
    return {x: [s + (length * GAIN) * r for s, r in zip(spins[x], rate[x])] for x in rate}


def finish(spins, first, second, length, planes):
    return {
        x: [s + (0.5 * length * GAIN) * (f + g) for s, f, g in zip(spins[x], first[x], second[x])]
        for x in planes
    }


def heun(even, odd, aniso_even, aniso_odd, applied, length, low, high):
    evens, odds, inner = range(low, high), range(low + 1, high + 1), range(low + 1, high)
    first_e, first_o = rates(even, odd, aniso_even, aniso_odd, applied, evens, odds)
    pred_e, pred_o = ahead(even, first_e, length), ahead(odd, first_o, length)
    second_e, second_o = rates(pred_e, pred_o, aniso_even, aniso_odd, applied, inner, inner)
    return finish(even, first_e, second_e, length, inner), finish(odd, first_o, second_o, length, inner)


def lane_select(tile, low, high, a, b):
    lane = lax.broadcasted_iota(jnp.int32, (8, 128), 1) % tile
    return jnp.where((lane >= low) & (lane < high), a, b)


def tiles_of(wide):
    return [wide[:, 128 * q : 128 * (q + 1)] for q in range(wide.shape[1] // 128)]


def turn(x, by):
    by = by % x.shape[1]
    return pltpu.roll(x, by, axis=1) if by else x


def by_parity(planes, out, layers, scale=None):
    for x in range(2):
        for q in range(layers.shape[1]):
            at = slice(128 * q, 128 * (q + 1))
            layers[x, q] = planes[x, :, at]
            for parity in range(2):
                tile = layers[x, q, pl.ds(parity, 8, stride=2), :]
                out[x, parity, :, at] = tile if scale is None else scale * tile


def prepare(slab, applied, out, field, layers):
    for comp in range(4):
        by_parity(slab.at[comp], out.at[comp], layers.at[comp], 2.0 if comp == 3 else None)
    for c in range(3):
        field[c] = jnp.full(field.shape[1:], applied[c], F32)


def beside(own, sides, first=0):
    def load(comp, plane, parity):
        if 0 <= plane < 2:
            return own[comp, plane, parity]
        return sides[int(plane > 1), comp - first, plane % 2, parity]

    return load


def first_sums(own, right, left, field, sides, near, inner, outer, layers):
    for side, spins in enumerate((left, right)):
        for comp in range(3):
            by_parity(spins.at[comp], sides.at[side, comp], layers.at[side, comp])
    load = beside(own, sides)
    even = {x: [load(c, x, 0) for c in range(3)] for x in range(-2, 4)}
    odd = {x: [load(c, x, 1) for c in range(3)] for x in range(-2, 4)}
    for k in range(5):
        for c, value in enumerate(near_even(odd[k - 2], odd[k - 1])):
            near[0, k, c] = value
        for c, value in enumerate(near_odd(even[k - 2], even[k - 1])):
            near[1, k, c] = value
    applied = [jnp.concatenate([field[c]] * layers.shape[3], axis=1) for c in range(3)]
    sides_own = (lambda x: load(3, x, 0), lambda x: load(3, x, 1), applied)
    first_e, first_o = rates(even, odd, *sides_own, range(2), range(2))
    for x in range(2):
        for c in range(3):
            inner[0, x, c], inner[1, x, c] = first_e[x][c], first_o[x][c]
    for k, length in enumerate((STEP, COARSE)):
        pred_e, pred_o = ahead(even, first_e, length), ahead(odd, first_o, length)
        second_e, second_o = rates(pred_e, pred_o, *sides_own, (0,), (1,))
        for c in range(3):
            outer[k, 0, c], outer[k, 1, c] = second_e[0][c], second_o[1][c]


def prologue(own, sides, near, inner, outer, right_a, left_a, field, payload, aniso, layers):
    by_parity(left_a, aniso.at[0, 0], layers.at[0], 2.0)
    by_parity(right_a, aniso.at[1, 0], layers.at[1], 2.0)
    load, load_a = beside(own, sides), beside(own, aniso, 3)
    applied = [jnp.concatenate([field[c]] * layers.shape[2], axis=1) for c in range(3)]

    planes = range(-2, 4)
    even = {x: [load(c, x, 0) for c in range(3)] for x in planes}
    odd = {x: [load(c, x, 1) for c in range(3)] for x in planes}

    def aniso_even(x):
        return load_a(3, x, 0)

    def aniso_odd(x):
        return load_a(3, x, 1)

    sides = (aniso_even, aniso_odd, applied)
    first_e = {x: [inner[0, x, c] for c in range(3)] for x in range(2)}
    first_o = {x: [inner[1, x, c] for c in range(3)] for x in range(2)}
    for x in (-2, -1, 2):
        first_e[x] = bare_rate(even[x], [near[0, x + 2, c] for c in range(3)], aniso_even(x), applied)
    for x in (-1, 2, 3):
        first_o[x] = bare_rate(odd[x], [near[1, x + 1, c] for c in range(3)], aniso_odd(x), applied)
    pred_e, pred_o = ahead(even, first_e, STEP), ahead(odd, first_o, STEP)
    second_e, second_o = rates(pred_e, pred_o, *sides, (-1, 1, 2), (-1, 0, 2))
    second_e[0], second_o[1] = ([outer[0, k, c] for c in range(3)] for k in range(2))
    fine_e = finish(even, first_e, second_e, STEP, range(-1, 3))
    fine_o = finish(odd, first_o, second_o, STEP, range(-1, 3))
    fine_e, fine_o = heun(fine_e, fine_o, *sides, STEP, -1, 2)
    pred_e, pred_o = ahead(even, first_e, COARSE), ahead(odd, first_o, COARSE)
    second_e, second_o = rates(pred_e, pred_o, *sides, (1,), (0,))
    second_e[0], second_o[1] = ([outer[1, k, c] for c in range(3)] for k in range(2))
    coarse_e = finish(even, first_e, second_e, COARSE, range(2))
    coarse_o = finish(odd, first_o, second_o, COARSE, range(2))

    keep = jnp.where(lax.axis_index("tm") == 0, 0.0, 1.0).astype(F32)
    for comp in range(3):
        for x in range(2):
            evens = tiles_of(fine_e[x][comp] - keep * coarse_e[x][comp])
            odds = [turn(t, 64) for t in tiles_of(fine_o[x][comp] - keep * coarse_o[x][comp])]
            for at in range(payload.shape[0]):
                payload[at, x, comp] = cut(evens, odds, at)


def cut(evens, odds, at):
    q, part = divmod(at, 4)
    if part == 0:
        return lanes(48, lanes(64, lanes(112, evens[q - 1], odds[q]), odds[q - 1]), evens[q])
    if part == 3:
        after = (q + 1) % len(evens)
        return lanes(16, lanes(64, lanes(80, evens[q], odds[after]), odds[q]), evens[after])
    first = 32 * part - 16
    return lanes(first, lanes(first + 64, odds[q], evens[q]), odds[q])


def lanes(count, here, before):
    return jnp.where(lax.broadcasted_iota(jnp.int32, (8, 128), 1) < count, before, here)


def logical_lane(row):
    return (lax.broadcasted_iota(jnp.int32, (8, 128), 1) + 16 - 32 * (row % 4)) & 127


def window(own, aniso, windows):
    load = beside(own, aniso, 3)
    row = lax.axis_index("tm")
    windows[6] = logical_lane(row).astype(F32)
    for at in range(own.shape[-1] // 32):

        @pl.when(row == at)
        def _():
            for k in range(6):
                even, odd = (tiles_of(load(3, k - 2, parity)) for parity in range(2))
                windows[k] = cut(even, [turn(t, 64) for t in odd], at)


def near_pair(pair, is_even):
    row = lax.broadcasted_iota(jnp.int32, (8, 128), 0)
    lane = lax.broadcasted_iota(jnp.int32, (8, 128), 1)
    source = (lane + jnp.where(is_even, 65, 63)) & 127
    out = []
    for p in pair:
        near = turn(p, 64) + jnp.take_along_axis(p, source, axis=1)
        lower = jnp.where(is_even & (row > 0), pltpu.roll(near, 1, axis=0), 0.0)
        out.append(near + jnp.where(~is_even & (row < 7), pltpu.roll(near, 7, axis=0), lower))
    return out


def pair_heun(spins, aniso, applied, is_even, length, low, high):
    def pick(a, b):
        return [jnp.where(is_even, p, r) for p, r in zip(a, b)]

    def plus(a, b):
        return [p + r for p, r in zip(a, b)]

    def rate(spins, x):
        pair = plus(spins[x], pick(spins[x - 1], spins[x + 1]))
        return bare_rate(spins[x], near_pair(pair, is_even), aniso(x), applied)

    inner = range(low + 1, high)
    first = {x: rate(spins, x) for x in inner}
    pair = pick(plus(spins[high - 1], spins[high]), plus(spins[low], spins[low + 1]))
    edge = pick(spins[low], spins[high])
    edge_aniso = jnp.where(is_even, aniso(low), aniso(high))
    edge_rate = bare_rate(edge, near_pair(pair, is_even), edge_aniso, applied)
    predicted = ahead(spins, first, length)
    predicted[low] = predicted[high] = ahead({0: edge}, {0: edge_rate}, length)[0]
    second = {x: rate(predicted, x) for x in inner}
    return finish(spins, first, second, length, inner)


def emit(ref, at, below, above, logical):
    inside = (logical & 63 >= 16) & (logical & 63 < 48)
    for c in range(3):
        ref[at, c] = jnp.where(inside, below[c], turn(above[c], 32))


def triple(ref, *at):
    return [ref[(*at, c)] for c in range(3)]


def chain(block, blocks, own, right, left, corr, windows, field, *rest):
    applied = [field[c] for c in range(3)]
    is_even = windows[6] < 64.0
    first_slice = 2 * block + 1
    start, last = block == 0, block == blocks - 1

    if last:
        below, above = own
        spins = {-1: triple(left, 0), 0: triple(below, 0), 1: triple(above, 0), 2: triple(right, 0)}
    elif start:
        spins = {base + k: triple(ref, k) for ref, base in ((own, 0), (right, 2)) for k in range(2)}
        spins |= {k - 2: triple(left, 0, k) for k in range(2)}
        extra = {-1: triple(left, 1, 1), 2: triple(right, 2)}
    else:
        spins = {base + k: triple(ref, k) for ref, base in ((left, -2), (own, 0), (right, 2)) for k in range(2)}
        extra = {-1: triple(left, 2), 2: triple(right, 2)}

    def added(spins, extra):
        return {x: [s + e for s, e in zip(spins[x], extra[x])] for x in spins}

    def aniso(x):
        return windows[x + 2]

    reach = (-1, 2) if last else (-2, 3)
    inside = {x: triple(corr, first_slice, x) for x in range(2)}
    ends = pair_heun(spins, aniso, applied, is_even, COARSE, *reach)
    if last:
        earlier, sent = rest
        ends = added(ends, inside)
        emit(sent, sent.shape[0] - 1, ends[0], ends[1], windows[6].astype(jnp.int32))
        return

    up, down, middle = rest
    ends = added(ends, inside | extra)
    for x in range(2):
        for c in range(3):
            middle[x, c] = ends[x][c]
    inside = {x: triple(corr, first_slice + 1, x) for x in range(2)}
    ends = added(pair_heun(ends, aniso, applied, is_even, COARSE, -1, 2), inside)
    for c in range(3):
        if block == blocks - 2:
            up[0, c], down[0, c] = ends[1][c], ends[0][c]
        else:
            for x in range(2):
                up[x, c] = down[x, c] = ends[x][c]
            up[2, c] = corr[first_slice + 2, 1, c]
            down[2, c] = corr[first_slice + 2, 0, c]


def final(block, blocks, above, below, *rest):
    chain(block, blocks, (below, above), *rest)


def pack(corr, windows, below, above, *rest):
    *kept, sent = rest
    logical = windows[6].astype(jnp.int32)
    emit(sent, 0, triple(corr, 0, 0), triple(corr, 0, 1), logical)
    for k, ref in enumerate(kept):
        emit(sent, k + 1, triple(ref, 0), triple(ref, 1), logical)
    emit(sent, len(kept) + 1, triple(below, 0), triple(above, 0), logical)


def assemble(sent, out, layers):
    for comp in range(3):
        for q in range(layers.shape[2]):
            tiles = [sent[4 * q + i, comp] for i in range(4)]
            for k in range(4):
                whole = tiles[0]
                for i in range(1, 4):
                    at = 32 * ((k + i) % 4)
                    whole = lane_select(128, at, at + 32, tiles[i], whole)
                layers[comp, k % 2, q, pl.ds(k // 2, 8, stride=2), :] = turn(whole, -32 * k)
            out[0, comp, :, :, 128 * q : 128 * (q + 1)] = layers[comp, :, q]


def both_sides(to_above, to_below):
    count = lax.axis_size("space")
    up = [(i, (i + 1) % count) for i in range(count)]
    down = [(j, i) for i, j in up]
    from_above = lax.ppermute(to_below, "space", down)
    return from_above, lax.ppermute(to_above, "space", up)


def call(kernel, shapes, *args, scratch=(), **more):
    return pl.pallas_call(
        kernel,
        out_shape=[jax.ShapeDtypeStruct(s, F32) for s in shapes],
        out_specs=[VMEM] * len(shapes),
        scratch_shapes=[pltpu.VMEM(s, F32) for s in scratch],
        **({"in_specs": [VMEM] * len(args)} | more),
        compiler_params=pltpu.CompilerParams(vmem_limit_bytes=32 * 1024 * 1024),
    )(*args)


def per_device(starts, anisotropy, applied):
    slices = lax.axis_size("tm")
    width = starts.shape[-1]
    layers = (4, 2, width // 128, 16, 128)
    slab = jnp.concatenate([starts[0], anisotropy[None]], axis=0)
    right, left = both_sides(starts[0], starts[0])
    right_a, left_a = both_sides(anisotropy, anisotropy)
    own, field = call(
        prepare,
        [(4, 2, 2, 8, width), (3, 8, 128)],
        *(slab, applied),
        scratch=[layers],
        in_specs=[VMEM, pl.BlockSpec(memory_space=pltpu.SMEM)],
    )
    sides, near, inner, outer = call(
        first_sums,
        [(2, 3, 2, 2, 8, width), (2, 5, 3, 8, width), (2, 2, 3, 8, width), (2, 2, 3, 8, width)],
        *(own, right, left, field),
        scratch=[(2, *layers)],
    )
    payload, aniso = call(
        prologue,
        [(slices, 2, 3, 8, 128), (2, 1, 2, 2, 8, width)],
        *(own, sides, near, inner, outer, right_a, left_a, field),
        scratch=[(2, *layers[1:])],
    )
    (windows,) = call(window, [(7, 8, 128)], own, aniso)
    corr = lax.all_to_all(payload, "tm", 0, 0, tiled=True)
    up, down = corr[:2], corr.reshape(-1, *corr.shape[2:])[:3]
    kept = []
    blocks = slices // 2
    for block in range(blocks - 1):
        kernel = functools.partial(chain, block, blocks)
        ahead_of_last = block == blocks - 2
        shapes = [(1 if ahead_of_last else 3, 3, 8, 128)] * 2 + [(2, 3, 8, 128)]
        up, down, middle = call(kernel, shapes, down, *both_sides(up, down), corr, windows, field)
        kept += [middle] if ahead_of_last else [middle, down]
    right, left = both_sides(up, down)
    (sent,) = call(pack, [(slices, 3, 8, 128)], corr, windows, down, up, *kept)
    kernel = functools.partial(final, blocks - 1, blocks)
    (sent,) = call(
        kernel, [sent.shape], up, down, right, left, corr, windows, field, sent, input_output_aliases={7: 0}
    )
    sent = lax.all_to_all(sent, "tm", 0, 0, tiled=True)
    (out,) = call(assemble, [starts.shape], sent, scratch=[(3, 2, width // 128, 16, 128)])
    return out


def solution(mesh):
    placed = (P("tm", None, "space", None, None), P("space", None, None), P())
    return jax.shard_map(
        per_device,
        mesh=mesh,
        in_specs=placed,
        out_specs=P("tm", None, "space", None, None),
        check_vma=False,
    )
```

```python
import functools

import jax
import jax.numpy as jnp
from jax import lax
from jax.experimental import pallas as pl
from jax.experimental.pallas import tpu as pltpu
from jax.sharding import PartitionSpec as P

DAMPING = 0.1
STEP = 0.02
COARSE = 2 * STEP
GAIN = -1.0 / (1.0 + DAMPING * DAMPING)
F32 = jnp.float32
VMEM = pl.BlockSpec(memory_space=pltpu.VMEM)


def near_odd(even_below, even_here):
    out = []
    for below, here in zip(even_below, even_here):
        pair = below + here
        pair = pair + pltpu.roll(pair, 1, axis=1)
        row = lax.broadcasted_iota(jnp.int32, pair.shape, 0)
        out.append(pair + jnp.where(row < 7, pltpu.roll(pair, 7, axis=0), 0.0))
    return out


def near_even(odd_here, odd_above):
    out = []
    for here, above in zip(odd_here, odd_above):
        pair = here + above
        pair = pair + pltpu.roll(pair, pair.shape[1] - 1, axis=1)
        row = lax.broadcasted_iota(jnp.int32, pair.shape, 0)
        out.append(pair + jnp.where(row > 0, pltpu.roll(pair, 1, axis=0), 0.0))
    return out


def cross(a, b):
    return [a[1] * b[2] - a[2] * b[1], a[2] * b[0] - a[0] * b[2], a[0] * b[1] - a[1] * b[0]]


def bare_rate(spin, near, twice_aniso, applied):
    field = [n + h for n, h in zip(near, applied)]
    field[2] = field[2] + twice_aniso * spin[2]
    turn = cross(spin, field)
    return cross(spin, [f + DAMPING * c for f, c in zip(field, turn)])


def rates(even, odd, aniso_even, aniso_odd, applied, evens, odds):
    rate_even = {x: bare_rate(even[x], near_even(odd[x], odd[x + 1]), aniso_even(x), applied) for x in evens}
    rate_odd = {x: bare_rate(odd[x], near_odd(even[x - 1], even[x]), aniso_odd(x), applied) for x in odds}
    return rate_even, rate_odd


def ahead(spins, rate, length):
    return {x: [s + (length * GAIN) * r for s, r in zip(spins[x], rate[x])] for x in rate}


def finish(spins, first, second, length, planes):
    return {
        x: [s + (0.5 * length * GAIN) * (f + g) for s, f, g in zip(spins[x], first[x], second[x])]
        for x in planes
    }


def heun(even, odd, aniso_even, aniso_odd, applied, length, low, high):
    evens, odds, inner = range(low, high), range(low + 1, high + 1), range(low + 1, high)
    first_e, first_o = rates(even, odd, aniso_even, aniso_odd, applied, evens, odds)
    pred_e, pred_o = ahead(even, first_e, length), ahead(odd, first_o, length)
    second_e, second_o = rates(pred_e, pred_o, aniso_even, aniso_odd, applied, inner, inner)
    return finish(even, first_e, second_e, length, inner), finish(odd, first_o, second_o, length, inner)


def lane_select(tile, low, high, a, b):
    lane = lax.broadcasted_iota(jnp.int32, (8, 128), 1) % tile
    return jnp.where((lane >= low) & (lane < high), a, b)


def tiles_of(wide):
    return [wide[:, 128 * q : 128 * (q + 1)] for q in range(wide.shape[1] // 128)]


def turn(x, by):
    by = by % x.shape[1]
    return pltpu.roll(x, by, axis=1) if by else x


def by_parity(planes, out, layers, scale=None):
    for x in range(2):
        for q in range(layers.shape[1]):
            at = slice(128 * q, 128 * (q + 1))
            layers[x, q] = planes[x, :, at]
            for parity in range(2):
                tile = layers[x, q, pl.ds(parity, 8, stride=2), :]
                out[x, parity, :, at] = tile if scale is None else scale * tile


def prepare(slab, applied, out, field, layers):
    for comp in range(4):
        by_parity(slab.at[comp], out.at[comp], layers.at[comp], 2.0 if comp == 3 else None)
    for c in range(3):
        field[c] = jnp.full(field.shape[1:], applied[c], F32)


def beside(own, sides, first=0):
    def load(comp, plane, parity):
        if 0 <= plane < 2:
            return own[comp, plane, parity]
        return sides[int(plane > 1), comp - first, plane % 2, parity]

    return load


def first_sums(own, right, left, field, sides, near, inner, outer, layers):
    for side, spins in enumerate((left, right)):
        for comp in range(3):
            by_parity(spins.at[comp], sides.at[side, comp], layers.at[side, comp])
    load = beside(own, sides)
    even = {x: [load(c, x, 0) for c in range(3)] for x in range(-2, 4)}
    odd = {x: [load(c, x, 1) for c in range(3)] for x in range(-2, 4)}
    for k in (0, 1, 4):
        for c, value in enumerate(near_even(odd[k - 2], odd[k - 1])):
            near[0, k, c] = value
    for k in (0, 3, 4):
        for c, value in enumerate(near_odd(even[k - 2], even[k - 1])):
            near[1, k, c] = value
    applied = [jnp.concatenate([field[c]] * layers.shape[3], axis=1) for c in range(3)]
    sides_own = (lambda x: load(3, x, 0), lambda x: load(3, x, 1), applied)
    first_e, first_o = rates(even, odd, *sides_own, range(2), range(2))
    for x in range(2):
        for c in range(3):
            inner[0, x, c], inner[1, x, c] = first_e[x][c], first_o[x][c]
    for k, length in enumerate((STEP, COARSE)):
        pred_e, pred_o = ahead(even, first_e, length), ahead(odd, first_o, length)
        second_e, second_o = rates(pred_e, pred_o, *sides_own, (0,), (1,))
        for c in range(3):
            outer[k, 0, c], outer[k, 1, c] = second_e[0][c], second_o[1][c]


def prologue(own, sides, near, inner, outer, right_a, left_a, field, payload, aniso, layers):
    by_parity(left_a, aniso.at[0, 0], layers.at[0], 2.0)
    by_parity(right_a, aniso.at[1, 0], layers.at[1], 2.0)
    load, load_a = beside(own, sides), beside(own, aniso, 3)
    applied = [jnp.concatenate([field[c]] * layers.shape[2], axis=1) for c in range(3)]

    planes = range(-2, 4)
    even = {x: [load(c, x, 0) for c in range(3)] for x in planes}
    odd = {x: [load(c, x, 1) for c in range(3)] for x in planes}

    def aniso_even(x):
        return load_a(3, x, 0)

    def aniso_odd(x):
        return load_a(3, x, 1)

    sides = (aniso_even, aniso_odd, applied)
    first_e = {x: [inner[0, x, c] for c in range(3)] for x in range(2)}
    first_o = {x: [inner[1, x, c] for c in range(3)] for x in range(2)}
    for x in (-2, -1, 2):
        first_e[x] = bare_rate(even[x], [near[0, x + 2, c] for c in range(3)], aniso_even(x), applied)
    for x in (-1, 2, 3):
        first_o[x] = bare_rate(odd[x], [near[1, x + 1, c] for c in range(3)], aniso_odd(x), applied)
    pred_e, pred_o = ahead(even, first_e, STEP), ahead(odd, first_o, STEP)
    second_e, second_o = rates(pred_e, pred_o, *sides, (-1, 1, 2), (-1, 0, 2))
    second_e[0], second_o[1] = ([outer[0, k, c] for c in range(3)] for k in range(2))
    fine_e = finish(even, first_e, second_e, STEP, range(-1, 3))
    fine_o = finish(odd, first_o, second_o, STEP, range(-1, 3))
    fine_e, fine_o = heun(fine_e, fine_o, *sides, STEP, -1, 2)
    pred_e, pred_o = ahead(even, first_e, COARSE), ahead(odd, first_o, COARSE)
    second_e, second_o = rates(pred_e, pred_o, *sides, (1,), (0,))
    second_e[0], second_o[1] = ([outer[1, k, c] for c in range(3)] for k in range(2))
    coarse_e = finish(even, first_e, second_e, COARSE, range(2))
    coarse_o = finish(odd, first_o, second_o, COARSE, range(2))

    keep = jnp.where(lax.axis_index("tm") == 0, 0.0, 1.0).astype(F32)
    for comp in range(3):
        for x in range(2):
            evens = tiles_of(fine_e[x][comp] - keep * coarse_e[x][comp])
            odds = [turn(t, 64) for t in tiles_of(fine_o[x][comp] - keep * coarse_o[x][comp])]
            for at in range(payload.shape[0]):
                payload[at, x, comp] = cut(evens, odds, at)


def cut(evens, odds, at):
    q, part = divmod(at, 4)
    if part == 0:
        return lanes(48, lanes(64, lanes(112, evens[q - 1], odds[q]), odds[q - 1]), evens[q])
    if part == 3:
        after = (q + 1) % len(evens)
        return lanes(16, lanes(64, lanes(80, evens[q], odds[after]), odds[q]), evens[after])
    first = 32 * part - 16
    return lanes(first, lanes(first + 64, odds[q], evens[q]), odds[q])


def lanes(count, here, before):
    return jnp.where(lax.broadcasted_iota(jnp.int32, (8, 128), 1) < count, before, here)


def logical_lane(row):
    return (lax.broadcasted_iota(jnp.int32, (8, 128), 1) + 16 - 32 * (row % 4)) & 127


def window(own, aniso, windows):
    load = beside(own, aniso, 3)
    row = lax.axis_index("tm")
    windows[6] = logical_lane(row).astype(F32)
    for at in range(own.shape[-1] // 32):

        @pl.when(row == at)
        def _():
            for k in range(6):
                even, odd = (tiles_of(load(3, k - 2, parity)) for parity in range(2))
                windows[k] = cut(even, [turn(t, 64) for t in odd], at)


def near_pair(pair, is_even):
    row = lax.broadcasted_iota(jnp.int32, (8, 128), 0)
    lane = lax.broadcasted_iota(jnp.int32, (8, 128), 1)
    source = (lane + jnp.where(is_even, 65, 63)) & 127
    out = []
    for p in pair:
        near = turn(p, 64) + jnp.take_along_axis(p, source, axis=1)
        lower = jnp.where(is_even & (row > 0), pltpu.roll(near, 1, axis=0), 0.0)
        out.append(near + jnp.where(~is_even & (row < 7), pltpu.roll(near, 7, axis=0), lower))
    return out


def pair_heun(spins, aniso, applied, is_even, length, low, high):
    def pick(a, b):
        return [jnp.where(is_even, p, r) for p, r in zip(a, b)]

    def plus(a, b):
        return [p + r for p, r in zip(a, b)]

    def rate(spins, x):
        pair = plus(spins[x], pick(spins[x - 1], spins[x + 1]))
        return bare_rate(spins[x], near_pair(pair, is_even), aniso(x), applied)

    inner = range(low + 1, high)
    first = {x: rate(spins, x) for x in inner}
    pair = pick(plus(spins[high - 1], spins[high]), plus(spins[low], spins[low + 1]))
    edge = pick(spins[low], spins[high])
    edge_aniso = jnp.where(is_even, aniso(low), aniso(high))
    edge_rate = bare_rate(edge, near_pair(pair, is_even), edge_aniso, applied)
    predicted = ahead(spins, first, length)
    predicted[low] = predicted[high] = ahead({0: edge}, {0: edge_rate}, length)[0]
    second = {x: rate(predicted, x) for x in inner}
    return finish(spins, first, second, length, inner)


def emit(ref, at, below, above, logical):
    inside = (logical & 63 >= 16) & (logical & 63 < 48)
    for c in range(3):
        ref[at, c] = jnp.where(inside, below[c], turn(above[c], 32))


def triple(ref, *at):
    return [ref[(*at, c)] for c in range(3)]


def chain(block, blocks, own, right, left, corr, windows, field, *rest):
    applied = [field[c] for c in range(3)]
    is_even = windows[6] < 64.0
    first_slice = 2 * block + 1
    start, last = block == 0, block == blocks - 1

    if last:
        below, above = own
        spins = {-1: triple(left, 0), 0: triple(below, 0), 1: triple(above, 0), 2: triple(right, 0)}
    elif start:
        spins = {base + k: triple(ref, k) for ref, base in ((own, 0), (right, 2)) for k in range(2)}
        spins |= {k - 2: triple(left, 0, k) for k in range(2)}
        extra = {-1: triple(left, 1, 1), 2: triple(right, 2)}
    else:
        spins = {base + k: triple(ref, k) for ref, base in ((left, -2), (own, 0), (right, 2)) for k in range(2)}
        extra = {-1: triple(left, 2), 2: triple(right, 2)}

    def added(spins, extra):
        return {x: [s + e for s, e in zip(spins[x], extra[x])] for x in spins}

    def aniso(x):
        return windows[x + 2]

    reach = (-1, 2) if last else (-2, 3)
    inside = {x: triple(corr, first_slice, x) for x in range(2)}
    ends = pair_heun(spins, aniso, applied, is_even, COARSE, *reach)
    if last:
        earlier, sent = rest
        ends = added(ends, inside)
        emit(sent, sent.shape[0] - 1, ends[0], ends[1], windows[6].astype(jnp.int32))
        return

    up, down, middle = rest
    ends = added(ends, inside | extra)
    for x in range(2):
        for c in range(3):
            middle[x, c] = ends[x][c]
    inside = {x: triple(corr, first_slice + 1, x) for x in range(2)}
    ends = added(pair_heun(ends, aniso, applied, is_even, COARSE, -1, 2), inside)
    for c in range(3):
        if block == blocks - 2:
            up[0, c], down[0, c] = ends[1][c], ends[0][c]
        else:
            for x in range(2):
                up[x, c] = down[x, c] = ends[x][c]
            up[2, c] = corr[first_slice + 2, 1, c]
            down[2, c] = corr[first_slice + 2, 0, c]


def final(block, blocks, above, below, *rest):
    chain(block, blocks, (below, above), *rest)


def pack(corr, windows, below, above, *rest):
    *kept, sent = rest
    logical = windows[6].astype(jnp.int32)
    emit(sent, 0, triple(corr, 0, 0), triple(corr, 0, 1), logical)
    for k, ref in enumerate(kept):
        emit(sent, k + 1, triple(ref, 0), triple(ref, 1), logical)
    emit(sent, len(kept) + 1, triple(below, 0), triple(above, 0), logical)


def assemble(sent, out, layers):
    for comp in range(3):
        for q in range(layers.shape[2]):
            tiles = [sent[4 * q + i, comp] for i in range(4)]
            for k in range(4):
                whole = tiles[0]
                for i in range(1, 4):
                    at = 32 * ((k + i) % 4)
                    whole = lane_select(128, at, at + 32, tiles[i], whole)
                layers[comp, k % 2, q, pl.ds(k // 2, 8, stride=2), :] = turn(whole, -32 * k)
            out[0, comp, :, :, 128 * q : 128 * (q + 1)] = layers[comp, :, q]


def both_sides(to_above, to_below):
    count = lax.axis_size("space")
    up = [(i, (i + 1) % count) for i in range(count)]
    down = [(j, i) for i, j in up]
    from_above = lax.ppermute(to_below, "space", down)
    return from_above, lax.ppermute(to_above, "space", up)


def call(kernel, shapes, *args, scratch=(), **more):
    return pl.pallas_call(
        kernel,
        out_shape=[jax.ShapeDtypeStruct(s, F32) for s in shapes],
        out_specs=[VMEM] * len(shapes),
        scratch_shapes=[pltpu.VMEM(s, F32) for s in scratch],
        **({"in_specs": [VMEM] * len(args)} | more),
        compiler_params=pltpu.CompilerParams(vmem_limit_bytes=32 * 1024 * 1024),
    )(*args)


def per_device(starts, anisotropy, applied):
    slices = lax.axis_size("tm")
    width = starts.shape[-1]
    layers = (4, 2, width // 128, 16, 128)
    slab = jnp.concatenate([starts[0], anisotropy[None]], axis=0)
    right, left = both_sides(starts[0], starts[0])
    right_a, left_a = both_sides(anisotropy, anisotropy)
    own, field = call(
        prepare,
        [(4, 2, 2, 8, width), (3, 8, 128)],
        *(slab, applied),
        scratch=[layers],
        in_specs=[VMEM, pl.BlockSpec(memory_space=pltpu.SMEM)],
    )
    sides, near, inner, outer = call(
        first_sums,
        [(2, 3, 2, 2, 8, width), (2, 5, 3, 8, width), (2, 2, 3, 8, width), (2, 2, 3, 8, width)],
        *(own, right, left, field),
        scratch=[(2, *layers)],
    )
    payload, aniso = call(
        prologue,
        [(slices, 2, 3, 8, 128), (2, 1, 2, 2, 8, width)],
        *(own, sides, near, inner, outer, right_a, left_a, field),
        scratch=[(2, *layers[1:])],
    )
    (windows,) = call(window, [(7, 8, 128)], own, aniso)
    corr = lax.all_to_all(payload, "tm", 0, 0, tiled=True)
    up, down = corr[:2], corr.reshape(-1, *corr.shape[2:])[:3]
    kept = []
    blocks = slices // 2
    for block in range(blocks - 1):
        kernel = functools.partial(chain, block, blocks)
        ahead_of_last = block == blocks - 2
        shapes = [(1 if ahead_of_last else 3, 3, 8, 128)] * 2 + [(2, 3, 8, 128)]
        up, down, middle = call(kernel, shapes, down, *both_sides(up, down), corr, windows, field)
        kept += [middle] if ahead_of_last else [middle, down]
    right, left = both_sides(up, down)
    (sent,) = call(pack, [(slices, 3, 8, 128)], corr, windows, down, up, *kept)
    kernel = functools.partial(final, blocks - 1, blocks)
    (sent,) = call(
        kernel, [sent.shape], up, down, right, left, corr, windows, field, sent, input_output_aliases={7: 0}
    )
    sent = lax.all_to_all(sent, "tm", 0, 0, tiled=True)
    (out,) = call(assemble, [starts.shape], sent, scratch=[(3, 2, width // 128, 16, 128)])
    return out


def solution(mesh):
    placed = (P("tm", None, "space", None, None), P("space", None, None), P())
    return jax.shard_map(
        per_device,
        mesh=mesh,
        in_specs=placed,
        out_specs=P("tm", None, "space", None, None),
        check_vma=False,
    )
```
